32 devices in a mesh: dp: 16 (over z, y, x), tensor: 2 (over core).
Axes of the slice: x: 2, y: 2, z: 4, core: 2. Of those that a mesh axis runs over, the one named last changes fastest.
Arguments:
- inputs: bfloat16 [16, 1024, 512], P('dp', 'tensor'), may hold values from -6 to 6
- memory: bfloat16 [16, 1024, 512], P('dp', 'tensor'), may hold values from -6 to 6
- tgt_seg: int32 [16, 1024], P('dp'), may hold values from 0 to 127, as said below
- mem_seg: int32 [16, 1024], P('dp'), may hold values from 0 to 127, as said below
- self_qkv: bfloat16 [3, 512, 512], P(None, None, 'tensor'), may hold values from -0.25 to 0.25
- self_out: bfloat16 [512, 512], P('tensor'), may hold values from -1 to 1
- cross_q: bfloat16 [512, 512], P(None, 'tensor'), may hold values from -0.25 to 0.25
- cross_kv: bfloat16 [2, 512, 512], P(None, None, 'tensor'), may hold values from -0.25 to 0.25
- cross_out: bfloat16 [512, 512], P('tensor'), may hold values from -1 to 1
- ffn_in: bfloat16 [512, 2048], P(None, 'tensor'), may hold values from -0.25 to 0.25
- ffn_out: bfloat16 [2048, 512], P('tensor'), may hold values from -0.125 to 0.125
- norm_gain: float32 [3, 512], replicated, may hold values from 0.5 to 1.5
- norm_bias: float32 [3, 512], replicated, may hold values from -3 to 3
- cotangent: bfloat16 [16, 1024, 512], P('dp', 'tensor'), may hold values from -6 to 6
Outputs:
- output: bfloat16 [16, 1024, 512], P('dp', 'tensor')
- grad_input: float32 [16, 1024, 512], P('dp', 'tensor')
- grad_memory: float32 [16, 1024, 512], P('dp', 'tensor')
- grad_self_qkv: float32 [3, 512, 512], P(None, None, 'tensor')
- grad_self_out: float32 [512, 512], P('tensor')
- grad_cross_q: float32 [512, 512], P(None, 'tensor')
- grad_cross_kv: float32 [2, 512, 512], P(None, None, 'tensor')
- grad_cross_out: float32 [512, 512], P('tensor')
- grad_ffn_in: float32 [512, 2048], P(None, 'tensor')
- grad_ffn_out: float32 [2048, 512], P('tensor')
- grad_norm_gain: float32 [3, 512], replicated
- grad_norm_bias: float32 [3, 512], replicated
The draws below stay inside these ranges and needn't reach their ends.
Inputs may be any that keep to these rules, and one draw needn't show every extreme that they name: `tgt_seg`: along each row, ids start at 0 and rise by at most one from one position to the next. `mem_seg`: along each row, ids start at 0 and rise by at most one from one position to the next; each row names exactly the ids that tgt_seg names in the same row.
All inputs are finite; a program needn't handle non-finite values.
Results may differ from the reference program's by a relative error of at most 0.028.
Values may be sent and summed in bfloat16 or wider, within the bound.
No kernel may reach another device: no remote copies, remote signals or barrier semaphores. Data moves between devices by JAX's collectives and lax.ppermute only.
A program may use at most 128 MiB of HBM per device.

```python
import jax
import jax.numpy as jnp
from jax import lax

D = 512
HEADS = 8
HD = 64
FF = 2048
SEQ = 1024
ROWS = 16


def segment_pair(key):
    position = jnp.arange(SEQ, dtype=jnp.int32)[None, :]
    outer_part = (position < SEQ // 4) | (position >= 3 * SEQ // 4)
    allowed = outer_part & (position % 4 == 0) & (position > 0)
    chosen = jax.random.randint(jax.random.fold_in(key, 1), (ROWS, SEQ), 0, 8) == 0
    full_row = jax.random.randint(jax.random.fold_in(key, 3), (), 0, ROWS)
    row_index = jnp.arange(ROWS, dtype=jnp.int32)[:, None]
    chosen = chosen | (row_index == full_row)
    cut_flags = (allowed & chosen).astype(jnp.int32)
    offset = jax.random.randint(jax.random.fold_in(key, 2), (ROWS, SEQ), -1, 2)
    stay_flags = cut_flags * (offset == 0).astype(jnp.int32)
    later_flags = jnp.roll(cut_flags * (offset == 1).astype(jnp.int32), 1, axis=1)
    early_flags = jnp.roll(cut_flags * (offset == -1).astype(jnp.int32), -1, axis=1)
    moved_flags = stay_flags + later_flags + early_flags
    target_ids = jnp.cumsum(cut_flags, axis=1).astype(jnp.int32)
    memory_ids = jnp.cumsum(moved_flags, axis=1).astype(jnp.int32)
    return (target_ids, memory_ids)


def draw_tgt_seg(key, part):
    return segment_pair(key)[0]


def draw_mem_seg(key, part):
    return segment_pair(key)[1]


def levels(own_key, dims, cuts, least, largest):
    level = 1.0
    for dim, parts in cuts:
        heights = jax.random.uniform(jax.random.fold_in(jax.random.fold_in(own_key, 6), dim), (parts,), jnp.float32, least / len(cuts), largest / len(cuts))
        level = level * jnp.repeat(jnp.exp(heights), dims[dim] // parts).reshape((-1,) + (1,) * (len(dims) - 1 - dim))
    return level


def normal_values(stream_key, extent, width, limit, shards=(), kind=jnp.bfloat16):
    factor_of = levels(stream_key, extent, shards, -0.22, 0.18) if shards else 1.0
    entries = jax.random.normal(stream_key, extent, jnp.float32) * width * factor_of
    return jnp.minimum(jnp.maximum(entries, -limit), limit).astype(kind)


def setup_inputs(seed: int = 0) -> dict:
    seeds = jax.random.split(jax.random.key(seed), 15)
    return {
        "inputs": normal_values(seeds[0], (ROWS, SEQ, D), 1.0, 6.0, ((0, 16), (1, 2))),
        "memory": normal_values(seeds[1], (ROWS, SEQ, D), 1.0, 6.0, ((0, 16), (1, 2))),
        "tgt_seg": draw_tgt_seg(jax.random.fold_in(seeds[14], 71), 0),
        "mem_seg": draw_mem_seg(jax.random.fold_in(seeds[14], 71), 0),
        "self_qkv": normal_values(seeds[4], (3, D, D), D ** -0.5, 0.25, ((2, 2),)),
        "self_out": normal_values(seeds[5], (D, D), (D // 16) ** -0.5, 1.0, ((0, 2),)),
        "cross_q": normal_values(seeds[6], (D, D), D ** -0.5, 0.25, ((1, 2),)),
        "cross_kv": normal_values(seeds[7], (2, D, D), D ** -0.5, 0.25, ((2, 2),)),
        "cross_out": normal_values(seeds[8], (D, D), (D // 16) ** -0.5, 1.0, ((0, 2),)),
        "ffn_in": normal_values(seeds[9], (D, FF), D ** -0.5, 0.25, ((1, 2),)),
        "ffn_out": normal_values(seeds[10], (FF, D), FF ** -0.5, 0.125, ((0, 2),)),
        "norm_gain": jnp.clip(1.0 + 0.1 * jax.random.normal(seeds[11], (3, D), jnp.float32), 0.5, 1.5),
        "norm_bias": normal_values(seeds[12], (3, D), 0.5, 3.0, (), jnp.float32),
        "cotangent": normal_values(seeds[13], (ROWS, SEQ, D), 1.0, 6.0, ((0, 16), (1, 2))),
    }


@jax.custom_vjp
def low(v):
    return lax.optimization_barrier(v.astype(jnp.bfloat16)).astype(jnp.float32)

@jax.custom_vjp
def low_back(v):
    return v

def low_keep(v):
    return (low(v), None)

def low_pass(kept, grad):
    return (grad,)

def back_keep(v):
    return (v, None)

def back_low(kept, grad):
    return (low(grad),)
low.defvjp(low_keep, low_pass)
low_back.defvjp(back_keep, back_low)
eps_norm = 1e-05
masked_score = -1000000000.0

def layer_norm(stream, norm_scale, norm_shift):
    centred = stream - lax.optimization_barrier(jnp.mean(stream, axis=-1, keepdims=True))
    spread = lax.optimization_barrier(jnp.mean(centred * centred, axis=-1, keepdims=True))
    return centred * lax.rsqrt(spread + eps_norm) * norm_scale + norm_shift

def project(stream, weight):
    return jnp.dot(stream, weight, precision=lax.Precision.HIGHEST)

def attend(queries, key_vecs, values, query_seg, key_seg):
    length = queries.shape[0]
    block_rows = min(512, length)
    heads_q = queries.reshape(length // block_rows, block_rows, HEADS, HD)
    heads_k = key_vecs.reshape(key_vecs.shape[0], HEADS, HD)
    heads_v = values.reshape(values.shape[0], HEADS, HD)
    seg_blocks = query_seg.reshape(length // block_rows, block_rows)

    def one_block(row_args):
        query_blk, seg_blk = row_args
        scores = jnp.einsum('qhd,khd->hqk', query_blk, heads_k, precision=lax.Precision.HIGHEST) * HD ** (-0.5)
        same_seg = (seg_blk[:, None] == key_seg[None, :])[None]
        scores = low_back(jnp.where(same_seg, scores, masked_score))
        row_max = lax.optimization_barrier(jnp.max(scores, axis=-1, keepdims=True))
        exp_scores = jnp.exp(scores - row_max)
        probs = low(exp_scores / lax.optimization_barrier(jnp.sum(exp_scores, axis=-1, keepdims=True)))
        mixed = jnp.einsum('hqk,khd->qhd', probs, heads_v, precision=lax.Precision.HIGHEST)
        return low(low_back(mixed))
    blocks_out = lax.map(jax.checkpoint(one_block), (heads_q, seg_blocks))
    return blocks_out.reshape(length, HEADS * HD)

def layer(params, inputs, memory, tgt_seg, mem_seg):
    self_qkv, self_out, cross_q, cross_kv, cross_out, ffn_in, ffn_out, norm_gain, norm_bias = params
    normed = low(layer_norm(inputs, norm_gain[0], norm_bias[0]))
    queries = low(low_back(project(normed, self_qkv[0])))
    key_vecs = low(low_back(project(normed, self_qkv[1])))
    values = low(low_back(project(normed, self_qkv[2])))
    branch = low_back(project(attend(queries, key_vecs, values, tgt_seg, tgt_seg), self_out))
    first_stream = inputs + branch
    normed = low(layer_norm(first_stream, norm_gain[1], norm_bias[1]))
    queries = low(low_back(project(normed, cross_q)))
    key_vecs = low(low_back(project(memory, cross_kv[0])))
    values = low(low_back(project(memory, cross_kv[1])))
    branch = low_back(project(attend(queries, key_vecs, values, tgt_seg, mem_seg), cross_out))
    second_stream = first_stream + branch
    normed = low(layer_norm(second_stream, norm_gain[2], norm_bias[2]))
    hidden = low_back(project(normed, ffn_in))
    active = low(jax.nn.gelu(hidden, approximate=False))
    return second_stream + low_back(project(active, ffn_out))

def reference(inputs, memory, tgt_seg, mem_seg, self_qkv, self_out, cross_q, cross_kv, cross_out, ffn_in, ffn_out, norm_gain, norm_bias, cotangent):
    params = tuple((weight.astype(jnp.float32) for weight in (self_qkv, self_out, cross_q, cross_kv, cross_out, ffn_in, ffn_out, norm_gain, norm_bias)))

    def run(params, inputs_all, memory_all):

        def one_row(row_args):
            return jax.checkpoint(layer)(params, row_args[0], row_args[1], row_args[2], row_args[3])
        return lax.map(one_row, (inputs_all, memory_all, tgt_seg, mem_seg))
    output, pullback = jax.vjp(run, params, inputs.astype(jnp.float32), memory.astype(jnp.float32))
    param_grads, grad_input, grad_memory = pullback(cotangent.astype(jnp.float32))
    return (output.astype(jnp.bfloat16), grad_input, grad_memory, param_grads[0], param_grads[1], param_grads[2], param_grads[3], param_grads[4], param_grads[5], param_grads[6], param_grads[7], param_grads[8])
```

```python
import functools
import math

import jax
import jax.numpy as jnp
from jax import lax
from jax.experimental import pallas as pl
from jax.experimental.pallas import tpu as pltpu
from jax.sharding import PartitionSpec as P

F32 = jnp.float32
BF16 = jnp.bfloat16
HD = 64
QB = 128
EPS = 1e-05
NEG = -1e9
LN2 = math.log(2.0)
QSCALE = HD**-0.5 / LN2
WIDTHS = (256, 768, 1024)


def mm(a, b):
    return lax.dot_general(a, b, (((1,), (0,)), ((), ())), preferred_element_type=F32)


def mm_t(a, b):
    return lax.dot_general(a, b, (((1,), (1,)), ((), ())), preferred_element_type=F32)


def normalised(v):
    centred = v - jnp.mean(v, axis=-1, keepdims=True)
    inv = lax.rsqrt(jnp.mean(centred * centred, axis=-1, keepdims=True) + EPS)
    return centred * inv, inv


def norm_back(n, inv, gain, e):
    ge = gain * e
    return (ge - jnp.mean(ge, axis=-1, keepdims=True) - n * jnp.mean(ge * n, axis=-1, keepdims=True)) * inv


def total_rows(v):
    return jnp.sum(v, axis=0, keepdims=True)


def window(seg_q_smem, seg_k_ref, first):
    seg_k = seg_k_ref[...]
    s0 = seg_q_smem[0, first]
    s1 = seg_q_smem[0, first + QB - 1]
    below = jnp.sum(jnp.where(seg_k < s0, 1.0, 0.0)).astype(jnp.int32)
    upto = jnp.sum(jnp.where(seg_k <= s1, 1.0, 0.0)).astype(jnp.int32)
    return below // 128 * 128, upto


def by_width(seq, lo, hi, run):
    need = hi - lo
    widths = [w for w in WIDTHS if w < seq] + [seq]
    for i, w in enumerate(widths):
        cond = need <= w
        if i:
            cond = jnp.logical_and(cond, need > widths[i - 1])

        @pl.when(cond)
        def _(w=w):
            run(w, pl.multiple_of(jnp.minimum(lo, seq - w), 128))


def seg_columns(seg_k_ref, out_ref):
    seq = seg_k_ref.shape[1]
    for j in range(seq // 128):
        row = jnp.broadcast_to(seg_k_ref[:, j * 128 : (j + 1) * 128], (128, 128))
        out_ref[j * 128 : (j + 1) * 128, :] = row.T


def two_heads(x):
    lane = lax.broadcasted_iota(jnp.int32, x.shape, 1)
    zero = jnp.zeros_like(x)
    return jnp.concatenate([jnp.where(lane < HD, x, zero), jnp.where(lane >= HD, x, zero)], axis=0)


def fill_bias(bias_ref, segcol_ref, seg_q_row, base, w):
    same = segcol_ref[pl.ds(base, w), :] == seg_q_row
    b = jnp.where(same, 0.0, NEG)
    bias_ref[0:w, 0:QB] = b
    bias_ref[0:w, QB : 2 * QB] = b


def attend_forward(core, q_ref, k_ref, v_ref, vt_ref, seg_q_smem, seg_q_ref, seg_k_ref, segcol_ref, bias_ref, o_ref, lse_ref):
    tokens, width = q_ref.shape
    seq = k_ref.shape[0]
    vt_ref[...] = v_ref[...].T
    seg_columns(seg_k_ref, segcol_ref)

    def block(qb, carry):
        first = pl.multiple_of(core * tokens + qb * QB, QB)
        rows = pl.ds(pl.multiple_of(qb * QB, QB), QB)
        lo, hi = window(seg_q_smem, seg_k_ref, first)

        def run(w, base):
            fill_bias(bias_ref, segcol_ref, seg_q_ref[:, pl.ds(first, QB)], base, w)
            for pr in range(width // 128):
                cols = slice(pr * 128, (pr + 1) * 128)
                q2 = two_heads(q_ref[rows, cols])
                s = mm_t(k_ref[pl.ds(base, w), cols], q2) + bias_ref[0:w, :]
                m = jnp.max(s, axis=0, keepdims=True)
                e = jnp.exp2(s - m)
                total = jnp.sum(e, axis=0, keepdims=True)
                ot = mm(vt_ref[cols, pl.ds(base, w)], e.astype(BF16)) / total
                ot = jnp.concatenate([ot[:HD, :QB], ot[HD:, QB:]], axis=0)
                o_ref[rows, cols] = ot.T.astype(BF16)
                lse_ref[qb, pr] = m + jnp.log2(total)

        by_width(seq, lo, hi, run)
        return carry

    lax.fori_loop(0, tokens // QB, block, 0)


def attend_backward(core, q_ref, k_ref, v_ref, kt_ref, seg_q_smem, seg_q_ref, seg_k_ref, segcol_ref, bias_ref, o_ref, do_ref, lse_ref, dq_ref, dk_ref, dv_ref):
    tokens, width = q_ref.shape
    seq = k_ref.shape[0]
    kt_ref[...] = k_ref[...].T
    seg_columns(seg_k_ref, segcol_ref)
    dk_ref[...] = jnp.zeros_like(dk_ref)
    dv_ref[...] = jnp.zeros_like(dv_ref)

    def block(qb, carry):
        first = pl.multiple_of(core * tokens + qb * QB, QB)
        rows = pl.ds(pl.multiple_of(qb * QB, QB), QB)
        lo, hi = window(seg_q_smem, seg_k_ref, first)

        def run(w, base):
            fill_bias(bias_ref, segcol_ref, seg_q_ref[:, pl.ds(first, QB)], base, w)
            keys = pl.ds(base, w)
            for pr in range(width // 128):
                cols = slice(pr * 128, (pr + 1) * 128)
                q2 = two_heads(q_ref[rows, cols])
                do = do_ref[rows, cols]
                do2 = two_heads(do)
                inner = (do.astype(F32) * o_ref[rows, cols].astype(F32)).T
                inner = jnp.concatenate([total_rows(inner[:HD]), total_rows(inner[HD:])], axis=1)
                p = jnp.exp2(mm_t(k_ref[keys, cols], q2) + bias_ref[0:w, :] - lse_ref[qb, pr])
                dv_ref[keys, cols] += mm(p.astype(BF16), do2)
                ds = (p * (mm_t(v_ref[keys, cols], do2) - inner)).astype(BF16)
                dk_ref[keys, cols] += mm(ds, q2)
                dqt = mm(kt_ref[cols, keys], ds)
                dqt = jnp.concatenate([dqt[:HD, :QB], dqt[HD:, QB:]], axis=0) * HD**-0.5
                dq_ref[rows, cols] = dqt.T.astype(BF16)

        by_width(seq, lo, hi, run)
        return carry

    lax.fori_loop(0, tokens // QB, block, 0)


def self_forward(x_own, x_oth, w_own, w_oth, so_own, so_oth, gain, shift, tseg_s, tseg, a_ref, q_ref, k_ref, v_ref, o_ref, lse_ref, first_ref, vt, segcol, bias):
    core = lax.axis_index("tensor")
    tokens, _ = x_own.shape
    half = w_own.shape[2]
    for x, place in ((x_own, core), (x_oth, 1 - core)):
        at = pl.ds(pl.multiple_of(place * tokens, tokens), tokens)
        n, _ = normalised(x[...].astype(F32))
        a = (n * gain[0:1, :] + shift[0:1, :]).astype(BF16)
        a_ref[at, :] = a
        for w, cols in ((w_own, slice(0, half)), (w_oth, slice(half, 2 * half))):
            if x is x_own:
                q_ref[:, cols] = (mm(a, w[0]) * QSCALE).astype(BF16)
            k_ref[at, cols] = mm(a, w[1]).astype(BF16)
            v_ref[at, cols] = mm(a, w[2]).astype(BF16)
    attend_forward(core, q_ref, k_ref, v_ref, vt, tseg_s, tseg, tseg, segcol, bias, o_ref, lse_ref)
    first_ref[...] = x_own[...].astype(F32) + mm(o_ref[:, :half], so_own[...]) + mm(o_ref[:, half:], so_oth[...])


def gelu_parts(h):
    z = jnp.abs(h)
    t = 1.0 / (1.0 + (0.3275911 / math.sqrt(2.0)) * z)
    poly = t * (0.254829592 + t * (-0.284496736 + t * (1.421413741 + t * (-1.453152027 + t * 1.061405429))))
    gauss = jnp.exp2(h * h * (-0.5 / LN2))
    tail = 0.5 * poly * gauss
    cdf = jnp.where(h >= 0, 1.0 - tail, tail)
    return cdf, gauss * (1.0 / math.sqrt(2.0 * math.pi))


def cross_ffn(
    first_ref, m_own, m_oth, q_own, q_oth, kv_own, kv_oth, co_own, co_oth, fi_own, fi_oth, fo_own, fo_oth, gain, shift, tseg_s, tseg, mseg, cot_ref,
    out_ref, b_ref, q_ref, k_ref, v_ref, o_ref, lse_ref, second_grad_ref, g_own, g_oth, norm_ref,
    vt, segcol, bias, ct, y_ref, dc_ref,
):
    core = lax.axis_index("tensor")
    tokens, dim = first_ref.shape
    half = q_own.shape[1]
    n, _ = normalised(first_ref[...])
    b = (n * gain[1:2, :] + shift[1:2, :]).astype(BF16)
    b_ref[...] = b
    for w, kv, cols in ((q_own, kv_own, slice(0, half)), (q_oth, kv_oth, slice(half, 2 * half))):
        q_ref[:, cols] = (mm(b, w[...]) * QSCALE).astype(BF16)
        for m, place in ((m_own, core), (m_oth, 1 - core)):
            at = pl.ds(pl.multiple_of(place * tokens, tokens), tokens)
            k_ref[at, cols] = mm(m[...], kv[0]).astype(BF16)
            v_ref[at, cols] = mm(m[...], kv[1]).astype(BF16)
    attend_forward(core, q_ref, k_ref, v_ref, vt, tseg_s, tseg, mseg, segcol, bias, o_ref, lse_ref)
    second = first_ref[...] + mm(o_ref[:, :half], co_own[...]) + mm(o_ref[:, half:], co_oth[...])
    y_ref[...] = second
    n, _ = normalised(second)
    c = (n * gain[2:3, :] + shift[2:3, :]).astype(BF16)
    b2 = c
    ct[...] = c.T
    dc_ref[...] = jnp.zeros_like(dc_ref)
    chunk = 256
    ff_half = fi_own.shape[1]
    for fi, fo, g in ((fi_oth, fo_oth, g_oth), (fi_own, fo_own, g_own)):

        def step(j, carry, fi=fi, fo=fo, g=g):
            at = pl.ds(pl.multiple_of(j * chunk, chunk), chunk)
            cot = cot_ref[...]
            h = mm(b2, fi[:, at])
            cdf, pdf = gelu_parts(h)
            act = (h * cdf).astype(BF16)
            y_ref[...] += mm(act, fo[at, :])
            du = mm_t(cot, fo[at, :])
            dh = (du * (cdf + h * pdf)).astype(BF16)
            dc_ref[...] += mm_t(dh, fi[:, at])
            gi = mm(ct[...], dh).astype(BF16)
            per = dim // chunk
            g[pl.ds(pl.multiple_of(j // per * dim, dim), dim), pl.ds(pl.multiple_of(j % per * chunk, chunk), chunk)] = gi
            g[pl.ds(pl.multiple_of(ff_half + j * chunk, chunk), chunk), :] = mm(act.T, cot).astype(BF16)
            return carry

        lax.fori_loop(0, ff_half // chunk, step, 0)
    out_ref[...] = y_ref[...].astype(BF16)
    second = first_ref[...] + mm(o_ref[:, :half], co_own[...]) + mm(o_ref[:, half:], co_oth[...])
    n, inv = normalised(second)
    e = dc_ref[...]
    norm_ref[0:1, :] = total_rows(e * n)
    norm_ref[1:2, :] = total_rows(e)
    second_grad_ref[...] = cot_ref[...].astype(F32) + norm_back(n, inv, gain[2:3, :], e)


def put_rows(g, start, value):
    rows = value.shape[0]
    g[start : start + rows, :] = value.astype(BF16)


def put_columns(g, start, value):
    half = g.shape[1]
    for j in range(value.shape[1] // half):
        put_rows(g, start + j * value.shape[0], value[:, j * half : (j + 1) * half])


def cross_back(
    first_ref, second_grad_ref, b_ref, m_own, m_oth, q_ref, k_ref, v_ref, o_ref, lse_ref, q_own, q_oth, kv_own, kv_oth, co_own, co_oth, gain, tseg_s, tseg, mseg,
    first_grad_ref, g_own, g_oth, gm_own, gm_oth, norm_ref,
    kt, segcol, bias, do_ref, dq_ref, dk_ref, dv_ref,
):
    core = lax.axis_index("tensor")
    tokens, dim = first_ref.shape
    half = q_own.shape[1]
    dy = second_grad_ref[...].astype(BF16)
    sides = ((q_own, kv_own, co_own, g_own, slice(0, half)), (q_oth, kv_oth, co_oth, g_oth, slice(half, 2 * half)))
    for _, _, co, g, cols in sides:
        do_ref[:, cols] = mm_t(dy, co[...]).astype(BF16)
        put_columns(g, 3 * dim, mm(o_ref[:, cols].T, dy))
    attend_backward(core, q_ref, k_ref, v_ref, kt, tseg_s, tseg, mseg, segcol, bias, o_ref, do_ref, lse_ref, dq_ref, dk_ref, dv_ref)
    db = jnp.zeros((tokens, dim), F32)
    bt = b_ref[...].T
    for q, kv, _, g, cols in sides:
        dq = dq_ref[:, cols]
        put_rows(g, 0, mm(bt, dq))
        db = db + mm_t(dq, q[...])
    own = pl.ds(pl.multiple_of(core * tokens, tokens), tokens)
    oth = pl.ds(pl.multiple_of((1 - core) * tokens, tokens), tokens)
    mt_own, mt_oth = m_own[...].T, m_oth[...].T
    gm = {}
    for q, kv, _, g, cols in sides:
        for i, (ref, factor) in enumerate(((dk_ref, LN2), (dv_ref, 1.0))):
            d_own = (ref[own, cols] * factor).astype(BF16)
            d_oth = (ref[oth, cols] * factor).astype(BF16)
            put_rows(g, (1 + i) * dim, mm(mt_own, d_own) + mm(mt_oth, d_oth))
            for key, d in (("own", d_own), ("oth", d_oth)):
                term = mm_t(d, kv[i])
                gm[key] = gm[key] + term if key in gm else term
    gm_own[...] = gm["own"]
    gm_oth[...] = gm["oth"].astype(BF16)
    n, inv = normalised(first_ref[...])
    norm_ref[0:1, :] = total_rows(db * n)
    norm_ref[1:2, :] = total_rows(db)
    first_grad_ref[...] = second_grad_ref[...] + norm_back(n, inv, gain[1:2, :], db)


def self_back(
    x_own, x_oth, first_grad_ref, a_ref, q_ref, k_ref, v_ref, o_ref, lse_ref, w_own, w_oth, so_own, so_oth, tseg_s, tseg,
    g_own, g_oth, da_own, da_oth, norm_ref,
    kt, segcol, bias, do_ref, dq_ref, dk_ref, dv_ref,
):
    core = lax.axis_index("tensor")
    tokens, dim = x_own.shape
    half = w_own.shape[2]
    dy = first_grad_ref[...].astype(BF16)
    sides = ((w_own, so_own, g_own, slice(0, half)), (w_oth, so_oth, g_oth, slice(half, 2 * half)))
    for _, so, g, cols in sides:
        do_ref[:, cols] = mm_t(dy, so[...]).astype(BF16)
        put_columns(g, 3 * dim, mm(o_ref[:, cols].T, dy))
    attend_backward(core, q_ref, k_ref, v_ref, kt, tseg_s, tseg, tseg, segcol, bias, o_ref, do_ref, lse_ref, dq_ref, dk_ref, dv_ref)
    own = pl.ds(pl.multiple_of(core * tokens, tokens), tokens)
    oth = pl.ds(pl.multiple_of((1 - core) * tokens, tokens), tokens)
    at_own, at_oth = a_ref[own, :].T, a_ref[oth, :].T
    da = {}
    for w, _, g, cols in sides:
        dq = dq_ref[:, cols]
        put_rows(g, 0, mm(at_own, dq))
        term = mm_t(dq, w[0])
        da["own"] = da["own"] + term if "own" in da else term
        for i, (ref, factor) in enumerate(((dk_ref, LN2), (dv_ref, 1.0))):
            d_own = (ref[own, cols] * factor).astype(BF16)
            d_oth = (ref[oth, cols] * factor).astype(BF16)
            put_rows(g, (1 + i) * dim, mm(at_own, d_own) + mm(at_oth, d_oth))
            for key, d in (("own", d_own), ("oth", d_oth)):
                term = mm_t(d, w[1 + i])
                da[key] = da[key] + term if key in da else term
    da_own[...] = da["own"]
    da_oth[...] = da["oth"].astype(BF16)
    n_own, _ = normalised(x_own[...].astype(F32))
    n_oth, _ = normalised(x_oth[...].astype(F32))
    norm_ref[0:1, :] = total_rows(da["own"] * n_own) + total_rows(da["oth"] * n_oth)
    norm_ref[1:2, :] = total_rows(da["own"]) + total_rows(da["oth"])


def finish_input(x_own, first_grad_ref, da_own, da_got, gain, out_ref):
    n, inv = normalised(x_own[...].astype(F32))
    e = da_own[...] + da_got[...].astype(F32)
    out_ref[...] = first_grad_ref[...] + norm_back(n, inv, gain[0:1, :], e)


def shape(dims, dtype):
    return jax.ShapeDtypeStruct(dims, dtype)


def call(body, outs, scratch, args, smem=(), flops=0, name=None):
    vmem = pl.BlockSpec(memory_space=pltpu.VMEM)
    smem_spec = pl.BlockSpec(memory_space=pltpu.SMEM)
    size = sum(a.size * a.dtype.itemsize for a in args) + sum(math.prod(o.shape) * o.dtype.itemsize for o in outs)
    return pl.pallas_call(
        body,
        out_shape=outs,
        in_specs=[smem_spec if i in smem else vmem for i in range(len(args))],
        out_specs=[vmem] * len(outs),
        scratch_shapes=[pltpu.VMEM(s, d) for s, d in scratch],
        compiler_params=pltpu.CompilerParams(vmem_limit_bytes=56 * 1024 * 1024),
        cost_estimate=pl.CostEstimate(flops=flops, bytes_accessed=size, transcendentals=0),
        name=name,
    )(*args)


def mask_orders(n):
    if n == 16:
        return [[[1, 2, 4, 12], [2, 1, 12, 4]], [[4, 12, 1, 2], [12, 4, 2, 1]]]
    base = [1 << j for j in range(n.bit_length() - 1)]
    q = len(base) // 4
    turn = lambda r: base[r:] + base[:r]
    return [[turn(0), turn(q)], [turn(2 * q), turn(3 * q)]]


def coordinate(index, n, mask):
    if n == 16:
        bits = [(index >> j) & 1 for j in range(4)]
        return {1: bits[0], 2: bits[1], 4: bits[2] ^ bits[3], 12: bits[3]}[mask]
    return (index >> (mask.bit_length() - 1)) & 1


def swap(x, n, masks):
    pairs = [(i * 2 + t, (i ^ masks[t]) * 2 + t) for i in range(n) for t in range(2)]
    return lax.ppermute(x, ("dp", "tensor"), pairs)


def other(x):
    return lax.ppermute(x, "tensor", [(0, 1), (1, 0)])


def reduce_over_rows(g, stream):
    n = lax.axis_size("dp")
    index, core = lax.axis_index("dp"), lax.axis_index("tensor")
    orders = mask_orders(n)[stream]
    steps = len(orders[0])
    masks = [(orders[0][j], orders[1][j]) for j in range(steps)]
    bits = [jnp.where(core == 0, coordinate(index, n, a), coordinate(index, n, b)) for a, b in masks]
    for j in range(steps):
        halves = g.reshape((2, g.shape[0] // 2) + g.shape[1:])
        got = swap(lax.dynamic_index_in_dim(halves, 1 - bits[j], 0, False), n, masks[j])
        keep = lax.dynamic_index_in_dim(halves, bits[j], 0, False)
        g = (keep.astype(F32) + got.astype(F32)).astype(BF16)
    for j in reversed(range(steps)):
        got = swap(g, n, masks[j])
        low, high = jnp.where(bits[j] == 0, g, got), jnp.where(bits[j] == 0, got, g)
        if j == 0:
            return low, high
        g = jnp.concatenate([low, high], axis=0)


def reduce_small(v):
    n = lax.axis_size("dp")
    step = 1
    while step < n:
        v = v + swap(v, n, (step, step))
        step *= 2
    return v + other(v)


def local(inputs, memory, tgt_seg, mem_seg, self_qkv, self_out, cross_q, cross_kv, cross_out, ffn_in, ffn_out, norm_gain, norm_bias, cotangent):
    x_own, m_own, cot = inputs[0], memory[0], cotangent[0]
    tokens, dim = x_own.shape
    seq = 2 * tokens
    half = cross_q.shape[1]
    ff = ffn_in.shape[1]
    pairs, blocks = dim // 128, tokens // QB
    x_oth, w_oth, so_oth = other(x_own), other(self_qkv), other(self_out)
    m_oth, cq_oth, ckv_oth, co_oth = other(m_own), other(cross_q), other(cross_kv), other(cross_out)
    fi_oth, fo_oth = other(ffn_in), other(ffn_out)

    lse = shape((blocks, pairs, 1, 2 * QB), F32)
    full, part = shape((seq, dim), BF16), shape((tokens, dim), BF16)
    wide = shape((tokens, dim), F32)
    norm = shape((2, dim), F32)
    segcol, bias, turned = ((seq, 128), jnp.int32), ((seq, 2 * QB), F32), ((dim, seq), BF16)
    G = 10**9
    a, q, k, v, o, lse_s, first = call(
        self_forward,
        [full, part, full, full, part, lse, wide],
        [turned, segcol, bias],
        [x_own, x_oth, self_qkv, w_oth, self_out, so_oth, norm_gain, norm_bias, tgt_seg, tgt_seg],
        smem=(8,), flops=3 * G, name="self_forward",
    )
    out, b, qc, kc, vc, oc, lse_c, second_grad, gf_own, gf_oth, norm_ffn = call(
        cross_ffn,
        [part, part, part, full, full, part, lse, wide, shape((2 * ff, dim), BF16), shape((2 * ff, dim), BF16), norm],
        [turned, segcol, bias, ((dim, tokens), BF16), ((tokens, dim), F32), ((tokens, dim), F32)],
        [first, m_own, m_oth, cross_q, cq_oth, cross_kv, ckv_oth, cross_out, co_oth, ffn_in, fi_oth, ffn_out, fo_oth, norm_gain, norm_bias, tgt_seg, tgt_seg, mem_seg, cot],
        smem=(15,), flops=12 * G, name="cross_ffn",
    )
    gf_low, gf_high = reduce_over_rows(gf_own + other(gf_oth), 0)
    pack = shape((4 * dim, half), BF16)
    work = [turned, segcol, bias, ((tokens, dim), BF16), ((tokens, dim), BF16), ((seq, dim), F32), ((seq, dim), F32)]
    first_grad, gc_own, gc_oth, gm_own, gm_oth, norm_cross = call(
        cross_back,
        [wide, pack, pack, wide, part, norm],
        work,
        [first, second_grad, b, m_own, m_oth, qc, kc, vc, oc, lse_c, cross_q, cq_oth, cross_kv, ckv_oth, cross_out, co_oth, norm_gain, tgt_seg, tgt_seg, mem_seg],
        smem=(17,), flops=6 * G, name="cross_back",
    )
    gc_low, gc_high = reduce_over_rows(gc_own + other(gc_oth), 1)
    gs_own, gs_oth, da_own, da_oth, norm_self = call(
        self_back,
        [pack, pack, wide, part, norm],
        work,
        [x_own, x_oth, first_grad, a, q, k, v, o, lse_s, self_qkv, w_oth, self_out, so_oth, tgt_seg, tgt_seg],
        smem=(13,), flops=6 * G, name="self_back",
    )
    gs_low, gs_high = reduce_over_rows(gs_own + other(gs_oth), 0)
    (grad_input,) = call(
        finish_input, [wide], [], [x_own, first_grad, da_own, other(da_oth), norm_gain], flops=10**6, name="finish_input"
    )
    grad_memory = gm_own + other(gm_oth).astype(F32)
    norms = reduce_small(jnp.concatenate([norm_self, norm_cross, norm_ffn], axis=0))
    norms = norms.reshape(3, 2, dim)

    def wide_columns(g):
        return jnp.concatenate([g[:half], g[half:]], axis=1).astype(F32)

    return (
        out[None],
        grad_input[None],
        grad_memory[None],
        jnp.concatenate([gs_low, gs_high[:dim]], axis=0).astype(F32).reshape(3, dim, half),
        wide_columns(gs_high[dim:]),
        gc_low[:dim].astype(F32),
        jnp.stack([gc_low[dim:], gc_high[:dim]]).astype(F32),
        wide_columns(gc_high[dim:]),
        jnp.concatenate([gf_low[j * dim : (j + 1) * dim] for j in range(ff // dim)], axis=1).astype(F32),
        gf_high.astype(F32),
        norms[:, 0],
        norms[:, 1],
    )


def solution(mesh):
    tokens = P("dp", "tensor", None)
    columns, rows = P(None, "tensor"), P("tensor", None)
    stacked = P(None, None, "tensor")
    return jax.shard_map(
        local,
        mesh=mesh,
        in_specs=(tokens, tokens, P("dp", None), P("dp", None), stacked, rows, columns, stacked, rows, columns, rows, P(), P(), tokens),
        out_specs=(tokens, tokens, tokens, stacked, rows, columns, stacked, rows, columns, rows, P(), P()),
        check_vma=False,
    )
```

```python
import functools
import math

import jax
import jax.numpy as jnp
from jax import lax
from jax.experimental import pallas as pl
from jax.experimental.pallas import tpu as pltpu
from jax.sharding import PartitionSpec as P

F32 = jnp.float32
BF16 = jnp.bfloat16
HD = 64
QB = 128
EPS = 1e-05
NEG = -1e9
LN2 = math.log(2.0)
QSCALE = HD**-0.5 / LN2
WIDTHS = (256, 768, 896)
SAFE = 1e4


def mm(a, b):
    return lax.dot_general(a, b, (((1,), (0,)), ((), ())), preferred_element_type=F32)


def mm_t(a, b):
    return lax.dot_general(a, b, (((1,), (1,)), ((), ())), preferred_element_type=F32)


def normalised(v):
    centred = v - jnp.mean(v, axis=-1, keepdims=True)
    inv = lax.rsqrt(jnp.mean(centred * centred, axis=-1, keepdims=True) + EPS)
    return centred * inv, inv


def norm_back(n, inv, gain, e):
    ge = gain * e
    return (ge - jnp.mean(ge, axis=-1, keepdims=True) - n * jnp.mean(ge * n, axis=-1, keepdims=True)) * inv


def total_rows(v):
    return jnp.sum(v, axis=0, keepdims=True)


def count_below(seg, value):
    return jnp.sum(jnp.where(seg < value, 1.0, 0.0)).astype(jnp.int32)


def windows(core, tokens, seg_q_smem, seg_k_ref, win_ref):
    seg_k = seg_k_ref[...]
    for qb in range(tokens // QB):
        first = core * tokens + qb * QB
        win_ref[2 * qb] = count_below(seg_k, seg_q_smem[0, first]) // 128 * 128
        win_ref[2 * qb + 1] = count_below(seg_k, seg_q_smem[0, first + QB - 1] + 1)


def by_width(seq, lo, hi, run, extra=None):
    need = hi - lo
    widths = [w for w in WIDTHS if w < seq] + [seq]
    for i, w in enumerate(widths):
        cond = need <= w
        if i:
            cond = jnp.logical_and(cond, need > widths[i - 1])
        if extra is not None:
            cond = jnp.logical_and(cond, extra)

        @pl.when(cond)
        def _(w=w):
            run(w, pl.multiple_of(jnp.minimum(lo, seq - w), 128))


def seg_columns(seg_k_ref, out_ref):
    seq = seg_k_ref.shape[1]
    for j in range(seq // 128):
        row = jnp.broadcast_to(seg_k_ref[:, j * 128 : (j + 1) * 128], (128, 128))
        out_ref[j * 128 : (j + 1) * 128, :] = row.T


def two_heads(x):
    lane = lax.broadcasted_iota(jnp.int32, x.shape, 1)
    zero = jnp.zeros_like(x)
    return jnp.concatenate([jnp.where(lane < HD, x, zero), jnp.where(lane >= HD, x, zero)], axis=0)


def masked(s, segcol_ref, keys, seg_q_row):
    same = segcol_ref[keys, :] == seg_q_row
    return jnp.concatenate([jnp.where(same, s[:, :QB], NEG), jnp.where(same, s[:, QB:], NEG)], axis=1)


def head_norms(x):
    row = lax.broadcasted_iota(jnp.int32, (x.shape[1], 128), 0) // HD
    lane = lax.broadcasted_iota(jnp.int32, (x.shape[1], 128), 1)
    pick = jnp.where(row == lane, 1.0, 0.0).astype(BF16)
    xf = x.astype(F32)
    return jnp.max(mm((xf * xf).astype(BF16), pick), axis=0, keepdims=True)


def attend_forward(core, q_ref, k_ref, v_ref, vt_ref, win_ref, seg_q_ref, segcol_ref, o_ref, lse_ref):
    tokens, width = q_ref.shape
    seq = k_ref.shape[0]
    vt_ref[...] = v_ref[...].T
    small = jnp.max(head_norms(q_ref[...]) * head_norms(k_ref[...])) < SAFE

    def place(qb):
        first = pl.multiple_of(core * tokens + qb * QB, QB)
        return pl.ds(pl.multiple_of(qb * QB, QB), QB), seg_q_ref[:, pl.ds(first, QB)]

    def finish(qb, pr, rows, cols, ot, total, m):
        ot = ot / total
        ot = jnp.concatenate([ot[:HD, :QB], ot[HD:, QB:]], axis=0)
        o_ref[rows, cols] = ot.T.astype(BF16)
        lse_ref[qb, pr] = m + jnp.log2(total)

    def block(qb, carry):
        rows, seg_row = place(qb)

        def run(w, base):
            for pr in range(width // 128):
                cols = slice(pr * 128, (pr + 1) * 128)
                q2 = two_heads(q_ref[rows, cols])
                ot = jnp.zeros((128, 2 * QB), F32)
                total = jnp.zeros((1, 2 * QB), F32)
                for c in range(0, w, 256):
                    keys = pl.ds(base + c, min(256, w - c))
                    e = jnp.exp2(masked(mm_t(k_ref[keys, cols], q2), segcol_ref, keys, seg_row))
                    total = total + jnp.sum(e, axis=0, keepdims=True)
                    ot = ot + mm(vt_ref[cols, keys], e.astype(BF16))
                finish(qb, pr, rows, cols, ot, total, 0.0)

        by_width(seq, win_ref[2 * qb], win_ref[2 * qb + 1], run)
        return carry

    def block_any(i, carry):
        qb, pr = i // (width // 128), i % (width // 128)
        rows, seg_row = place(qb)
        cols = pl.ds(pl.multiple_of(pr * 128, 128), 128)
        s = masked(mm_t(k_ref[:, cols], two_heads(q_ref[rows, cols])), segcol_ref, slice(0, seq), seg_row)
        m = jnp.max(s, axis=0, keepdims=True)
        e = jnp.exp2(s - m)
        finish(qb, pr, rows, cols, mm(vt_ref[cols, :], e.astype(BF16)), jnp.sum(e, axis=0, keepdims=True), m)
        return carry

    @pl.when(small)
    def _():
        lax.fori_loop(0, tokens // QB, block, 0)

    @pl.when(jnp.logical_not(small))
    def _():
        lax.fori_loop(0, tokens // QB * (width // 128), block_any, 0)


def attend_backward(core, col, q_ref, k_ref, v_ref, kt_ref, win_ref, seg_q_ref, segcol_ref, o_ref, do_ref, lse_ref, dq_ref, dk_ref, dv_ref):
    tokens = q_ref.shape[0]
    width = do_ref.shape[1]
    seq = k_ref.shape[0]
    kt_ref[...] = k_ref[:, col : col + width].T
    dk_ref[...] = jnp.zeros_like(dk_ref)
    dv_ref[...] = jnp.zeros_like(dv_ref)

    def block(qb, carry):
        first = pl.multiple_of(core * tokens + qb * QB, QB)
        rows = pl.ds(pl.multiple_of(qb * QB, QB), QB)
        lo, hi = win_ref[2 * qb], win_ref[2 * qb + 1]

        def run(w, base):
            seg_row = seg_q_ref[:, pl.ds(first, QB)]
            keys = pl.ds(base, w)
            for pr in range(width // 128):
                cols = slice(pr * 128, (pr + 1) * 128)
                wide = slice(col + pr * 128, col + (pr + 1) * 128)
                q2 = two_heads(q_ref[rows, wide])
                do = do_ref[rows, cols]
                do2 = two_heads(do)
                inner = (do.astype(F32) * o_ref[rows, wide].astype(F32)).T
                inner = jnp.concatenate([total_rows(inner[:HD]), total_rows(inner[HD:])], axis=1)
                s = masked(mm_t(k_ref[keys, wide], q2), segcol_ref, keys, seg_row)
                p = jnp.exp2(s - lse_ref[qb, col // 128 + pr])
                dv_ref[keys, cols] += mm(p.astype(BF16), do2)
                ds = (p * (mm_t(v_ref[keys, wide], do2) - inner)).astype(BF16)
                dk_ref[keys, cols] += mm(ds, q2)
                dqt = mm(kt_ref[cols, keys], ds)
                dqt = jnp.concatenate([dqt[:HD, :QB], dqt[HD:, QB:]], axis=0) * HD**-0.5
                dq_ref[rows, cols] = dqt.T.astype(BF16)

        by_width(seq, lo, hi, run)
        return carry

    lax.fori_loop(0, tokens // QB, block, 0)


def self_start(
    x_own, w_own, gain, shift, tseg_s, tseg, mseg,
    a_ref, q_ref, k_ref, v_ref, tcol_ref, mcol_ref, gain_ref, shift_ref, seg_ref, twin_ref, mwin_ref,
):
    core = lax.axis_index("tensor")
    tseg, mseg = tseg.get(), mseg.get()
    seg_ref[...] = tseg[...]
    windows(core, q_ref.shape[0], tseg_s, tseg, twin_ref)
    windows(core, q_ref.shape[0], tseg_s, mseg, mwin_ref)
    seg_columns(tseg, tcol_ref)
    seg_columns(mseg, mcol_ref)
    gain_ref[...] = gain.get()[...]
    shift_ref[...] = shift.get()[...]
    n, _ = normalised(x_own.get()[...].astype(F32))
    a = (n * gain_ref[0:1, :] + shift_ref[0:1, :]).astype(BF16)
    a_ref[...] = a
    w = w_own.get()
    q_ref[...] = (mm(a, w[0]) * QSCALE).astype(BF16)
    k_ref[...] = mm(a, w[1]).astype(BF16)
    v_ref[...] = mm(a, w[2]).astype(BF16)


def self_forward(
    x_own, x_oth, w_own, w_oth, so_own, so_oth, a_own, q_in, k_in, v_in, gain, shift, twin_ref, tseg, tcol_ref,
    a_ref, q_ref, k_ref, v_ref, o_ref, lse_ref, first_ref,
    vt,
):
    core = lax.axis_index("tensor")
    tokens, half = q_in.shape
    own, oth = slice(0, half), slice(half, 2 * half)
    here = pl.ds(pl.multiple_of(core * tokens, tokens), tokens)
    there = pl.ds(pl.multiple_of((1 - core) * tokens, tokens), tokens)
    a = a_own[...]
    a_ref[here, :] = a
    q_ref[:, own] = q_in[...]
    k_ref[here, own] = k_in[...]
    v_ref[here, own] = v_in[...]
    n, _ = normalised(x_oth.get()[...].astype(F32))
    a2 = (n * gain[0:1, :] + shift[0:1, :]).astype(BF16)
    a_ref[there, :] = a2
    w = w_oth.get()
    q_ref[:, oth] = (mm(a, w[0]) * QSCALE).astype(BF16)
    k_ref[here, oth] = mm(a, w[1]).astype(BF16)
    v_ref[here, oth] = mm(a, w[2]).astype(BF16)
    k_ref[there, oth] = mm(a2, w[1]).astype(BF16)
    v_ref[there, oth] = mm(a2, w[2]).astype(BF16)
    w = w_own.get()
    k_ref[there, own] = mm(a2, w[1]).astype(BF16)
    v_ref[there, own] = mm(a2, w[2]).astype(BF16)
    attend_forward(core, q_ref, k_ref, v_ref, vt, twin_ref, tseg, tcol_ref, o_ref, lse_ref)
    first_ref[...] = x_own.get()[...].astype(F32) + mm(o_ref[:, own], so_own.get()[...]) + mm(o_ref[:, oth], so_oth.get()[...])


def gelu_parts(h):
    z = jnp.abs(h)
    t = 1.0 / (1.0 + (0.3275911 / math.sqrt(2.0)) * z)
    poly = t * (0.254829592 + t * (-0.284496736 + t * (1.421413741 + t * (-1.453152027 + t * 1.061405429))))
    gauss = jnp.exp2(h * h * (-0.5 / LN2))
    tail = 0.5 * poly * gauss
    cdf = jnp.where(h >= 0, 1.0 - tail, tail)
    return cdf, gauss * (1.0 / math.sqrt(2.0 * math.pi))


def cross_forward(
    first_ref, m_own, m_oth, q_own, q_oth, kv_own, kv_oth, co_own, co_oth, gain, shift, win_ref, tseg, mcol_ref,
    b_ref, mem_ref, q_ref, k_ref, v_ref, o_ref, lse_ref, second_ref, c_ref,
    vt, sems,
):
    core = lax.axis_index("tensor")
    tokens, _ = first_ref.shape
    half = kv_own.ref.shape[2]
    copies = []
    for i, (m, place) in enumerate(((m_own, core), (m_oth, 1 - core))):
        copies.append(pltpu.make_async_copy(getattr(m, "ref", m), mem_ref.at[pl.ds(pl.multiple_of(place * tokens, tokens), tokens), :], sems.at[i]))
        copies[-1].start()
    n, _ = normalised(first_ref[...])
    b = (n * gain[1:2, :] + shift[1:2, :]).astype(BF16)
    b_ref[...] = b
    sides = ((q_own, kv_own, slice(0, half)), (q_oth, kv_oth, slice(half, 2 * half)))
    for w, _, cols in sides:
        q_ref[:, cols] = (mm(b, w.get()[...]) * QSCALE).astype(BF16)
    for copy in copies:
        copy.wait()
    for _, kv, cols in sides:
        kv = kv.get()
        k_ref[:, cols] = mm(mem_ref[...], kv[0]).astype(BF16)
        v_ref[:, cols] = mm(mem_ref[...], kv[1]).astype(BF16)
    attend_forward(core, q_ref, k_ref, v_ref, vt, win_ref, tseg, mcol_ref, o_ref, lse_ref)
    second = first_ref[...] + mm(o_ref[:, :half], co_own.get()[...]) + mm(o_ref[:, half:], co_oth.get()[...])
    second_ref[...] = second
    n, _ = normalised(second)
    c_ref[...] = (n * gain[2:3, :] + shift[2:3, :]).astype(BF16)


def ffn_side(last, *refs):
    if last:
        c_ref, cot_late, fi_in, fo_in, y_in, dc_in, second_ref, gain, out_ref, second_grad_ref, dy_ref, g, norm_ref, ct, y_ref, dc_ref, fi, fo, sems = refs
    else:
        c_ref, cot_late, fi_in, fo_in, second_ref, y_ref, dc_ref, g, ct, fi, fo, sems = refs
    dim = c_ref.shape[1]
    ff_half = fi.shape[1]
    chunk = 256
    per = dim // chunk

    def loads(j):
        at = pl.ds(pl.multiple_of(j * chunk, chunk), chunk)
        return (
            pltpu.make_async_copy(fi_in.at[:, at], fi.at[:, at], sems.at[j, 0]),
            pltpu.make_async_copy(fo_in.at[at, :], fo.at[at, :], sems.at[j, 1]),
        )

    for j in range(ff_half // chunk):
        for copy in loads(j):
            copy.start()
    if last:
        y_ref[...] = y_in[...]
        dc_ref[...] = dc_in[...]
    else:
        y_ref[...] = second_ref[...]
        dc_ref[...] = jnp.zeros_like(dc_ref)
    ct[...] = c_ref[...].T
    cot_ref = cot_late.get()

    def step(j, carry):
        at = pl.ds(pl.multiple_of(j * chunk, chunk), chunk)
        for copy in loads(j):
            copy.wait()
        cot = cot_ref[...]
        h = mm(c_ref[...], fi[:, at])
        cdf, pdf = gelu_parts(h)
        act = (h * cdf).astype(BF16)
        y_ref[...] += mm(act, fo[at, :])
        dh = (mm_t(cot, fo[at, :]) * (cdf + h * pdf)).astype(BF16)
        dc_ref[...] += mm_t(dh, fi[:, at])
        gi_rows = pl.ds(pl.multiple_of(j // per * dim, dim), dim)
        g[gi_rows, pl.ds(pl.multiple_of(j % per * chunk, chunk), chunk)] = mm(ct[...], dh).astype(BF16)
        g[pl.ds(pl.multiple_of(ff_half + j * chunk, chunk), chunk), :] = mm(act.T, cot).astype(BF16)
        return carry

    lax.fori_loop(0, ff_half // chunk, step, 0)
    if last:
        out_ref[...] = y_ref[...].astype(BF16)
        n, inv = normalised(second_ref[...])
        e = dc_ref[...]
        norm_ref[0:1, :] = total_rows(e * n)
        norm_ref[1:2, :] = total_rows(e)
        second_grad = cot_ref[...].astype(F32) + norm_back(n, inv, gain[2:3, :], e)
        second_grad_ref[...] = second_grad
        dy_ref[...] = second_grad.astype(BF16)


def attention_side(col, queries_inside, *refs):
    dy_ref, w_out, xq_ref, xk_ref, q_ref, k_ref, v_ref, o_ref, lse_ref, win_ref, tseg, segcol_ref = refs[:12]
    dq_ref, dk_out, dv_out, g_ref, kt, do_ref, dk_ref, dv_ref = refs[-8:]
    core = lax.axis_index("tensor")
    tokens, dim = dy_ref.shape
    half = do_ref.shape[1]
    cols = slice(col, col + half)
    dy = dy_ref[...]
    out = mm(o_ref[:, cols].T, dy).astype(BF16)
    for j in range(dim // half):
        g_ref[3 * dim + j * half : 3 * dim + (j + 1) * half, :] = out[:, j * half : (j + 1) * half]
    do_ref[...] = mm_t(dy, w_out.get()[...]).astype(BF16)
    attend_backward(core, col, q_ref, k_ref, v_ref, kt, win_ref, tseg, segcol_ref, o_ref, do_ref, lse_ref, dq_ref, dk_ref, dv_ref)
    dk_out[...] = (dk_ref[...] * LN2).astype(BF16)
    dv_out[...] = dv_ref[...].astype(BF16)
    if queries_inside:
        xq = xk_ref[pl.ds(pl.multiple_of(core * tokens, tokens), tokens), :]
    else:
        xq = xq_ref[...]
    xt = xk_ref[...].T
    g_ref[0:dim, :] = mm(xq.T, dq_ref[...]).astype(BF16)
    g_ref[dim : 2 * dim, :] = mm(xt, dk_out[...]).astype(BF16)
    g_ref[2 * dim : 3 * dim, :] = mm(xt, dv_out[...]).astype(BF16)


def cross_join(
    first_ref, second_grad_ref, dq_own, dk_own, dv_own, dq_oth, dk_oth, dv_oth, q_own, q_oth, kv_own, kv_oth, gain,
    first_grad_ref, dy_ref, gm_own, gm_oth, norm_ref,
):
    core = lax.axis_index("tensor")
    tokens, _ = first_ref.shape
    kv_own, kv_oth = kv_own.get(), kv_oth.get()
    db = mm_t(dq_own[...], q_own.get()[...]) + mm_t(dq_oth[...], q_oth.get()[...])
    n, inv = normalised(first_ref[...])
    norm_ref[0:1, :] = total_rows(db * n)
    norm_ref[1:2, :] = total_rows(db)
    first_grad = second_grad_ref[...] + norm_back(n, inv, gain[1:2, :], db)
    first_grad_ref[...] = first_grad
    dy_ref[...] = first_grad.astype(BF16)
    for out, place in ((gm_own, core), (gm_oth, 1 - core)):
        at = pl.ds(pl.multiple_of(place * tokens, tokens), tokens)
        term = mm_t(dk_own[at, :], kv_own[0]) + mm_t(dv_own[at, :], kv_own[1])
        term = term + mm_t(dk_oth[at, :], kv_oth[0]) + mm_t(dv_oth[at, :], kv_oth[1])
        out[...] = term.astype(out.dtype)


def self_join(
    x_own, x_oth, dq_own, dk_own, dv_own, dq_oth, dk_oth, dv_oth, w_own, w_oth,
    da_own, da_oth, norm_ref,
):
    core = lax.axis_index("tensor")
    tokens, _ = da_own.shape
    w_own, w_oth = w_own.get(), w_oth.get()
    gain_sum, shift_sum = 0.0, 0.0
    for x, out, place in ((x_own, da_own, core), (x_oth, da_oth, 1 - core)):
        at = pl.ds(pl.multiple_of(place * tokens, tokens), tokens)
        e = mm_t(dk_own[at, :], w_own[1]) + mm_t(dv_own[at, :], w_own[2])
        e = e + mm_t(dk_oth[at, :], w_oth[1]) + mm_t(dv_oth[at, :], w_oth[2])
        if x is x_own:
            e = e + mm_t(dq_own[...], w_own[0]) + mm_t(dq_oth[...], w_oth[0])
        out[...] = e.astype(out.dtype)
        n, _ = normalised(x.get()[...].astype(F32))
        gain_sum = gain_sum + total_rows(e * n)
        shift_sum = shift_sum + total_rows(e)
    norm_ref[0:1, :] = gain_sum
    norm_ref[1:2, :] = shift_sum


def finish_input(x_own, first_grad_ref, da_own, da_got, gain, out_ref):
    n, inv = normalised(x_own.get()[...].astype(F32))
    e = da_own[...] + da_got[...].astype(F32)
    out_ref[...] = first_grad_ref[...] + norm_back(n, inv, gain[0:1, :], e)


def shape(dims, dtype):
    return pltpu.VMEM(dims, dtype)


def smem_shape(dims, dtype):
    return jax.ShapeDtypeStruct(dims, dtype)


def hbm_shape(dims, dtype):
    return jax.ShapeDtypeStruct(dims, dtype)


class Late:
    def __init__(self, copy, ref):
        self.copy, self.ref, self.pending = copy, ref, True

    def get(self):
        if self.pending:
            self.copy.wait()
            self.pending = False
        return self.ref


class Here:
    def __init__(self, ref):
        self.ref = ref

    def get(self):
        return self.ref


def call(body, outs, scratch, args, smem=(), smem_out=(), late=(), raw=(), near=(), after=(), us=5.0, vmem=12, name=None):
    in_vmem = pl.BlockSpec(memory_space=pltpu.VMEM)
    in_smem = pl.BlockSpec(memory_space=pltpu.SMEM)
    anywhere = pl.BlockSpec(memory_space=pl.ANY)
    n_args, n_after, n_late = len(args), len(after), len(late)

    def wrapped(*refs):
        ins, rest = list(refs[:n_args]), refs[n_args + n_after :]
        if n_late:
            rest, held, sems = rest[: -n_late - 1], rest[-n_late - 1 : -1], rest[-1]
            for j, i in enumerate(late):
                copy = pltpu.make_async_copy(ins[i], held[j], sems.at[j])
                copy.start()
                ins[i] = Late(copy, held[j])
        for i in near:
            ins[i] = Here(ins[i])
        body(*ins, *rest)

    kind = lambda i: in_smem if i in smem else anywhere if i in late or i in raw else in_vmem
    held = [pltpu.VMEM(args[i].shape, args[i].dtype) for i in late]
    place = lambda i: pltpu.HBM if i in late or i in raw else pltpu.VMEM
    args = [x if i in smem or i in near else pltpu.with_memory_space_constraint(x, place(i)) for i, x in enumerate(args)]
    return pl.pallas_call(
        wrapped,
        out_shape=outs,
        in_specs=[kind(i) for i in range(n_args)] + [anywhere] * n_after,
        out_specs=[in_smem if i in smem_out else in_vmem for i in range(len(outs))],
        scratch_shapes=[x if not isinstance(x, tuple) else pltpu.VMEM(*x) for x in scratch]
        + held
        + ([pltpu.SemaphoreType.DMA((n_late,))] if n_late else []),
        compiler_params=pltpu.CompilerParams(vmem_limit_bytes=vmem * 1024 * 1024),
        cost_estimate=pl.CostEstimate(flops=int(us * 1.1e9), bytes_accessed=0, transcendentals=0),
        name=name,
    )(*args, *after)


def mask_orders(n):
    if n == 16:
        return [[[1, 2, 4, 8], [2, 4, 1, 8]], [[4, 1, 2, 8], [1, 2, 4, 8]], [[2, 4, 1, 8], [4, 1, 2, 8]]]
    base = [1 << j for j in range(n.bit_length() - 1)]
    return [[base, base[1:] + base[:1]]] * 3


def swap(x, n, masks):
    pairs = [(i * 2 + t, (i ^ masks[t]) * 2 + t) for i in range(n) for t in range(2)]
    return lax.ppermute(x, ("dp", "tensor"), pairs)


def other(x):
    return lax.ppermute(x, "tensor", [(0, 1), (1, 0)])


def reduction_plans():
    n = lax.axis_size("dp")
    index, core = lax.axis_index("dp").astype(jnp.uint32), lax.axis_index("tensor")
    plans = []
    for orders in mask_orders(n):
        place = lambda mask: (index >> jnp.uint32(mask.bit_length() - 1)) & jnp.uint32(1)
        bits = [jnp.where(core == 0, place(a), place(b)) for a, b in zip(*orders)]
        plans.append([(bit, jnp.uint32(1) - bit, bit == 0) for bit in bits])
    return plans


class Reduction:
    def __init__(self, g, stream, plans):
        n = lax.axis_size("dp")
        self.n, self.g = n, g
        self.masks = list(zip(*mask_orders(n)[stream]))
        self.plan = plans[stream]
        self.hops = [(j, True) for j in range(len(self.masks))]
        self.hops += [(j, False) for j in reversed(range(len(self.masks)))]
        self.done = 0

    def send(self):
        j, halving = self.hops[self.done]
        if halving:
            halves = self.g.reshape((2, self.g.shape[0] // 2) + self.g.shape[1:])
            self.keep = lax.dynamic_index_in_dim(halves, self.plan[j][0], 0, False)
            out = lax.dynamic_index_in_dim(halves, self.plan[j][1], 0, False)
        else:
            out = self.g
        self.got = swap(out, self.n, self.masks[j])
        return out

    def receive(self, *after):
        j, halving = self.hops[self.done]
        self.got = lax.optimization_barrier((self.got, *after))[0]
        self.done += 1
        if halving:
            self.g = (self.keep.astype(F32) + self.got.astype(F32)).astype(BF16)
            return
        own, got, first = self.g, self.got, self.plan[j][2]
        self.low, self.high = jnp.where(first, own, got), jnp.where(first, got, own)
        if self.done < len(self.hops):
            self.g = jnp.concatenate([self.low, self.high], axis=0)

    def hop(self, *after):
        self.receive(*after)
        return self.send()

    def running(self):
        return self.done < len(self.hops)


class Doubling:
    def __init__(self, value):
        self.value, self.step, self.n = value, 1, lax.axis_size("dp")

    def running(self):
        return self.step < self.n

    def send(self):
        self.got = swap(self.value, self.n, (self.step, self.step))

    def receive(self):
        self.value = self.value + self.got
        self.step *= 2


def local(inputs, memory, tgt_seg, mem_seg, self_qkv, self_out, cross_q, cross_kv, cross_out, ffn_in, ffn_out, norm_gain, norm_bias, cotangent):
    x_own, m_own, cot = inputs[0], memory[0], cotangent[0]
    tokens, dim = x_own.shape
    seq = 2 * tokens
    half = cross_q.shape[1]
    ff = ffn_in.shape[1]
    pairs, blocks = dim // 128, tokens // QB
    flat, tree = jax.tree.flatten(reduction_plans())
    x_own, *flat = lax.optimization_barrier((x_own, *flat))
    plans = jax.tree.unflatten(tree, flat)
    x_oth, w_oth, so_oth = other(x_own), other(self_qkv), other(self_out)

    lse = shape((blocks, pairs, 1, 2 * QB), F32)
    full, part = shape((seq, dim), BF16), shape((tokens, dim), BF16)
    wide = shape((tokens, dim), F32)
    norm = shape((2, dim), F32)
    col, win = shape((seq, 128), jnp.int32), smem_shape((2 * blocks,), jnp.int32)
    turned = ((dim, seq), BF16)
    narrow = shape((tokens, half), BF16)
    a_own, q, k, v, tcol, mcol, gain, shift, tseg, twin, mwin = call(
        self_start,
        [part, narrow, narrow, narrow, col, col, shape((3, dim), F32), shape((3, dim), F32), shape((1, seq), jnp.int32), win, win],
        [],
        [x_own, self_qkv, norm_gain, norm_bias, tgt_seg, tgt_seg, mem_seg],
        smem=(4,), smem_out=(9, 10), late=(5, 6, 0, 2, 3, 1), us=3.0, name="self_start",
    )
    later = lax.optimization_barrier((m_own, cross_q, cross_kv, cross_out, ffn_in, ffn_out, a_own))
    m_oth, cq_oth, ckv_oth, co_oth, fi_oth, fo_oth = [other(x) for x in later[:6]]
    a, q, k, v, o, lse_s, first = call(
        self_forward,
        [full, part, full, full, part, lse, wide],
        [turned],
        [x_own, x_oth, self_qkv, w_oth, self_out, so_oth, a_own, q, k, v, gain, shift, twin, tseg, tcol],
        smem=(12,), near=(1, 3, 5), late=(2, 0, 4), us=8.0, name="self_forward",
    )
    b, mem, qc, kc, vc, oc, lse_c, second, c = call(
        cross_forward,
        [part, full, part, full, full, part, lse, wide, part],
        [turned, pltpu.SemaphoreType.DMA((2,))],
        [first, m_own, m_oth, cross_q, cq_oth, cross_kv, ckv_oth, cross_out, co_oth, gain, shift, mwin, tseg, mcol],
        smem=(11,), raw=(1,), near=(2, 4, 6, 8), late=(3, 5, 7), us=9.0, name="cross_forward",
    )
    g_ffn = shape((2 * ff, dim), BF16)
    ffn_work = [((dim, ff), BF16), ((ff, dim), BF16), pltpu.SemaphoreType.DMA((ff // 256, 2))]
    turned_c = ((dim, tokens), BF16)
    y, dc, gf_oth = call(
        functools.partial(ffn_side, False), [wide, wide, g_ffn], [turned_c] + ffn_work,
        [c, cot, fi_oth, fo_oth, second], late=(1,), raw=(2, 3), us=6.0, name="ffn_other",
    )
    gf_got = other(gf_oth)
    out, second_grad, dy, gf_own, norm_ffn = call(
        functools.partial(ffn_side, True), [hbm_shape((tokens, dim), BF16), wide, part, g_ffn, norm],
        [turned_c, ((tokens, dim), F32), ((tokens, dim), F32)] + ffn_work,
        [c, cot, ffn_in, ffn_out, y, dc, second, gain], late=(1,), raw=(2, 3), after=[gf_oth], us=7.5, name="ffn_own",
    )
    gf = gf_own + gf_got
    red_in, red_out = Reduction(gf[:ff], 0, plans), Reduction(gf[ff:], 1, plans)
    pending = [red_in.send(), red_out.send()]

    narrow_full, pack = shape((seq, half), BF16), shape((4 * dim, half), BF16)
    side_outs = [narrow, narrow_full, narrow_full, pack]
    side_work = [((half, seq), BF16), ((tokens, half), BF16), ((seq, half), F32), ((seq, half), F32)]

    def side(start, inside, args, after, name):
        here = (1,) if start else ()
        there = () if start else (1,)
        return call(
            functools.partial(attention_side, start, inside), side_outs, side_work, args,
            smem=(9,), near=here, late=there, after=after, us=7.0, name=name,
        )

    shared = [b, mem, qc, kc, vc, oc, lse_c, mwin, tseg, mcol]
    dq2, dk2, dv2, gc_oth = side(half, False, [dy, co_oth] + shared, pending, "cross_back_other")
    gc_got = other(gc_oth)
    pending = [red_in.hop(dq2), red_out.hop(dq2), gc_oth]
    dq1, dk1, dv1, gc_own = side(0, False, [dy, cross_out] + shared, pending, "cross_back_own")
    red_c = Reduction(gc_own + gc_got, 2, plans)
    pending = [red_in.hop(dq1), red_out.hop(dq1), red_c.send()]
    first_grad, dy, gm_own, gm_oth, norm_cross = call(
        cross_join, [wide, part, wide, part, norm], [],
        [first, second_grad, dq1, dk1, dv1, dq2, dk2, dv2, cross_q, cq_oth, cross_kv, ckv_oth, gain],
        near=(9, 11), late=(8, 10), after=pending, us=2.5, name="cross_join",
    )
    grad_memory = gm_own + other(gm_oth).astype(F32)
    pending = [red_in.hop(dy), red_out.hop(dy), red_c.hop(dy)]
    shared = [a, a, q, k, v, o, lse_s, twin, tseg, tcol]
    dq2, dk2, dv2, gs_oth = side(half, True, [dy, so_oth] + shared, pending, "self_back_other")
    gs_got = other(gs_oth)
    pending = [red_in.hop(dq2), red_out.hop(dq2), red_c.hop(dq2), gs_oth]
    dq1, dk1, dv1, gs_own = side(0, True, [dy, self_out] + shared, pending, "self_back_own")
    red_s = Reduction(gs_own + gs_got, 0, plans)
    pending = [red_in.hop(dq1), red_out.hop(dq1), red_c.hop(dq1), red_s.send()]
    da_own, da_oth, norm_self = call(
        self_join, [wide, part, norm], [],
        [x_own, x_oth, dq1, dk1, dv1, dq2, dk2, dv2, self_qkv, w_oth], near=(9, 1), late=(8, 0), after=pending, us=2.0, name="self_join",
    )
    (grad_input,) = call(finish_input, [hbm_shape((tokens, dim), F32)], [], [x_own, first_grad, da_own, other(da_oth), gain], late=(0,), us=2.0, name="finish_input")
    norms = Doubling(jnp.concatenate([norm_self, norm_cross, norm_ffn], axis=0))
    streams = [red_s, red_c, red_in, red_out, norms]
    norms.send()
    while red_s.running():
        live = [r for r in streams if r.running()]
        for r, got in zip(live, lax.optimization_barrier(tuple(r.got for r in live))):
            r.got = got
            r.receive()
            if r.running():
                r.send()
    norms = norms.value + other(norms.value)
    norms = norms.reshape(3, 2, dim)
    gf_in = jnp.concatenate([red_in.low, red_in.high], axis=0)
    gf_out = jnp.concatenate([red_out.low, red_out.high], axis=0)
    gc_low, gc_high = red_c.low, red_c.high
    gs_low, gs_high = red_s.low, red_s.high

    def wide_columns(g):
        return jnp.concatenate([g[:half], g[half:]], axis=1).astype(F32)

    return (
        out[None],
        grad_input[None],
        grad_memory[None],
        jnp.concatenate([gs_low, gs_high[:dim]], axis=0).astype(F32).reshape(3, dim, half),
        wide_columns(gs_high[dim:]),
        gc_low[:dim].astype(F32),
        jnp.stack([gc_low[dim:], gc_high[:dim]]).astype(F32),
        wide_columns(gc_high[dim:]),
        jnp.concatenate([gf_in[j * dim : (j + 1) * dim] for j in range(ff // dim)], axis=1).astype(F32),
        gf_out.astype(F32),
        norms[:, 0],
        norms[:, 1],
    )


def solution(mesh):
    tokens = P("dp", "tensor", None)
    columns, rows = P(None, "tensor"), P("tensor", None)
    stacked = P(None, None, "tensor")
    return jax.shard_map(
        local,
        mesh=mesh,
        in_specs=(tokens, tokens, P("dp", None), P("dp", None), stacked, rows, columns, stacked, rows, columns, rows, P(), P(), tokens),
        out_specs=(tokens, tokens, tokens, stacked, rows, columns, stacked, rows, columns, rows, P(), P()),
        check_vma=False,
    )
```

```python
import functools
import math

import jax
import jax.numpy as jnp
from jax import lax
from jax.experimental import pallas as pl
from jax.experimental.pallas import tpu as pltpu
from jax.sharding import PartitionSpec as P

F32 = jnp.float32
BF16 = jnp.bfloat16
HD = 64
QB = 128
EPS = 1e-05
NEG = -1e9
LN2 = math.log(2.0)
QSCALE = HD**-0.5 / LN2
SAFE = 1e4


def mm(a, b):
    return lax.dot_general(a, b, (((1,), (0,)), ((), ())), preferred_element_type=F32)


def mm_t(a, b):
    return lax.dot_general(a, b, (((1,), (1,)), ((), ())), preferred_element_type=F32)


def normalised(v):
    centred = v - jnp.mean(v, axis=-1, keepdims=True)
    inv = lax.rsqrt(jnp.mean(centred * centred, axis=-1, keepdims=True) + EPS)
    return centred * inv, inv


def norm_back(n, inv, gain, e):
    ge = gain * e
    return (ge - jnp.mean(ge, axis=-1, keepdims=True) - n * jnp.mean(ge * n, axis=-1, keepdims=True)) * inv


def put_norms(norm_ref, gain_term, shift_term):
    width = gain_term.shape[1] // 128
    for i, term in enumerate((gain_term, shift_term)):
        for j in range(width):
            norm_ref[i * width + j : i * width + j + 1, :] = term[:, j * 128 : (j + 1) * 128]


def total_rows(v):
    return jnp.sum(v, axis=0, keepdims=True)


def count_below(seg, value):
    return jnp.sum(jnp.where(seg < value, 1.0, 0.0))


def windows(core, tokens, seg_q_smem, seg_k_ref, win_ref):
    seg_k = seg_k_ref[...]
    for qb in range(tokens // QB):
        first = core * tokens + qb * QB
        win_ref[2 * qb : 2 * qb + 1, :] = jnp.full((1, 128), count_below(seg_k, seg_q_smem[0, first]))
        win_ref[2 * qb + 1 : 2 * qb + 2, :] = jnp.full((1, 128), count_below(seg_k, seg_q_smem[0, first + QB - 1] + 1))


def bounds(win_ref, qb):
    lo, hi = [jnp.max(win_ref[pl.ds(2 * qb + j, 1), :]).astype(jnp.int32) for j in range(2)]
    return lo // 128 * 128, hi


def by_width(seq, lo, hi, run, rest, safe=True):
    need = hi - lo
    few, most = seq // 4, seq // 8 * 7
    at = lambda w: pl.multiple_of(jnp.minimum(lo, seq - w), 128)
    fits = jnp.logical_and(need <= most, safe)

    @pl.when(jnp.logical_and(fits, need <= few))
    def _():
        run(few, at(few))

    @pl.when(jnp.logical_and(fits, need > few))
    def _():
        run(most, at(most))

    @pl.when(jnp.logical_not(fits))
    def _():
        rest()


def seg_columns(seg_k_ref, out_ref):
    seq = seg_k_ref.shape[1]
    for j in range(seq // 128):
        row = jnp.broadcast_to(seg_k_ref[:, j * 128 : (j + 1) * 128], (128, 128))
        out_ref[j * 128 : (j + 1) * 128, :] = row.T


def two_heads(x):
    lane = lax.broadcasted_iota(jnp.int32, x.shape, 1)
    zero = jnp.zeros_like(x)
    return jnp.concatenate([jnp.where(lane < HD, x, zero), jnp.where(lane >= HD, x, zero)], axis=0)


def masked(s, segcol_ref, keys, seg_q_row):
    same = segcol_ref[keys, :] == seg_q_row
    return jnp.concatenate([jnp.where(same, s[:, :QB], NEG), jnp.where(same, s[:, QB:], NEG)], axis=1)


def head_norms(x):
    row = lax.broadcasted_iota(jnp.int32, (x.shape[1], 128), 0) // HD
    lane = lax.broadcasted_iota(jnp.int32, (x.shape[1], 128), 1)
    pick = jnp.where(row == lane, 1.0, 0.0).astype(BF16)
    xf = x.astype(F32)
    return jnp.max(mm((xf * xf).astype(BF16), pick), axis=0, keepdims=True)


def attend_forward(core, q_ref, k_ref, v_ref, win_ref, seg_q_ref, segcol_ref, o_ref, lse_ref, vt_ref):
    tokens, width = q_ref.shape
    vt_ref[...] = v_ref[...].T
    seq = k_ref.shape[0]
    pairs = width // 128
    small = jnp.max(head_norms(q_ref[...]) * head_norms(k_ref[...])) < SAFE

    def place(qb):
        first = pl.multiple_of(core * tokens + qb * QB, QB)
        return pl.ds(pl.multiple_of(qb * QB, QB), QB), seg_q_ref[:, pl.ds(first, QB)]

    def finish(qb, pr, rows, cols, ot, total, m):
        ot = ot / total
        ot = jnp.concatenate([ot[:HD, :QB], ot[HD:, QB:]], axis=0)
        o_ref[rows, cols] = ot.T.astype(BF16)
        lse_ref[qb, pr] = m + jnp.log2(total)

    def block(qb, carry):
        rows, seg_row = place(qb)

        def run(w, base):
            for pr in range(pairs):
                cols = slice(pr * 128, (pr + 1) * 128)
                q2 = two_heads(q_ref[rows, cols])
                ot = jnp.zeros((128, 2 * QB), F32)
                total = jnp.zeros((1, 2 * QB), F32)
                for c in range(0, w, 256):
                    keys = pl.ds(base + c, min(256, w - c))
                    e = jnp.exp2(masked(mm_t(k_ref[keys, cols], q2), segcol_ref, keys, seg_row))
                    total = total + jnp.sum(e, axis=0, keepdims=True)
                    ot = ot + mm(vt_ref[cols, keys], e.astype(BF16))
                finish(qb, pr, rows, cols, ot, total, 0.0)

        def rest():
            def pair(pr, carry):
                cols = pl.ds(pl.multiple_of(pr * 128, 128), 128)
                q2 = two_heads(q_ref[rows, cols])

                def scores(j):
                    keys = pl.ds(pl.multiple_of(j * 256, 256), 256)
                    return keys, masked(mm_t(k_ref[keys, cols], q2), segcol_ref, keys, seg_row)

                def largest(j, m):
                    return jnp.maximum(m, jnp.max(scores(j)[1], axis=0, keepdims=True))

                m = lax.fori_loop(0, seq // 256, largest, jnp.full((1, 2 * QB), 2 * NEG, F32))

                def gather(j, acc):
                    keys, s = scores(j)
                    e = jnp.exp2(s - m)
                    return acc[0] + jnp.sum(e, axis=0, keepdims=True), acc[1] + mm(vt_ref[cols, keys], e.astype(BF16))

                start = (jnp.zeros((1, 2 * QB), F32), jnp.zeros((128, 2 * QB), F32))
                total, ot = lax.fori_loop(0, seq // 256, gather, start)
                finish(qb, pr, rows, cols, ot, total, m)
                return carry

            lax.fori_loop(0, pairs, pair, 0)

        by_width(seq, *bounds(win_ref, qb), run, rest, small)
        return carry

    lax.fori_loop(0, tokens // QB, block, 0)


def attend_backward(core, pr, q_ref, k_ref, v_ref, win_ref, seg_q_ref, segcol_ref, o_ref, do_ref, lse_ref, dq_ref, dkv_ref, kt_ref):
    tokens = q_ref.shape[0]
    seq = k_ref.shape[0]
    cols = slice(pr * 128, (pr + 1) * 128)
    kt_ref[...] = k_ref[:, cols].T
    dkv_ref[...] = jnp.zeros_like(dkv_ref)

    def block(qb, carry):
        first = pl.multiple_of(core * tokens + qb * QB, QB)
        rows = pl.ds(pl.multiple_of(qb * QB, QB), QB)
        seg_row = seg_q_ref[:, pl.ds(first, QB)]

        def operands():
            do = do_ref[rows, :]
            inner = (do.astype(F32) * o_ref[rows, cols].astype(F32)).T
            inner = jnp.concatenate([total_rows(inner[:HD]), total_rows(inner[HD:])], axis=1)
            return two_heads(q_ref[rows, cols]), two_heads(do), inner

        def part(keys, q2, do2, inner):
            s = masked(mm_t(k_ref[keys, cols], q2), segcol_ref, keys, seg_row)
            p = jnp.exp2(s - lse_ref[qb, pr])
            dkv_ref[keys, 128:] += mm(p.astype(BF16), do2)
            ds = (p * (mm_t(v_ref[keys, cols], do2) - inner)).astype(BF16)
            dkv_ref[keys, :128] += mm(ds, q2)
            return mm(kt_ref[:, keys], ds)

        def finish(dqt):
            dqt = jnp.concatenate([dqt[:HD, :QB], dqt[HD:, QB:]], axis=0) * HD**-0.5
            dq_ref[rows, :] = dqt.T.astype(BF16)

        def run(w, base):
            finish(part(pl.ds(base, w), *operands()))

        def rest():
            given = operands()
            step = lambda j, dqt: dqt + part(pl.ds(pl.multiple_of(j * 256, 256), 256), *given)
            finish(lax.fori_loop(0, seq // 256, step, jnp.zeros((128, 2 * QB), F32)))

        by_width(seq, *bounds(win_ref, qb), run, rest)
        return carry

    lax.fori_loop(0, tokens // QB, block, 0)


def self_start(
    x_own, w_own, gain, shift, tseg_s, tseg, mseg,
    a_ref, q_ref, k_ref, v_ref, tcol_ref, mcol_ref, gain_ref, shift_ref, seg_ref, twin_ref, mwin_ref,
):
    core = lax.axis_index("tensor")
    tseg, mseg = tseg.get(), mseg.get()
    seg_ref[...] = tseg[...]
    windows(core, q_ref.shape[0], tseg_s, tseg, twin_ref)
    windows(core, q_ref.shape[0], tseg_s, mseg, mwin_ref)
    seg_columns(tseg, tcol_ref)
    seg_columns(mseg, mcol_ref)
    gain_ref[...] = gain.get()[...]
    shift_ref[...] = shift.get()[...]
    n, _ = normalised(x_own.get()[...].astype(F32))
    a = (n * gain_ref[0:1, :] + shift_ref[0:1, :]).astype(BF16)
    a_ref[...] = a
    w = w_own.get()
    q_ref[...] = (mm(a, w[0]) * QSCALE).astype(BF16)
    k_ref[...] = mm(a, w[1]).astype(BF16)
    v_ref[...] = mm(a, w[2]).astype(BF16)


def self_forward(
    x_own, x_oth, w_own, w_oth, so_own, so_oth, a_own, q_in, k_in, v_in, gain, shift, twin_ref, tseg, tcol_ref,
    at_ref, q_ref, k_ref, v_ref, o_ref, lse_ref, first_ref,
    *work,
):
    core = lax.axis_index("tensor")
    tokens, half = q_in.shape
    own, oth = slice(0, half), slice(half, 2 * half)
    here = pl.ds(pl.multiple_of(core * tokens, tokens), tokens)
    there = pl.ds(pl.multiple_of((1 - core) * tokens, tokens), tokens)
    a = a_own[...]
    at_ref[:, here] = a.T
    q_ref[:, own] = q_in[...]
    k_ref[here, own] = k_in[...]
    v_ref[here, own] = v_in[...]
    n, _ = normalised(x_oth[...].astype(F32))
    a2 = (n * gain[0:1, :] + shift[0:1, :]).astype(BF16)
    at_ref[:, there] = a2.T
    w = w_oth
    q_ref[:, oth] = (mm(a, w[0]) * QSCALE).astype(BF16)
    k_ref[here, oth] = mm(a, w[1]).astype(BF16)
    v_ref[here, oth] = mm(a, w[2]).astype(BF16)
    k_ref[there, oth] = mm(a2, w[1]).astype(BF16)
    v_ref[there, oth] = mm(a2, w[2]).astype(BF16)
    w = w_own
    k_ref[there, own] = mm(a2, w[1]).astype(BF16)
    v_ref[there, own] = mm(a2, w[2]).astype(BF16)
    attend_forward(core, q_ref, k_ref, v_ref, twin_ref, tseg, tcol_ref, o_ref, lse_ref, *work)
    first_ref[...] = x_own[...].astype(F32) + mm(o_ref[:, own], so_own[...]) + mm(o_ref[:, oth], so_oth[...])


def gelu_parts(h):
    z = jnp.abs(h)
    t = 1.0 / (1.0 + (0.3275911 / math.sqrt(2.0)) * z)
    poly = t * (0.254829592 + t * (-0.284496736 + t * (1.421413741 + t * (-1.453152027 + t * 1.061405429))))
    gauss = jnp.exp2(h * h * (-0.5 / LN2))
    tail = 0.5 * poly * gauss
    cdf = jnp.where(h >= 0, 1.0 - tail, tail)
    return cdf, gauss * (1.0 / math.sqrt(2.0 * math.pi))


def cross_forward(
    first_ref, m_own, m_oth, q_own, q_oth, kv_own, kv_oth, co_own, co_oth, gain, shift, win_ref, tseg, mcol_ref,
    bt_ref, mt_ref, q_ref, k_ref, v_ref, o_ref, lse_ref, second_ref, c_ref, ct_ref,
    *work,
):
    core = lax.axis_index("tensor")
    tokens, _ = first_ref.shape
    half = kv_own.shape[2]
    n, _ = normalised(first_ref[...])
    b = (n * gain[1:2, :] + shift[1:2, :]).astype(BF16)
    bt_ref[...] = b.T
    sides = ((q_own, kv_own, slice(0, half)), (q_oth, kv_oth, slice(half, 2 * half)))
    for w, _, cols in sides:
        q_ref[:, cols] = (mm(b, w[...]) * QSCALE).astype(BF16)
    for m, place in ((m_own, core), (m_oth, 1 - core)):
        at = pl.ds(pl.multiple_of(place * tokens, tokens), tokens)
        m = m[...]
        mt_ref[:, at] = m.T
        for _, kv, cols in sides:
            k_ref[at, cols] = mm(m, kv[0]).astype(BF16)
            v_ref[at, cols] = mm(m, kv[1]).astype(BF16)
    attend_forward(core, q_ref, k_ref, v_ref, win_ref, tseg, mcol_ref, o_ref, lse_ref, *work)
    second = first_ref[...] + mm(o_ref[:, :half], co_own[...]) + mm(o_ref[:, half:], co_oth[...])
    second_ref[...] = second
    n, _ = normalised(second)
    c = (n * gain[2:3, :] + shift[2:3, :]).astype(BF16)
    c_ref[...] = c
    ct_ref[...] = c.T


def ffn_side(last, *refs):
    if last:
        c_ref, ct, cot_ref, fi, fo, y_in, dc_in, second_ref, gain, out_ref, second_grad_ref, dy_ref, g, norm_ref, y_ref, dc_ref = refs
        y_ref[...] = y_in[...]
        dc_ref[...] = dc_in[...]
    else:
        c_ref, ct, cot_ref, fi, fo, second_ref, y_ref, dc_ref, g = refs
        y_ref[...] = second_ref[...]
        dc_ref[...] = jnp.zeros_like(dc_ref)
    dim = c_ref.shape[1]
    ff_half = fi.shape[1]
    chunk = 256
    per = dim // chunk

    def step(j, carry):
        at = pl.ds(pl.multiple_of(j * chunk, chunk), chunk)
        cot = cot_ref[...]
        h = mm(c_ref[...], fi[:, at])
        cdf, pdf = gelu_parts(h)
        act = (h * cdf).astype(BF16)
        y_ref[...] += mm(act, fo[at, :])
        dh = (mm_t(cot, fo[at, :]) * (cdf + h * pdf)).astype(BF16)
        dc_ref[...] += mm_t(dh, fi[:, at])
        gi_rows = pl.ds(pl.multiple_of(j // per * dim, dim), dim)
        g[gi_rows, pl.ds(pl.multiple_of(j % per * chunk, chunk), chunk)] = mm(ct[...], dh).astype(BF16)
        g[pl.ds(pl.multiple_of(ff_half + j * chunk, chunk), chunk), :] = mm(act.T, cot).astype(BF16)
        return carry

    lax.fori_loop(0, ff_half // chunk, step, 0)
    if last:
        out_ref[...] = y_ref[...].astype(BF16)
        n, inv = normalised(second_ref[...])
        e = dc_ref[...]
        put_norms(norm_ref, total_rows(e * n), total_rows(e))
        second_grad = cot_ref[...].astype(F32) + norm_back(n, inv, gain[2:3, :], e)
        second_grad_ref[...] = second_grad
        dy_ref[...] = second_grad.astype(BF16)


def attention_pair(pr, half, inside, *refs):
    dy_ref, w_out, xqt_ref, xt_ref, q_ref, k_ref, v_ref, o_ref, lse_ref, win_ref, tseg, segcol_ref = refs[:12]
    dq_ref, dkv_out, g_ref, do_ref, dkv_ref, *work = refs[12:]
    core = lax.axis_index("tensor")
    tokens, dim = dy_ref.shape
    cols = slice(pr * 128, (pr + 1) * 128)
    start = pr * 128 % half
    dy = dy_ref[...]
    do_ref[...] = mm_t(dy, w_out[start : start + 128, :]).astype(BF16)
    out = mm(o_ref[:, cols].T, dy).astype(BF16)
    for j in range(dim // 128):
        g_ref[3 * dim + j * 128 : 3 * dim + (j + 1) * 128, :] = out[:, j * 128 : (j + 1) * 128]
    attend_backward(core, pr, q_ref, k_ref, v_ref, win_ref, tseg, segcol_ref, o_ref, do_ref, lse_ref, dq_ref, dkv_ref, *work)
    dkv_out[:, :128] = (dkv_ref[:, :128] * LN2).astype(BF16)
    dkv_out[:, 128:] = dkv_ref[:, 128:].astype(BF16)
    xqt = xt_ref[:, pl.ds(pl.multiple_of(core * tokens, tokens), tokens)] if inside else xqt_ref[...]
    g_ref[0:dim, :] = mm(xqt, dq_ref[...]).astype(BF16)
    gkv = mm(xt_ref[...], dkv_out[...]).astype(BF16)
    g_ref[dim : 2 * dim, :] = gkv[:, :128]
    g_ref[2 * dim : 3 * dim, :] = gkv[:, 128:]


def both(first, second, cols):
    return jnp.concatenate([first[:, cols], second[:, cols]], axis=1)


def cross_join(first_ref, second_grad_ref, *refs):
    dqs, dkvs = refs[0:4], refs[4:8]
    q_own, q_oth, kv_own, kv_oth, gain, first_grad_ref, dy_ref, gm_own, gm_oth, norm_ref = refs[8:]
    core = lax.axis_index("tensor")
    tokens, _ = first_ref.shape
    half = q_own.shape[1]
    weights = []
    for pr in range(len(dqs)):
        near = pr * 128 < half
        cols = slice(pr * 128 % half, pr * 128 % half + 128)
        weights.append((q_own if near else q_oth, kv_own if near else kv_oth, cols))
    db = sum(mm_t(dq[...], q[:, cols]) for dq, (q, _, cols) in zip(dqs, weights))
    n, inv = normalised(first_ref[...])
    put_norms(norm_ref, total_rows(db * n), total_rows(db))
    first_grad = second_grad_ref[...] + norm_back(n, inv, gain[1:2, :], db)
    first_grad_ref[...] = first_grad
    dy_ref[...] = first_grad.astype(BF16)
    pairs = [both(kv.at[0], kv.at[1], cols) for _, kv, cols in weights]
    for out, place in ((gm_own, core), (gm_oth, 1 - core)):
        at = pl.ds(pl.multiple_of(place * tokens, tokens), tokens)
        out[...] = sum(mm_t(d[at, :], w) for d, w in zip(dkvs, pairs)).astype(out.dtype)


def self_join(x_own, x_oth, *refs):
    dqs, dkvs = refs[0:4], refs[4:8]
    w_own, w_oth, da_own, da_oth, norm_ref = refs[8:]
    core = lax.axis_index("tensor")
    tokens, _ = x_own.shape
    half = w_own.shape[2]
    weights = []
    for pr in range(len(dqs)):
        weights.append((w_own if pr * 128 < half else w_oth, slice(pr * 128 % half, pr * 128 % half + 128)))
    pairs = [both(w.at[1], w.at[2], cols) for w, cols in weights]
    gain_sum, shift_sum = 0.0, 0.0
    for x, out, place in ((x_own, da_own, core), (x_oth, da_oth, 1 - core)):
        at = pl.ds(pl.multiple_of(place * tokens, tokens), tokens)
        e = sum(mm_t(d[at, :], w) for d, w in zip(dkvs, pairs))
        if x is x_own:
            e = e + sum(mm_t(dq[...], w[0, :, cols]) for dq, (w, cols) in zip(dqs, weights))
        out[...] = e.astype(out.dtype)
        n, _ = normalised(x[...].astype(F32))
        gain_sum = gain_sum + total_rows(e * n)
        shift_sum = shift_sum + total_rows(e)
    put_norms(norm_ref, gain_sum, shift_sum)


def finish_input(x_own, first_grad_ref, da_own, da_got, gain, out_ref):
    n, inv = normalised(x_own[...].astype(F32))
    e = da_own[...] + da_got[...].astype(F32)
    out_ref[...] = first_grad_ref[...] + norm_back(n, inv, gain[0:1, :], e)


def finish_norms(a_ref, b_ref, gain_ref, shift_ref):
    v = a_ref[...].astype(F32) + b_ref[...].astype(F32)
    width = gain_ref.shape[1] // 128
    for layer in range(gain_ref.shape[0]):
        for j in range(width):
            row = 2 * layer * width + j
            gain_ref[layer : layer + 1, j * 128 : (j + 1) * 128] = v[row : row + 1, :]
            shift_ref[layer : layer + 1, j * 128 : (j + 1) * 128] = v[row + width : row + width + 1, :]


def shape(dims, dtype):
    return pltpu.VMEM(dims, dtype)


def smem_shape(dims, dtype):
    return jax.ShapeDtypeStruct(dims, dtype)


def hbm_shape(dims, dtype):
    return jax.ShapeDtypeStruct(dims, dtype)


class Late:
    def __init__(self, copy, ref):
        self.copy, self.ref, self.pending = copy, ref, True

    def get(self):
        if self.pending:
            self.copy.wait()
            self.pending = False
        return self.ref


def call(body, outs, scratch, args, smem=(), smem_out=(), late=(), near=(), after=(), us=5.0, vmem=12, name=None):
    in_vmem = pl.BlockSpec(memory_space=pltpu.VMEM)
    in_smem = pl.BlockSpec(memory_space=pltpu.SMEM)
    anywhere = pl.BlockSpec(memory_space=pl.ANY)
    n_args, n_after, n_late = len(args), len(after), len(late)

    def wrapped(*refs):
        ins, rest = list(refs[:n_args]), refs[n_args + n_after :]
        if n_late:
            rest, held, sems = rest[: -n_late - 1], rest[-n_late - 1 : -1], rest[-1]
            for j, i in enumerate(late):
                copy = pltpu.make_async_copy(ins[i], held[j], sems.at[j])
                copy.start()
                ins[i] = Late(copy, held[j])
        body(*ins, *rest)

    kind = lambda i: in_smem if i in smem else anywhere if i in late else in_vmem
    held = [pltpu.VMEM(args[i].shape, args[i].dtype) for i in late]
    place = lambda i: pltpu.HBM if i in late else pltpu.VMEM
    args = [x if i in smem or i in near else pltpu.with_memory_space_constraint(x, place(i)) for i, x in enumerate(args)]
    return pl.pallas_call(
        wrapped,
        out_shape=outs,
        in_specs=[kind(i) for i in range(n_args)] + [anywhere] * n_after,
        out_specs=[in_smem if i in smem_out else in_vmem for i in range(len(outs))],
        scratch_shapes=[x if not isinstance(x, tuple) else pltpu.VMEM(*x) for x in scratch]
        + held
        + ([pltpu.SemaphoreType.DMA((n_late,))] if n_late else []),
        compiler_params=pltpu.CompilerParams(vmem_limit_bytes=vmem * 1024 * 1024),
        cost_estimate=pl.CostEstimate(flops=int(us * 1.1e9), bytes_accessed=0, transcendentals=0),
        name=name,
    )(*args, *after)


FFN, CROSS, SELF_A, SELF_B = range(4)


def mask_orders(n):
    if n == 16:
        small = [[1, 2, 4, 8], [2, 1, 4, 8]]
        return [[[1, 2, 4, 8], [2, 1, 4, 8]], [[4, 1, 2, 8], [1, 4, 2, 8]], small, small]
    base = [1 << j for j in range(n.bit_length() - 1)]
    return [[base, base[1:] + base[:1]]] * 4


def swap(x, n, masks):
    pairs = [(i * 2 + t, (i ^ masks[t]) * 2 + t) for i in range(n) for t in range(2)]
    return lax.ppermute(x, ("dp", "tensor"), pairs)


def other(x):
    return lax.ppermute(x, "tensor", [(0, 1), (1, 0)])


def reduction_plans():
    n = lax.axis_size("dp")
    index, core = lax.axis_index("dp").astype(jnp.uint32), lax.axis_index("tensor")
    plans = []
    for orders in mask_orders(n):
        place = lambda mask: (index >> jnp.uint32(mask.bit_length() - 1)) & jnp.uint32(1)
        bits = [jnp.where(core == 0, place(a), place(b)) for a, b in zip(*orders)]
        plans.append([(bit, jnp.uint32(1) - bit, bit == 0) for bit in bits])
    return plans


class Reduction:
    def __init__(self, g, stream, plans):
        n = lax.axis_size("dp")
        self.n, self.g = n, g
        self.masks = list(zip(*mask_orders(n)[stream]))
        self.plan = plans[stream]
        steps = list(range(len(self.masks)))
        split = steps[:-1] if stream in (FFN, CROSS) else steps[:-2]
        self.hops = [(j, "halve") for j in split]
        self.hops += [(j, "add") for j in steps[len(split) :]]
        self.hops += [(j, "join") for j in reversed(split)]
        self.done, self.extra = 0, None

    def send(self):
        j, kind = self.hops[self.done]
        if kind == "halve":
            halves = self.g.reshape((2, self.g.shape[0] // 2) + self.g.shape[1:])
            self.keep = lax.dynamic_index_in_dim(halves, self.plan[j][0], 0, False)
            out = lax.dynamic_index_in_dim(halves, self.plan[j][1], 0, False)
        else:
            out = self.g if self.extra is None else jnp.concatenate([self.g, self.extra], axis=0)
            self.keep = self.g
        self.got = swap(out, self.n, self.masks[j])
        return out

    def receive(self, *after):
        j, kind = self.hops[self.done]
        if after:
            self.got = lax.optimization_barrier((self.got, *after))[0]
        self.done += 1
        got = self.got
        if kind != "halve" and self.extra is not None:
            rows = self.g.shape[0]
            total = self.extra.astype(F32) + got[rows:].astype(F32)
            self.extra = lax.reduce_precision(total, 8, 7).astype(BF16)
            got = got[:rows]
        if kind != "join":
            self.g = (self.keep.astype(F32) + got.astype(F32)).astype(BF16)
            return
        own, first = self.g, self.plan[j][2]
        self.low, self.high = jnp.where(first, own, got), jnp.where(first, got, own)
        if self.running():
            self.g = jnp.concatenate([self.low, self.high], axis=0)

    def hop(self, *after):
        self.receive(*after)
        return self.send()

    def running(self):
        return self.done < len(self.hops)

    def finish(self):
        while self.running():
            self.receive()
            if self.running():
                self.send()


def local(inputs, memory, tgt_seg, mem_seg, self_qkv, self_out, cross_q, cross_kv, cross_out, ffn_in, ffn_out, norm_gain, norm_bias, cotangent):
    x_own, m_own, cot = inputs[0], memory[0], cotangent[0]
    tokens, dim = x_own.shape
    seq = 2 * tokens
    half = cross_q.shape[1]
    ff = ffn_in.shape[1]
    pairs, blocks = dim // 128, tokens // QB
    flat, tree = jax.tree.flatten(reduction_plans())
    x_own, *flat = lax.optimization_barrier((x_own, *flat))
    plans = jax.tree.unflatten(tree, flat)
    x_oth, w_oth, so_oth = other(x_own), other(self_qkv), other(self_out)

    lse = shape((blocks, pairs, 1, 2 * QB), F32)
    full, part = shape((seq, dim), BF16), shape((tokens, dim), BF16)
    wide = shape((tokens, dim), F32)
    norm = shape((2 * dim // 128, 128), F32)
    col, win = shape((seq, 128), jnp.int32), shape((2 * blocks, 128), F32)
    work = [((dim, seq), BF16)]
    narrow = shape((tokens, half), BF16)
    a_own, q, k, v, tcol, mcol, gain, shift, tseg, twin, mwin = call(
        self_start,
        [part, narrow, narrow, narrow, col, col, shape((3, dim), F32), shape((3, dim), F32), shape((1, seq), jnp.int32), win, win],
        [],
        [x_own, self_qkv, norm_gain, norm_bias, tgt_seg, tgt_seg, mem_seg],
        smem=(4,), late=(5, 6, 0, 2, 3, 1), us=3.0, name="self_start",
    )
    later = lax.optimization_barrier((m_own, cross_q, cross_kv, cross_out, ffn_in, ffn_out, a_own))
    m_oth, cq_oth, ckv_oth, co_oth, fi_oth, fo_oth = [other(x) for x in later[:6]]
    at, q, k, v, o, lse_s, first = call(
        self_forward,
        [shape((dim, seq), BF16), part, full, full, part, lse, wide],
        work,
        [x_own, x_oth, self_qkv, w_oth, self_out, so_oth, a_own, q, k, v, gain, shift, twin, tseg, tcol],
        near=range(6), us=8.0, name="self_forward",
    )
    bt, mt, qc, kc, vc, oc, lse_c, second, c, ct = call(
        cross_forward,
        [shape((dim, tokens), BF16), shape((dim, seq), BF16), part, full, full, part, lse, wide, part, shape((dim, tokens), BF16)],
        work,
        [first, m_own, m_oth, cross_q, cq_oth, cross_kv, ckv_oth, cross_out, co_oth, gain, shift, mwin, tseg, mcol],
        near=range(1, 9), us=9.0, name="cross_forward",
    )
    g_ffn = shape((2 * ff, dim), BF16)
    y, dc, gf_oth = call(
        functools.partial(ffn_side, False), [wide, wide, g_ffn], [],
        [c, ct, cot, fi_oth, fo_oth, second], near=(2, 3, 4), us=6.0, name="ffn_other",
    )
    gf_got = other(gf_oth)
    out, second_grad, dy, gf_own, norm_ffn = call(
        functools.partial(ffn_side, True), [hbm_shape((tokens, dim), BF16), wide, part, g_ffn, norm],
        [((tokens, dim), F32), ((tokens, dim), F32)],
        [c, ct, cot, ffn_in, ffn_out, y, dc, second, gain], near=(2, 3, 4), after=[gf_oth], us=7.5, name="ffn_own",
    )
    red_f = Reduction(gf_own + gf_got, FFN, plans)

    def pair(pr, inside, args, after, name):
        return call(
            functools.partial(attention_pair, pr, half, inside),
            [shape((tokens, 128), BF16), shape((seq, 256), BF16), shape((4 * dim, 128), BF16)],
            [((tokens, 128), BF16), ((seq, 256), F32), ((128, seq), BF16)],
            args, near=(1,), after=after, us=4.0, name=name,
        )

    shared = [bt, mt, qc, kc, vc, oc, lse_c, mwin, tseg, mcol]
    dq2, dkv2, g2 = pair(2, False, [dy, co_oth] + shared, [red_f.send()], "cross_back_2")
    got0 = other(g2)
    dq3, dkv3, g3 = pair(3, False, [dy, co_oth] + shared, [g2], "cross_back_3")
    got1 = other(g3)
    dq0, dkv0, g0 = pair(0, False, [dy, cross_out] + shared, [g3, red_f.hop(dq3)], "cross_back_0")
    dq1, dkv1, g1 = pair(1, False, [dy, cross_out] + shared, [g0, red_f.hop(dq0)], "cross_back_1")
    red_c = Reduction(jnp.concatenate([g0 + got0, g1 + got1], axis=0), CROSS, plans)
    first_grad, dy, gm_own, gm_oth, norm_cross = call(
        cross_join, [wide, part, wide, part, norm], [],
        [first, second_grad, dq0, dq1, dq2, dq3, dkv0, dkv1, dkv2, dkv3, cross_q, cq_oth, cross_kv, ckv_oth, gain],
        near=(10, 11, 12, 13), after=[red_f.hop(dq1), red_c.send()], us=2.0, name="cross_join",
    )
    shared = [at, at, q, k, v, o, lse_s, twin, tseg, tcol]
    dq2, dkv2, g2 = pair(2, True, [dy, so_oth] + shared, [], "self_back_2")
    got0 = other(g2)
    dq3, dkv3, g3 = pair(3, True, [dy, so_oth] + shared, [g2, red_f.hop(dq2), red_c.hop(dq2)], "self_back_3")
    got1 = other(g3)
    dq0, dkv0, g0 = pair(0, True, [dy, self_out] + shared, [g3, red_f.hop(dq3), red_c.hop(dq3)], "self_back_0")
    red_s0 = Reduction(g0 + got0, SELF_A, plans)
    dq1, dkv1, g1 = pair(1, True, [dy, self_out] + shared, [red_f.hop(dq0), red_c.hop(dq0), red_s0.send()], "self_back_1")
    red_s1 = Reduction(g1 + got1, SELF_B, plans)
    first_sent = red_s1.send()
    red_s0.hop(dq1)
    red_c.hop(dq1)
    red_f.finish()
    grad_ffn_in = jnp.concatenate([red_f.low[j * dim : (j + 1) * dim] for j in range(ff // dim)], axis=1).astype(F32)
    grad_ffn_out = red_f.high.astype(F32)

    def lead(*done):
        leader = red_s1.got
        red_s1.got, *done = lax.optimization_barrier((leader, *done))
        sent = red_s1.hop()
        for r in (red_s0, red_c):
            if r.running():
                r.receive(leader)
                if r.running():
                    r.send()
        return sent, done

    da_own, da_oth, norm_self = call(
        self_join, [wide, part, norm], [],
        [x_own, x_oth, dq0, dq1, dq2, dq3, dkv0, dkv1, dkv2, dkv3, self_qkv, w_oth],
        near=(0, 1, 10, 11), after=[first_sent], us=2.0, name="self_join",
    )
    da_got, gm_got = other(da_oth), other(gm_oth)
    norms = jnp.concatenate([norm_self, norm_cross, norm_ffn], axis=0)
    norms = jnp.pad(lax.reduce_precision(norms, 8, 7).astype(BF16), ((0, -norms.shape[0] % 16), (0, 0)))
    red_s0.extra = norms
    _, (grad_ffn_in, grad_ffn_out) = lead(grad_ffn_in, grad_ffn_out)
    sent, _ = lead(da_oth)
    (grad_input,) = call(
        finish_input, [hbm_shape((tokens, dim), F32)], [], [x_own, first_grad, da_own, da_got, gain],
        near=(0, 3), after=[sent], us=2.0, name="finish_input",
    )
    grad_memory = gm_own + gm_got.astype(F32)
    sent, (grad_input, grad_memory) = lead(grad_input, grad_memory)
    while red_s1.done < len(red_s1.hops) - 1:
        lead()
    red_s0.finish()
    red_c.finish()
    norm_shape = hbm_shape((3, dim), F32)
    grad_gain, grad_shift = call(finish_norms, [norm_shape, norm_shape], [], [red_s0.extra, other(red_s0.extra)], near=(0, 1), us=1.0, name="finish_norms")

    def stack_columns(g):
        return jnp.concatenate([g[j * 128 : (j + 1) * 128] for j in range(dim // 128)], axis=1)

    cross = [jnp.concatenate([red_c.low[j * dim : (j + 1) * dim], red_c.high[j * dim : (j + 1) * dim]], axis=1) for j in range(3)]
    early = [
        cross[0].astype(F32),
        jnp.stack(cross[1:]).astype(F32),
        jnp.concatenate([stack_columns(red_c.low[3 * dim :]), stack_columns(red_c.high[3 * dim :])], axis=0).astype(F32),
        grad_gain,
        grad_shift,
    ]
    red_s1.got, *early = lax.optimization_barrier((red_s1.got, *early))
    red_s1.receive()
    selves = [[r.low[:dim], r.low[dim:], r.high[:dim], r.high[dim:]] for r in (red_s0, red_s1)]
    grad_self_qkv = jnp.stack([jnp.concatenate([selves[0][j], selves[1][j]], axis=1) for j in range(3)]).astype(F32)
    grad_self_out = jnp.concatenate([stack_columns(selves[0][3]), stack_columns(selves[1][3])], axis=0).astype(F32)
    return (
        out[None], grad_input[None], grad_memory[None], grad_self_qkv, grad_self_out,
        *early[:3], grad_ffn_in, grad_ffn_out, *early[3:],
    )


def solution(mesh):
    tokens = P("dp", "tensor", None)
    columns, rows = P(None, "tensor"), P("tensor", None)
    stacked = P(None, None, "tensor")
    return jax.shard_map(
        local,
        mesh=mesh,
        in_specs=(tokens, tokens, P("dp", None), P("dp", None), stacked, rows, columns, stacked, rows, columns, rows, P(), P(), tokens),
        out_specs=(tokens, tokens, tokens, stacked, rows, columns, stacked, rows, columns, rows, P(), P()),
        check_vma=False,
    )
```

```python
import functools
import math

import jax
import jax.numpy as jnp
from jax import lax
from jax.experimental import pallas as pl
from jax.experimental.pallas import tpu as pltpu
from jax.sharding import PartitionSpec as P

F32 = jnp.float32
BF16 = jnp.bfloat16
HD = 64
QB = 128
EPS = 1e-05
NEG = -1e9
LN2 = math.log(2.0)
QSCALE = HD**-0.5 / LN2
SAFE = 1e4


def mm(a, b):
    return lax.dot_general(a, b, (((1,), (0,)), ((), ())), preferred_element_type=F32)


def mm_t(a, b):
    return lax.dot_general(a, b, (((1,), (1,)), ((), ())), preferred_element_type=F32)


def normalised(v):
    centred = v - jnp.mean(v, axis=-1, keepdims=True)
    inv = lax.rsqrt(jnp.mean(centred * centred, axis=-1, keepdims=True) + EPS)
    return centred * inv, inv


def norm_back(n, inv, gain, e):
    ge = gain * e
    return (ge - jnp.mean(ge, axis=-1, keepdims=True) - n * jnp.mean(ge * n, axis=-1, keepdims=True)) * inv


def put_norms(norm_ref, gain_term, shift_term):
    width = gain_term.shape[1] // 128
    for i, term in enumerate((gain_term, shift_term)):
        for j in range(width):
            norm_ref[i * width + j : i * width + j + 1, :] = term[:, j * 128 : (j + 1) * 128]


def total_rows(v):
    return jnp.sum(v, axis=0, keepdims=True)


def count_below(seg, value):
    return jnp.sum(jnp.where(seg < value, 1.0, 0.0))


def windows(core, tokens, seg_q_smem, seg_k_ref, win_ref):
    seg_k = seg_k_ref[...]
    for qb in range(tokens // QB):
        first = core * tokens + qb * QB
        win_ref[2 * qb : 2 * qb + 1, :] = jnp.full((1, 128), count_below(seg_k, seg_q_smem[0, first]))
        win_ref[2 * qb + 1 : 2 * qb + 2, :] = jnp.full((1, 128), count_below(seg_k, seg_q_smem[0, first + QB - 1] + 1))


def bounds(win_ref, qb):
    lo, hi = [jnp.max(win_ref[pl.ds(2 * qb + j, 1), :]).astype(jnp.int32) for j in range(2)]
    return lo // 128 * 128, hi


def by_width(seq, lo, hi, run, rest, safe=True):
    need = hi - lo
    few, most = seq // 4, seq // 8 * 7
    at = lambda w: pl.multiple_of(jnp.minimum(lo, seq - w), 128)
    fits = jnp.logical_and(need <= most, safe)

    @pl.when(jnp.logical_and(fits, need <= few))
    def _():
        run(few, at(few))

    @pl.when(jnp.logical_and(fits, need > few))
    def _():
        run(most, at(most))

    @pl.when(jnp.logical_not(fits))
    def _():
        rest()


def seg_columns(seg_k_ref, out_ref):
    seq = seg_k_ref.shape[1]
    for j in range(seq // 128):
        row = jnp.broadcast_to(seg_k_ref[:, j * 128 : (j + 1) * 128], (128, 128))
        out_ref[j * 128 : (j + 1) * 128, :] = row.T


def two_heads(x):
    lane = lax.broadcasted_iota(jnp.int32, x.shape, 1)
    zero = jnp.zeros_like(x)
    return jnp.concatenate([jnp.where(lane < HD, x, zero), jnp.where(lane >= HD, x, zero)], axis=0)


def masked(s, segcol_ref, keys, seg_q_row):
    same = segcol_ref[keys, :] == seg_q_row
    return jnp.concatenate([jnp.where(same, s[:, :QB], NEG), jnp.where(same, s[:, QB:], NEG)], axis=1)


def head_norms(x):
    row = lax.broadcasted_iota(jnp.int32, (x.shape[1], 128), 0) // HD
    lane = lax.broadcasted_iota(jnp.int32, (x.shape[1], 128), 1)
    pick = jnp.where(row == lane, 1.0, 0.0).astype(BF16)
    xf = x.astype(F32)
    return jnp.max(mm((xf * xf).astype(BF16), pick), axis=0, keepdims=True)


def attend_forward(core, q_ref, k_ref, v_ref, win_ref, seg_q_ref, segcol_ref, o_ref, lse_ref, vt_ref):
    tokens, width = q_ref.shape
    vt_ref[...] = v_ref[...].T
    seq = k_ref.shape[0]
    pairs = width // 128
    small = jnp.max(head_norms(q_ref[...]) * head_norms(k_ref[...])) < SAFE

    def place(qb):
        first = pl.multiple_of(core * tokens + qb * QB, QB)
        return pl.ds(pl.multiple_of(qb * QB, QB), QB), seg_q_ref[:, pl.ds(first, QB)]

    def finish(qb, pr, rows, cols, ot, total, m):
        ot = ot / total
        ot = jnp.concatenate([ot[:HD, :QB], ot[HD:, QB:]], axis=0)
        o_ref[rows, cols] = ot.T.astype(BF16)
        lse_ref[qb, pr] = m + jnp.log2(total)

    def block(qb, carry):
        rows, seg_row = place(qb)

        def run(w, base):
            for pr in range(pairs):
                cols = slice(pr * 128, (pr + 1) * 128)
                q2 = two_heads(q_ref[rows, cols])
                ot = jnp.zeros((128, 2 * QB), F32)
                total = jnp.zeros((1, 2 * QB), F32)
                for c in range(0, w, 256):
                    keys = pl.ds(base + c, min(256, w - c))
                    e = jnp.exp2(masked(mm_t(k_ref[keys, cols], q2), segcol_ref, keys, seg_row))
                    total = total + jnp.sum(e, axis=0, keepdims=True)
                    ot = ot + mm(vt_ref[cols, keys], e.astype(BF16))
                finish(qb, pr, rows, cols, ot, total, 0.0)

        def rest():
            def pair(pr, carry):
                cols = pl.ds(pl.multiple_of(pr * 128, 128), 128)
                q2 = two_heads(q_ref[rows, cols])

                def scores(j):
                    keys = pl.ds(pl.multiple_of(j * 256, 256), 256)
                    return keys, masked(mm_t(k_ref[keys, cols], q2), segcol_ref, keys, seg_row)

                def largest(j, m):
                    return jnp.maximum(m, jnp.max(scores(j)[1], axis=0, keepdims=True))

                m = lax.fori_loop(0, seq // 256, largest, jnp.full((1, 2 * QB), 2 * NEG, F32))

                def gather(j, acc):
                    keys, s = scores(j)
                    e = jnp.exp2(s - m)
                    return acc[0] + jnp.sum(e, axis=0, keepdims=True), acc[1] + mm(vt_ref[cols, keys], e.astype(BF16))

                start = (jnp.zeros((1, 2 * QB), F32), jnp.zeros((128, 2 * QB), F32))
                total, ot = lax.fori_loop(0, seq // 256, gather, start)
                finish(qb, pr, rows, cols, ot, total, m)
                return carry

            lax.fori_loop(0, pairs, pair, 0)

        by_width(seq, *bounds(win_ref, qb), run, rest, small)
        return carry

    lax.fori_loop(0, tokens // QB, block, 0)


def attend_backward(core, pr, q_ref, k_ref, v_ref, win_ref, seg_q_ref, segcol_ref, o_ref, do_ref, lse_ref, dq_ref, dkv_ref, kt_ref):
    tokens = q_ref.shape[0]
    seq = k_ref.shape[0]
    cols = slice(pr * 128, (pr + 1) * 128)
    kt_ref[...] = k_ref[:, cols].T
    dkv_ref[...] = jnp.zeros_like(dkv_ref)

    def block(qb, carry):
        first = pl.multiple_of(core * tokens + qb * QB, QB)
        rows = pl.ds(pl.multiple_of(qb * QB, QB), QB)
        seg_row = seg_q_ref[:, pl.ds(first, QB)]

        def operands():
            do = do_ref[rows, :]
            inner = (do.astype(F32) * o_ref[rows, cols].astype(F32)).T
            inner = jnp.concatenate([total_rows(inner[:HD]), total_rows(inner[HD:])], axis=1)
            return two_heads(q_ref[rows, cols]), two_heads(do), inner

        def part(keys, q2, do2, inner):
            s = masked(mm_t(k_ref[keys, cols], q2), segcol_ref, keys, seg_row)
            p = jnp.exp2(s - lse_ref[qb, pr])
            dkv_ref[keys, 128:] += mm(p.astype(BF16), do2)
            ds = (p * (mm_t(v_ref[keys, cols], do2) - inner)).astype(BF16)
            dkv_ref[keys, :128] += mm(ds, q2)
            return mm(kt_ref[:, keys], ds)

        def finish(dqt):
            dqt = jnp.concatenate([dqt[:HD, :QB], dqt[HD:, QB:]], axis=0) * HD**-0.5
            dq_ref[rows, :] = dqt.T.astype(BF16)

        def run(w, base):
            finish(part(pl.ds(base, w), *operands()))

        def rest():
            given = operands()
            step = lambda j, dqt: dqt + part(pl.ds(pl.multiple_of(j * 256, 256), 256), *given)
            finish(lax.fori_loop(0, seq // 256, step, jnp.zeros((128, 2 * QB), F32)))

        by_width(seq, *bounds(win_ref, qb), run, rest)
        return carry

    lax.fori_loop(0, tokens // QB, block, 0)


def self_start(
    x_own, w_own, gain, shift, tseg_s, tseg, mseg,
    a_ref, q_ref, k_ref, v_ref, tcol_ref, mcol_ref, gain_ref, shift_ref, seg_ref, twin_ref, mwin_ref,
):
    core = lax.axis_index("tensor")
    tseg, mseg = tseg.get(), mseg.get()
    seg_ref[...] = tseg[...]
    windows(core, q_ref.shape[0], tseg_s, tseg, twin_ref)
    windows(core, q_ref.shape[0], tseg_s, mseg, mwin_ref)
    seg_columns(tseg, tcol_ref)
    seg_columns(mseg, mcol_ref)
    gain_ref[...] = gain.get()[...]
    shift_ref[...] = shift.get()[...]
    n, _ = normalised(x_own.get()[...].astype(F32))
    a = (n * gain_ref[0:1, :] + shift_ref[0:1, :]).astype(BF16)
    a_ref[...] = a
    w = w_own.get()
    q_ref[...] = (mm(a, w[0]) * QSCALE).astype(BF16)
    k_ref[...] = mm(a, w[1]).astype(BF16)
    v_ref[...] = mm(a, w[2]).astype(BF16)


def self_forward(
    x_own, x_oth, w_own, w_oth, so_own, so_oth, a_own, q_in, k_in, v_in, gain, shift, twin_ref, tseg, tcol_ref,
    at_ref, q_ref, k_ref, v_ref, o_ref, lse_ref, first_ref,
    *work,
):
    core = lax.axis_index("tensor")
    tokens, half = q_in.shape
    own, oth = slice(0, half), slice(half, 2 * half)
    here = pl.ds(pl.multiple_of(core * tokens, tokens), tokens)
    there = pl.ds(pl.multiple_of((1 - core) * tokens, tokens), tokens)
    a = a_own[...]
    at_ref[:, here] = a.T
    q_ref[:, own] = q_in[...]
    k_ref[here, own] = k_in[...]
    v_ref[here, own] = v_in[...]
    n, _ = normalised(x_oth[...].astype(F32))
    a2 = (n * gain[0:1, :] + shift[0:1, :]).astype(BF16)
    at_ref[:, there] = a2.T
    w = w_oth
    q_ref[:, oth] = (mm(a, w[0]) * QSCALE).astype(BF16)
    k_ref[here, oth] = mm(a, w[1]).astype(BF16)
    v_ref[here, oth] = mm(a, w[2]).astype(BF16)
    k_ref[there, oth] = mm(a2, w[1]).astype(BF16)
    v_ref[there, oth] = mm(a2, w[2]).astype(BF16)
    w = w_own
    k_ref[there, own] = mm(a2, w[1]).astype(BF16)
    v_ref[there, own] = mm(a2, w[2]).astype(BF16)
    attend_forward(core, q_ref, k_ref, v_ref, twin_ref, tseg, tcol_ref, o_ref, lse_ref, *work)
    first_ref[...] = x_own[...].astype(F32) + mm(o_ref[:, own], so_own[...]) + mm(o_ref[:, oth], so_oth[...])


def gelu_parts(h):
    z = jnp.abs(h)
    t = 1.0 / (1.0 + (0.3275911 / math.sqrt(2.0)) * z)
    poly = t * (0.254829592 + t * (-0.284496736 + t * (1.421413741 + t * (-1.453152027 + t * 1.061405429))))
    gauss = jnp.exp2(h * h * (-0.5 / LN2))
    tail = 0.5 * poly * gauss
    cdf = jnp.where(h >= 0, 1.0 - tail, tail)
    return cdf, gauss * (1.0 / math.sqrt(2.0 * math.pi))


def cross_forward(
    first_ref, m_own, m_oth, q_own, q_oth, kv_own, kv_oth, co_own, co_oth, gain, shift, win_ref, tseg, mcol_ref,
    bt_ref, mt_ref, q_ref, k_ref, v_ref, o_ref, lse_ref, second_ref, c_ref, ct_ref,
    *work,
):
    core = lax.axis_index("tensor")
    tokens, _ = first_ref.shape
    half = kv_own.shape[2]
    n, _ = normalised(first_ref[...])
    b = (n * gain[1:2, :] + shift[1:2, :]).astype(BF16)
    bt_ref[...] = b.T
    sides = ((q_own, kv_own, slice(0, half)), (q_oth, kv_oth, slice(half, 2 * half)))
    for w, _, cols in sides:
        q_ref[:, cols] = (mm(b, w[...]) * QSCALE).astype(BF16)
    for m, place in ((m_own, core), (m_oth, 1 - core)):
        at = pl.ds(pl.multiple_of(place * tokens, tokens), tokens)
        m = m[...]
        mt_ref[:, at] = m.T
        for _, kv, cols in sides:
            k_ref[at, cols] = mm(m, kv[0]).astype(BF16)
            v_ref[at, cols] = mm(m, kv[1]).astype(BF16)
    attend_forward(core, q_ref, k_ref, v_ref, win_ref, tseg, mcol_ref, o_ref, lse_ref, *work)
    second = first_ref[...] + mm(o_ref[:, :half], co_own[...]) + mm(o_ref[:, half:], co_oth[...])
    second_ref[...] = second
    n, _ = normalised(second)
    c = (n * gain[2:3, :] + shift[2:3, :]).astype(BF16)
    c_ref[...] = c
    ct_ref[...] = c.T


def ffn_side(last, *refs):
    if last:
        c_ref, ct, cot_ref, fi, fo, y_in, dc_in, second_ref, gain, out_ref, second_grad_ref, dy_ref, g, norm_ref, y_ref, dc_ref = refs
        y_ref[...] = y_in[...]
        dc_ref[...] = dc_in[...]
    else:
        c_ref, ct, cot_ref, fi, fo, second_ref, y_ref, dc_ref, g = refs
        y_ref[...] = second_ref[...]
        dc_ref[...] = jnp.zeros_like(dc_ref)
    dim = c_ref.shape[1]
    ff_half = fi.shape[1]
    chunk = 256
    per = dim // chunk

    def step(j, carry):
        at = pl.ds(pl.multiple_of(j * chunk, chunk), chunk)
        cot = cot_ref[...]
        h = mm(c_ref[...], fi[:, at])
        cdf, pdf = gelu_parts(h)
        act = (h * cdf).astype(BF16)
        y_ref[...] += mm(act, fo[at, :])
        dh = (mm_t(cot, fo[at, :]) * (cdf + h * pdf)).astype(BF16)
        dc_ref[...] += mm_t(dh, fi[:, at])
        gi_rows = pl.ds(pl.multiple_of(j // per * dim, dim), dim)
        g[gi_rows, pl.ds(pl.multiple_of(j % per * chunk, chunk), chunk)] = mm(ct[...], dh).astype(BF16)
        g[pl.ds(pl.multiple_of(ff_half + j * chunk, chunk), chunk), :] = mm(act.T, cot).astype(BF16)
        return carry

    lax.fori_loop(0, ff_half // chunk, step, 0)
    if last:
        out_ref[...] = y_ref[...].astype(BF16)
        n, inv = normalised(second_ref[...])
        e = dc_ref[...]
        put_norms(norm_ref, total_rows(e * n), total_rows(e))
        second_grad = cot_ref[...].astype(F32) + norm_back(n, inv, gain[2:3, :], e)
        second_grad_ref[...] = second_grad
        dy_ref[...] = second_grad.astype(BF16)


def attention_pair(pr, half, inside, *refs):
    dy_ref, w_out, xqt_ref, xt_ref, q_ref, k_ref, v_ref, o_ref, lse_ref, win_ref, tseg, segcol_ref = refs[:12]
    dq_ref, dkv_out, g_ref, do_ref, dkv_ref, *work = refs[12:]
    core = lax.axis_index("tensor")
    tokens, dim = dy_ref.shape
    cols = slice(pr * 128, (pr + 1) * 128)
    start = pr * 128 % half
    dy = dy_ref[...]
    do_ref[...] = mm_t(dy, w_out[start : start + 128, :]).astype(BF16)
    out = mm(o_ref[:, cols].T, dy).astype(BF16)
    for j in range(dim // 128):
        g_ref[3 * dim + j * 128 : 3 * dim + (j + 1) * 128, :] = out[:, j * 128 : (j + 1) * 128]
    attend_backward(core, pr, q_ref, k_ref, v_ref, win_ref, tseg, segcol_ref, o_ref, do_ref, lse_ref, dq_ref, dkv_ref, *work)
    dkv_out[:, :128] = (dkv_ref[:, :128] * LN2).astype(BF16)
    dkv_out[:, 128:] = dkv_ref[:, 128:].astype(BF16)
    xqt = xt_ref[:, pl.ds(pl.multiple_of(core * tokens, tokens), tokens)] if inside else xqt_ref[...]
    g_ref[0:dim, :] = mm(xqt, dq_ref[...]).astype(BF16)
    gkv = mm(xt_ref[...], dkv_out[...]).astype(BF16)
    g_ref[dim : 2 * dim, :] = gkv[:, :128]
    g_ref[2 * dim : 3 * dim, :] = gkv[:, 128:]


def both(first, second, cols):
    return jnp.concatenate([first[:, cols], second[:, cols]], axis=1)


def cross_join(first_ref, second_grad_ref, *refs):
    dqs, dkvs = refs[0:4], refs[4:8]
    q_own, q_oth, kv_own, kv_oth, gain, first_grad_ref, dy_ref, gm_own, gm_oth, norm_ref = refs[8:]
    core = lax.axis_index("tensor")
    tokens, _ = first_ref.shape
    half = q_own.shape[1]
    weights = []
    for pr in range(len(dqs)):
        near = pr * 128 < half
        cols = slice(pr * 128 % half, pr * 128 % half + 128)
        weights.append((q_own if near else q_oth, kv_own if near else kv_oth, cols))
    db = sum(mm_t(dq[...], q[:, cols]) for dq, (q, _, cols) in zip(dqs, weights))
    n, inv = normalised(first_ref[...])
    put_norms(norm_ref, total_rows(db * n), total_rows(db))
    first_grad = second_grad_ref[...] + norm_back(n, inv, gain[1:2, :], db)
    first_grad_ref[...] = first_grad
    dy_ref[...] = first_grad.astype(BF16)
    pairs = [both(kv.at[0], kv.at[1], cols) for _, kv, cols in weights]
    for out, place in ((gm_own, core), (gm_oth, 1 - core)):
        at = pl.ds(pl.multiple_of(place * tokens, tokens), tokens)
        out[...] = sum(mm_t(d[at, :], w) for d, w in zip(dkvs, pairs)).astype(out.dtype)


def self_join(x_own, x_oth, *refs):
    dqs, dkvs = refs[0:4], refs[4:8]
    w_own, w_oth, da_own, da_oth, norm_ref = refs[8:]
    core = lax.axis_index("tensor")
    tokens, _ = x_own.shape
    half = w_own.shape[2]
    weights = []
    for pr in range(len(dqs)):
        weights.append((w_own if pr * 128 < half else w_oth, slice(pr * 128 % half, pr * 128 % half + 128)))
    pairs = [both(w.at[1], w.at[2], cols) for w, cols in weights]
    gain_sum, shift_sum = 0.0, 0.0
    for x, out, place in ((x_own, da_own, core), (x_oth, da_oth, 1 - core)):
        at = pl.ds(pl.multiple_of(place * tokens, tokens), tokens)
        e = sum(mm_t(d[at, :], w) for d, w in zip(dkvs, pairs))
        if x is x_own:
            e = e + sum(mm_t(dq[...], w[0, :, cols]) for dq, (w, cols) in zip(dqs, weights))
        out[...] = e.astype(out.dtype)
        n, _ = normalised(x[...].astype(F32))
        gain_sum = gain_sum + total_rows(e * n)
        shift_sum = shift_sum + total_rows(e)
    put_norms(norm_ref, gain_sum, shift_sum)


def finish_input(x_own, first_grad_ref, da_own, da_got, gain, out_ref):
    n, inv = normalised(x_own[...].astype(F32))
    e = da_own[...] + da_got[...].astype(F32)
    out_ref[...] = first_grad_ref[...] + norm_back(n, inv, gain[0:1, :], e)


def finish_norms(a_ref, b_ref, gain_ref, shift_ref):
    v = a_ref[...].astype(F32) + b_ref[...].astype(F32)
    width = gain_ref.shape[1] // 128
    for layer in range(gain_ref.shape[0]):
        for j in range(width):
            row = 2 * layer * width + j
            gain_ref[layer : layer + 1, j * 128 : (j + 1) * 128] = v[row : row + 1, :]
            shift_ref[layer : layer + 1, j * 128 : (j + 1) * 128] = v[row + width : row + width + 1, :]


def shape(dims, dtype):
    return pltpu.VMEM(dims, dtype)


def smem_shape(dims, dtype):
    return jax.ShapeDtypeStruct(dims, dtype)


def hbm_shape(dims, dtype):
    return jax.ShapeDtypeStruct(dims, dtype)


class Late:
    def __init__(self, copy, ref):
        self.copy, self.ref, self.pending = copy, ref, True

    def get(self):
        if self.pending:
            self.copy.wait()
            self.pending = False
        return self.ref


def call(body, outs, scratch, args, smem=(), smem_out=(), late=(), near=(), after=(), us=5.0, vmem=12, name=None):
    in_vmem = pl.BlockSpec(memory_space=pltpu.VMEM)
    in_smem = pl.BlockSpec(memory_space=pltpu.SMEM)
    anywhere = pl.BlockSpec(memory_space=pl.ANY)
    n_args, n_after, n_late = len(args), len(after), len(late)

    def wrapped(*refs):
        ins, rest = list(refs[:n_args]), refs[n_args + n_after :]
        if n_late:
            rest, held, sems = rest[: -n_late - 1], rest[-n_late - 1 : -1], rest[-1]
            for j, i in enumerate(late):
                copy = pltpu.make_async_copy(ins[i], held[j], sems.at[j])
                copy.start()
                ins[i] = Late(copy, held[j])
        body(*ins, *rest)

    kind = lambda i: in_smem if i in smem else anywhere if i in late else in_vmem
    held = [pltpu.VMEM(args[i].shape, args[i].dtype) for i in late]
    place = lambda i: pltpu.HBM if i in late else pltpu.VMEM
    args = [x if i in smem or i in near else pltpu.with_memory_space_constraint(x, place(i)) for i, x in enumerate(args)]
    return pl.pallas_call(
        wrapped,
        out_shape=outs,
        in_specs=[kind(i) for i in range(n_args)] + [anywhere] * n_after,
        out_specs=[in_smem if i in smem_out else in_vmem for i in range(len(outs))],
        scratch_shapes=[x if not isinstance(x, tuple) else pltpu.VMEM(*x) for x in scratch]
        + held
        + ([pltpu.SemaphoreType.DMA((n_late,))] if n_late else []),
        compiler_params=pltpu.CompilerParams(vmem_limit_bytes=vmem * 1024 * 1024),
        cost_estimate=pl.CostEstimate(flops=int(us * 1.1e9), bytes_accessed=0, transcendentals=0),
        name=name,
    )(*args, *after)


FFN, CROSS, SELF_A, SELF_B = range(4)


def mask_orders(n):
    if n == 16:
        return [[[1, 2, 4, 8], [2, 1, 4, 8]], [[1, 2, 4, 8], [2, 1, 4, 8]], [[1, 2, 4, 8], [2, 1, 4, 8]], [[4, 1, 2, 8], [4, 2, 1, 8]]]
    base = [1 << j for j in range(n.bit_length() - 1)]
    return [[base, base[1:] + base[:1]]] * 4


def swap(x, n, masks):
    pairs = [(i * 2 + t, (i ^ masks[t]) * 2 + t) for i in range(n) for t in range(2)]
    return lax.ppermute(x, ("dp", "tensor"), pairs)


def other(x):
    return lax.ppermute(x, "tensor", [(0, 1), (1, 0)])


def reduction_plans():
    n = lax.axis_size("dp")
    index, core = lax.axis_index("dp").astype(jnp.uint32), lax.axis_index("tensor")
    plans = []
    for orders in mask_orders(n):
        place = lambda mask: (index >> jnp.uint32(mask.bit_length() - 1)) & jnp.uint32(1)
        bits = [jnp.where(core == 0, place(a), place(b)) for a, b in zip(*orders)]
        plans.append([(bit, jnp.uint32(1) - bit, bit == 0) for bit in bits])
    return plans


class Reduction:
    def __init__(self, g, stream, plans):
        n = lax.axis_size("dp")
        self.n, self.g = n, g
        self.masks = list(zip(*mask_orders(n)[stream]))
        self.plan = plans[stream]
        self.name = ("ffn", "cross", "self_a", "self_b")[stream]
        steps = list(range(len(self.masks)))
        split = steps[:-1] if stream in (FFN, CROSS) else steps[:-2]
        self.hops = [(j, "halve") for j in split]
        self.hops += [(j, "add") for j in steps[len(split) :]]
        self.hops += [(j, "join") for j in reversed(split)]
        self.done, self.extra = 0, None

    def send(self):
        j, kind = self.hops[self.done]
        if kind == "halve":
            halves = self.g.reshape((2, self.g.shape[0] // 2) + self.g.shape[1:])
            self.keep = lax.dynamic_index_in_dim(halves, self.plan[j][0], 0, False)
            out = lax.dynamic_index_in_dim(halves, self.plan[j][1], 0, False)
        else:
            out = self.g if self.extra is None else jnp.concatenate([self.g, self.extra], axis=0)
            self.keep = self.g
        with jax.named_scope(f"{self.name}_{kind}_{self.done}"):
            self.got = swap(out, self.n, self.masks[j])
        return out

    def receive(self, *after):
        j, kind = self.hops[self.done]
        if after:
            self.got = lax.optimization_barrier((self.got, *after))[0]
        self.done += 1
        got = self.got
        if kind != "halve" and self.extra is not None:
            rows = self.g.shape[0]
            total = self.extra.astype(F32) + got[rows:].astype(F32)
            self.extra = lax.reduce_precision(total, 8, 7).astype(BF16)
            got = got[:rows]
        if kind != "join":
            self.g = (self.keep.astype(F32) + got.astype(F32)).astype(BF16)
            return
        own, first = self.g, self.plan[j][2]
        self.low, self.high = jnp.where(first, own, got), jnp.where(first, got, own)
        if self.running():
            self.g = jnp.concatenate([self.low, self.high], axis=0)

    def hop(self, *after):
        self.receive(*after)
        return self.send()

    def running(self):
        return self.done < len(self.hops)

    def finish(self):
        while self.running():
            self.receive()
            if self.running():
                self.send()


def local(inputs, memory, tgt_seg, mem_seg, self_qkv, self_out, cross_q, cross_kv, cross_out, ffn_in, ffn_out, norm_gain, norm_bias, cotangent):
    x_own, m_own, cot = inputs[0], memory[0], cotangent[0]
    tokens, dim = x_own.shape
    seq = 2 * tokens
    half = cross_q.shape[1]
    ff = ffn_in.shape[1]
    pairs, blocks = dim // 128, tokens // QB
    flat, tree = jax.tree.flatten(reduction_plans())
    x_own, *flat = lax.optimization_barrier((x_own, *flat))
    plans = jax.tree.unflatten(tree, flat)
    x_oth, w_oth, so_oth = other(x_own), other(self_qkv), other(self_out)

    lse = shape((blocks, pairs, 1, 2 * QB), F32)
    full, part = shape((seq, dim), BF16), shape((tokens, dim), BF16)
    wide = shape((tokens, dim), F32)
    norm = shape((2 * dim // 128, 128), F32)
    col, win = shape((seq, 128), jnp.int32), shape((2 * blocks, 128), F32)
    work = [((dim, seq), BF16)]
    narrow = shape((tokens, half), BF16)
    a_own, q, k, v, tcol, mcol, gain, shift, tseg, twin, mwin = call(
        self_start,
        [part, narrow, narrow, narrow, col, col, shape((3, dim), F32), shape((3, dim), F32), shape((1, seq), jnp.int32), win, win],
        [],
        [x_own, self_qkv, norm_gain, norm_bias, tgt_seg, tgt_seg, mem_seg],
        smem=(4,), late=(5, 6, 0, 2, 3, 1), us=3.0, name="self_start",
    )
    later = lax.optimization_barrier((m_own, cross_q, cross_kv, cross_out, ffn_in, ffn_out, a_own))
    m_oth, cq_oth, ckv_oth, co_oth, fi_oth, fo_oth = [other(x) for x in later[:6]]
    at, q, k, v, o, lse_s, first = call(
        self_forward,
        [shape((dim, seq), BF16), part, full, full, part, lse, wide],
        work,
        [x_own, x_oth, self_qkv, w_oth, self_out, so_oth, a_own, q, k, v, gain, shift, twin, tseg, tcol],
        near=range(6), us=8.0, name="self_forward",
    )
    bt, mt, qc, kc, vc, oc, lse_c, second, c, ct = call(
        cross_forward,
        [shape((dim, tokens), BF16), shape((dim, seq), BF16), part, full, full, part, lse, wide, part, shape((dim, tokens), BF16)],
        work,
        [first, m_own, m_oth, cross_q, cq_oth, cross_kv, ckv_oth, cross_out, co_oth, gain, shift, mwin, tseg, mcol],
        near=range(1, 9), us=9.0, name="cross_forward",
    )
    g_ffn = shape((2 * ff, dim), BF16)
    y, dc, gf_oth = call(
        functools.partial(ffn_side, False), [wide, wide, g_ffn], [],
        [c, ct, cot, fi_oth, fo_oth, second], near=(2, 3, 4), us=6.0, name="ffn_other",
    )
    gf_got = other(gf_oth)
    out, second_grad, dy, gf_own, norm_ffn = call(
        functools.partial(ffn_side, True), [hbm_shape((tokens, dim), BF16), wide, part, g_ffn, norm],
        [((tokens, dim), F32), ((tokens, dim), F32)],
        [c, ct, cot, ffn_in, ffn_out, y, dc, second, gain], near=(2, 3, 4), after=[gf_oth], us=7.5, name="ffn_own",
    )
    red_f = Reduction(gf_own + gf_got, FFN, plans)

    def pair(pr, inside, args, after, name):
        return call(
            functools.partial(attention_pair, pr, half, inside),
            [shape((tokens, 128), BF16), shape((seq, 256), BF16), shape((4 * dim, 128), BF16)],
            [((tokens, 128), BF16), ((seq, 256), F32), ((128, seq), BF16)],
            args, near=(1,), after=after, us=4.0, name=name,
        )

    shared = [bt, mt, qc, kc, vc, oc, lse_c, mwin, tseg, mcol]
    dq2, dkv2, g2 = pair(2, False, [dy, co_oth] + shared, [red_f.send()], "cross_back_2")
    got0 = other(g2)
    dq3, dkv3, g3 = pair(3, False, [dy, co_oth] + shared, [g2], "cross_back_3")
    got1 = other(g3)
    dq0, dkv0, g0 = pair(0, False, [dy, cross_out] + shared, [g3, red_f.hop(dq3)], "cross_back_0")
    dq1, dkv1, g1 = pair(1, False, [dy, cross_out] + shared, [g0, red_f.hop(dq0)], "cross_back_1")
    red_c = Reduction(jnp.concatenate([g0 + got0, g1 + got1], axis=0), CROSS, plans)
    first_grad, dy, gm_own, gm_oth, norm_cross = call(
        cross_join, [wide, part, wide, part, norm], [],
        [first, second_grad, dq0, dq1, dq2, dq3, dkv0, dkv1, dkv2, dkv3, cross_q, cq_oth, cross_kv, ckv_oth, gain],
        near=(10, 11, 12, 13), after=[red_f.hop(dq1), red_c.send()], us=2.0, name="cross_join",
    )
    shared = [at, at, q, k, v, o, lse_s, twin, tseg, tcol]
    dq2, dkv2, g2 = pair(2, True, [dy, so_oth] + shared, [], "self_back_2")
    got0 = other(g2)
    dq3, dkv3, g3 = pair(3, True, [dy, so_oth] + shared, [g2, red_f.hop(dq2), red_c.hop(dq2)], "self_back_3")
    got1 = other(g3)
    dq0, dkv0, g0 = pair(0, True, [dy, self_out] + shared, [g3, red_f.hop(dq3), red_c.hop(dq3)], "self_back_0")
    red_s0 = Reduction(g0 + got0, SELF_A, plans)
    dq1, dkv1, g1 = pair(1, True, [dy, self_out] + shared, [red_f.hop(dq0), red_c.hop(dq0), red_s0.send()], "self_back_1")
    red_s1 = Reduction(g1 + got1, SELF_B, plans)
    first_sent = red_s1.send()
    red_s0.hop(dq1)
    red_c.hop(dq1)
    red_f.finish()
    grad_ffn_in = jnp.concatenate([red_f.low[j * dim : (j + 1) * dim] for j in range(ff // dim)], axis=1).astype(F32)
    grad_ffn_out = red_f.high.astype(F32)

    def lead(*done):
        leader = red_s1.got
        red_s1.got, *done = lax.optimization_barrier((leader, *done))
        sent = red_s1.hop()
        for r in (red_s0, red_c):
            if r.running():
                r.receive(leader)
                if r.running():
                    r.send()
        return sent, done

    da_own, da_oth, norm_self = call(
        self_join, [wide, part, norm], [],
        [x_own, x_oth, dq0, dq1, dq2, dq3, dkv0, dkv1, dkv2, dkv3, self_qkv, w_oth],
        near=(0, 1, 10, 11), after=[first_sent], us=2.0, name="self_join",
    )
    da_got, gm_got = other(da_oth), other(gm_oth)
    norms = jnp.concatenate([norm_self, norm_cross, norm_ffn], axis=0)
    norms = jnp.pad(lax.reduce_precision(norms, 8, 7).astype(BF16), ((0, -norms.shape[0] % 16), (0, 0)))
    red_s0.extra = norms
    _, (grad_ffn_in, grad_ffn_out) = lead(grad_ffn_in, grad_ffn_out)
    sent, _ = lead(da_oth)
    (grad_input,) = call(
        finish_input, [hbm_shape((tokens, dim), F32)], [], [x_own, first_grad, da_own, da_got, gain],
        near=(0, 3), after=[sent], us=2.0, name="finish_input",
    )
    grad_memory = gm_own + gm_got.astype(F32)
    sent, (grad_input, grad_memory) = lead(grad_input, grad_memory)
    while red_s1.done < len(red_s1.hops) - 1:
        lead()
    red_s0.finish()
    red_c.finish()
    norm_shape = hbm_shape((3, dim), F32)
    grad_gain, grad_shift = call(finish_norms, [norm_shape, norm_shape], [], [red_s0.extra, other(red_s0.extra)], near=(0, 1), us=1.0, name="finish_norms")

    def stack_columns(g):
        return jnp.concatenate([g[j * 128 : (j + 1) * 128] for j in range(dim // 128)], axis=1)

    cross = [jnp.concatenate([red_c.low[j * dim : (j + 1) * dim], red_c.high[j * dim : (j + 1) * dim]], axis=1) for j in range(3)]
    early = [
        cross[0].astype(F32),
        jnp.stack(cross[1:]).astype(F32),
        jnp.concatenate([stack_columns(red_c.low[3 * dim :]), stack_columns(red_c.high[3 * dim :])], axis=0).astype(F32),
        grad_gain,
        grad_shift,
    ]
    red_s1.got, *early = lax.optimization_barrier((red_s1.got, *early))
    red_s1.receive()
    selves = [[r.low[:dim], r.low[dim:], r.high[:dim], r.high[dim:]] for r in (red_s0, red_s1)]
    grad_self_qkv = jnp.stack([jnp.concatenate([selves[0][j], selves[1][j]], axis=1) for j in range(3)]).astype(F32)
    grad_self_out = jnp.concatenate([stack_columns(selves[0][3]), stack_columns(selves[1][3])], axis=0).astype(F32)
    return (
        out[None], grad_input[None], grad_memory[None], grad_self_qkv, grad_self_out,
        *early[:3], grad_ffn_in, grad_ffn_out, *early[3:],
    )


def solution(mesh):
    tokens = P("dp", "tensor", None)
    columns, rows = P(None, "tensor"), P("tensor", None)
    stacked = P(None, None, "tensor")
    return jax.shard_map(
        local,
        mesh=mesh,
        in_specs=(tokens, tokens, P("dp", None), P("dp", None), stacked, rows, columns, stacked, rows, columns, rows, P(), P(), tokens),
        out_specs=(tokens, tokens, tokens, stacked, rows, columns, stacked, rows, columns, rows, P(), P()),
        check_vma=False,
    )
```

```python
import functools
import math

import jax
import jax.numpy as jnp
from jax import lax
from jax.experimental import pallas as pl
from jax.experimental.pallas import tpu as pltpu
from jax.sharding import PartitionSpec as P

F32 = jnp.float32
BF16 = jnp.bfloat16
HD = 64
QB = 128
EPS = 1e-05
NEG = -1e9
LN2 = math.log(2.0)
QSCALE = HD**-0.5 / LN2
SAFE = 1e4


def mm(a, b):
    return lax.dot_general(a, b, (((1,), (0,)), ((), ())), preferred_element_type=F32)


def mm_t(a, b):
    return lax.dot_general(a, b, (((1,), (1,)), ((), ())), preferred_element_type=F32)


def normalised(v):
    centred = v - jnp.mean(v, axis=-1, keepdims=True)
    inv = lax.rsqrt(jnp.mean(centred * centred, axis=-1, keepdims=True) + EPS)
    return centred * inv, inv


def norm_back(n, inv, gain, e):
    ge = gain * e
    return (ge - jnp.mean(ge, axis=-1, keepdims=True) - n * jnp.mean(ge * n, axis=-1, keepdims=True)) * inv


def put_norms(norm_ref, gain_term, shift_term):
    width = gain_term.shape[1] // 128
    for i, term in enumerate((gain_term, shift_term)):
        for j in range(width):
            norm_ref[i * width + j : i * width + j + 1, :] = term[:, j * 128 : (j + 1) * 128]


def total_rows(v):
    return jnp.sum(v, axis=0, keepdims=True)


def count_below(seg, value):
    return jnp.sum(jnp.where(seg < value, 1.0, 0.0))


def windows(core, tokens, seg_q_smem, seg_k_ref, win_ref):
    seg_k = seg_k_ref[...]
    for qb in range(tokens // QB):
        first = core * tokens + qb * QB
        win_ref[2 * qb : 2 * qb + 1, :] = jnp.full((1, 128), count_below(seg_k, seg_q_smem[0, first]))
        win_ref[2 * qb + 1 : 2 * qb + 2, :] = jnp.full((1, 128), count_below(seg_k, seg_q_smem[0, first + QB - 1] + 1))


def bounds(win_ref, qb):
    lo, hi = [jnp.max(win_ref[pl.ds(2 * qb + j, 1), :]).astype(jnp.int32) for j in range(2)]
    return lo // 128 * 128, hi


def by_width(seq, lo, hi, run, rest, safe=True):
    need = hi - lo
    few, most = seq // 4, seq // 8 * 7
    at = lambda w: pl.multiple_of(jnp.minimum(lo, seq - w), 128)
    fits = jnp.logical_and(need <= most, safe)

    @pl.when(jnp.logical_and(fits, need <= few))
    def _():
        run(few, at(few))

    @pl.when(jnp.logical_and(fits, need > few))
    def _():
        run(most, at(most))

    @pl.when(jnp.logical_not(fits))
    def _():
        rest()


def seg_columns(seg_k_ref, out_ref):
    seq = seg_k_ref.shape[1]
    for j in range(seq // 128):
        row = jnp.broadcast_to(seg_k_ref[:, j * 128 : (j + 1) * 128], (128, 128))
        out_ref[j * 128 : (j + 1) * 128, :] = row.T


def two_heads(x):
    lane = lax.broadcasted_iota(jnp.int32, x.shape, 1)
    zero = jnp.zeros_like(x)
    return jnp.concatenate([jnp.where(lane < HD, x, zero), jnp.where(lane >= HD, x, zero)], axis=0)


def masked(s, segcol_ref, keys, seg_q_row):
    same = segcol_ref[keys, :] == seg_q_row
    return jnp.concatenate([jnp.where(same, s[:, :QB], NEG), jnp.where(same, s[:, QB:], NEG)], axis=1)


def head_norms(x):
    row = lax.broadcasted_iota(jnp.int32, (x.shape[1], 128), 0) // HD
    lane = lax.broadcasted_iota(jnp.int32, (x.shape[1], 128), 1)
    pick = jnp.where(row == lane, 1.0, 0.0).astype(BF16)
    xf = x.astype(F32)
    return jnp.max(mm((xf * xf).astype(BF16), pick), axis=0, keepdims=True)


def attend_forward(core, q_ref, k_ref, v_ref, win_ref, seg_q_ref, segcol_ref, o_ref, lse_ref, vt_ref):
    tokens, width = q_ref.shape
    vt_ref[...] = v_ref[...].T
    seq = k_ref.shape[0]
    pairs = width // 128
    small = jnp.max(head_norms(q_ref[...]) * head_norms(k_ref[...])) < SAFE

    def place(qb):
        first = pl.multiple_of(core * tokens + qb * QB, QB)
        return pl.ds(pl.multiple_of(qb * QB, QB), QB), seg_q_ref[:, pl.ds(first, QB)]

    def finish(qb, pr, rows, cols, ot, total, m):
        ot = ot / total
        ot = jnp.concatenate([ot[:HD, :QB], ot[HD:, QB:]], axis=0)
        o_ref[rows, cols] = ot.T.astype(BF16)
        lse_ref[qb, pr] = m + jnp.log2(total)

    def block(qb, carry):
        rows, seg_row = place(qb)

        def run(w, base):
            for pr in range(pairs):
                cols = slice(pr * 128, (pr + 1) * 128)
                q2 = two_heads(q_ref[rows, cols])
                ot = jnp.zeros((128, 2 * QB), F32)
                total = jnp.zeros((1, 2 * QB), F32)
                for c in range(0, w, 256):
                    keys = pl.ds(base + c, min(256, w - c))
                    e = jnp.exp2(masked(mm_t(k_ref[keys, cols], q2), segcol_ref, keys, seg_row))
                    total = total + jnp.sum(e, axis=0, keepdims=True)
                    ot = ot + mm(vt_ref[cols, keys], e.astype(BF16))
                finish(qb, pr, rows, cols, ot, total, 0.0)

        def rest():
            def pair(pr, carry):
                cols = pl.ds(pl.multiple_of(pr * 128, 128), 128)
                q2 = two_heads(q_ref[rows, cols])

                def scores(j):
                    keys = pl.ds(pl.multiple_of(j * 256, 256), 256)
                    return keys, masked(mm_t(k_ref[keys, cols], q2), segcol_ref, keys, seg_row)

                def largest(j, m):
                    return jnp.maximum(m, jnp.max(scores(j)[1], axis=0, keepdims=True))

                m = lax.fori_loop(0, seq // 256, largest, jnp.full((1, 2 * QB), 2 * NEG, F32))

                def gather(j, acc):
                    keys, s = scores(j)
                    e = jnp.exp2(s - m)
                    return acc[0] + jnp.sum(e, axis=0, keepdims=True), acc[1] + mm(vt_ref[cols, keys], e.astype(BF16))

                start = (jnp.zeros((1, 2 * QB), F32), jnp.zeros((128, 2 * QB), F32))
                total, ot = lax.fori_loop(0, seq // 256, gather, start)
                finish(qb, pr, rows, cols, ot, total, m)
                return carry

            lax.fori_loop(0, pairs, pair, 0)

        by_width(seq, *bounds(win_ref, qb), run, rest, small)
        return carry

    lax.fori_loop(0, tokens // QB, block, 0)


def attend_backward(core, pr, q_ref, k_ref, v_ref, win_ref, seg_q_ref, segcol_ref, o_ref, do_ref, lse_ref, dq_ref, dkv_ref, kt_ref):
    tokens = q_ref.shape[0]
    seq = k_ref.shape[0]
    cols = slice(pr * 128, (pr + 1) * 128)
    kt_ref[...] = k_ref[:, cols].T
    dkv_ref[...] = jnp.zeros_like(dkv_ref)

    def block(qb, carry):
        first = pl.multiple_of(core * tokens + qb * QB, QB)
        rows = pl.ds(pl.multiple_of(qb * QB, QB), QB)
        seg_row = seg_q_ref[:, pl.ds(first, QB)]

        def operands():
            do = do_ref[rows, :]
            inner = (do.astype(F32) * o_ref[rows, cols].astype(F32)).T
            inner = jnp.concatenate([total_rows(inner[:HD]), total_rows(inner[HD:])], axis=1)
            return two_heads(q_ref[rows, cols]), two_heads(do), inner

        def part(keys, q2, do2, inner):
            s = masked(mm_t(k_ref[keys, cols], q2), segcol_ref, keys, seg_row)
            p = jnp.exp2(s - lse_ref[qb, pr])
            dkv_ref[keys, 128:] += mm(p.astype(BF16), do2)
            ds = (p * (mm_t(v_ref[keys, cols], do2) - inner)).astype(BF16)
            dkv_ref[keys, :128] += mm(ds, q2)
            return mm(kt_ref[:, keys], ds)

        def finish(dqt):
            dqt = jnp.concatenate([dqt[:HD, :QB], dqt[HD:, QB:]], axis=0) * HD**-0.5
            dq_ref[rows, :] = dqt.T.astype(BF16)

        def run(w, base):
            finish(part(pl.ds(base, w), *operands()))

        def rest():
            given = operands()
            step = lambda j, dqt: dqt + part(pl.ds(pl.multiple_of(j * 256, 256), 256), *given)
            finish(lax.fori_loop(0, seq // 256, step, jnp.zeros((128, 2 * QB), F32)))

        by_width(seq, *bounds(win_ref, qb), run, rest)
        return carry

    lax.fori_loop(0, tokens // QB, block, 0)


def self_start(
    x_own, w_own, gain, shift, tseg_s, tseg, mseg,
    a_ref, q_ref, k_ref, v_ref, tcol_ref, mcol_ref, gain_ref, shift_ref, seg_ref, twin_ref, mwin_ref,
):
    core = lax.axis_index("tensor")
    tseg, mseg = tseg.get(), mseg.get()
    seg_ref[...] = tseg[...]
    windows(core, q_ref.shape[0], tseg_s, tseg, twin_ref)
    windows(core, q_ref.shape[0], tseg_s, mseg, mwin_ref)
    seg_columns(tseg, tcol_ref)
    seg_columns(mseg, mcol_ref)
    gain_ref[...] = gain.get()[...]
    shift_ref[...] = shift.get()[...]
    n, _ = normalised(x_own.get()[...].astype(F32))
    a = (n * gain_ref[0:1, :] + shift_ref[0:1, :]).astype(BF16)
    a_ref[...] = a
    w = w_own.get()
    q_ref[...] = (mm(a, w[0]) * QSCALE).astype(BF16)
    k_ref[...] = mm(a, w[1]).astype(BF16)
    v_ref[...] = mm(a, w[2]).astype(BF16)


def self_forward(
    x_own, x_oth, w_own, w_oth, so_own, so_oth, a_own, q_in, k_in, v_in, gain, shift, twin_ref, tseg, tcol_ref,
    at_ref, q_ref, k_ref, v_ref, o_ref, lse_ref, first_ref,
    *work,
):
    core = lax.axis_index("tensor")
    tokens, half = q_in.shape
    own, oth = slice(0, half), slice(half, 2 * half)
    here = pl.ds(pl.multiple_of(core * tokens, tokens), tokens)
    there = pl.ds(pl.multiple_of((1 - core) * tokens, tokens), tokens)
    a = a_own[...]
    at_ref[:, here] = a.T
    q_ref[:, own] = q_in[...]
    k_ref[here, own] = k_in[...]
    v_ref[here, own] = v_in[...]
    n, _ = normalised(x_oth[...].astype(F32))
    a2 = (n * gain[0:1, :] + shift[0:1, :]).astype(BF16)
    at_ref[:, there] = a2.T
    w = w_oth
    q_ref[:, oth] = (mm(a, w[0]) * QSCALE).astype(BF16)
    k_ref[here, oth] = mm(a, w[1]).astype(BF16)
    v_ref[here, oth] = mm(a, w[2]).astype(BF16)
    k_ref[there, oth] = mm(a2, w[1]).astype(BF16)
    v_ref[there, oth] = mm(a2, w[2]).astype(BF16)
    w = w_own
    k_ref[there, own] = mm(a2, w[1]).astype(BF16)
    v_ref[there, own] = mm(a2, w[2]).astype(BF16)
    attend_forward(core, q_ref, k_ref, v_ref, twin_ref, tseg, tcol_ref, o_ref, lse_ref, *work)
    first_ref[...] = x_own[...].astype(F32) + mm(o_ref[:, own], so_own[...]) + mm(o_ref[:, oth], so_oth[...])


def gelu_parts(h):
    z = jnp.abs(h)
    t = 1.0 / (1.0 + (0.3275911 / math.sqrt(2.0)) * z)
    poly = t * (0.254829592 + t * (-0.284496736 + t * (1.421413741 + t * (-1.453152027 + t * 1.061405429))))
    gauss = jnp.exp2(h * h * (-0.5 / LN2))
    tail = 0.5 * poly * gauss
    cdf = jnp.where(h >= 0, 1.0 - tail, tail)
    return cdf, gauss * (1.0 / math.sqrt(2.0 * math.pi))


def cross_forward(
    first_ref, m_own, m_oth, q_own, q_oth, kv_own, kv_oth, co_own, co_oth, gain, shift, win_ref, tseg, mcol_ref,
    bt_ref, mt_ref, q_ref, k_ref, v_ref, o_ref, lse_ref, second_ref, c_ref, ct_ref,
    *work,
):
    core = lax.axis_index("tensor")
    tokens, _ = first_ref.shape
    half = kv_own.shape[2]
    n, _ = normalised(first_ref[...])
    b = (n * gain[1:2, :] + shift[1:2, :]).astype(BF16)
    bt_ref[...] = b.T
    sides = ((q_own, kv_own, slice(0, half)), (q_oth, kv_oth, slice(half, 2 * half)))
    for w, _, cols in sides:
        q_ref[:, cols] = (mm(b, w[...]) * QSCALE).astype(BF16)
    for m, place in ((m_own, core), (m_oth, 1 - core)):
        at = pl.ds(pl.multiple_of(place * tokens, tokens), tokens)
        m = m[...]
        mt_ref[:, at] = m.T
        for _, kv, cols in sides:
            k_ref[at, cols] = mm(m, kv[0]).astype(BF16)
            v_ref[at, cols] = mm(m, kv[1]).astype(BF16)
    attend_forward(core, q_ref, k_ref, v_ref, win_ref, tseg, mcol_ref, o_ref, lse_ref, *work)
    second = first_ref[...] + mm(o_ref[:, :half], co_own[...]) + mm(o_ref[:, half:], co_oth[...])
    second_ref[...] = second
    n, _ = normalised(second)
    c = (n * gain[2:3, :] + shift[2:3, :]).astype(BF16)
    c_ref[...] = c
    ct_ref[...] = c.T


def ffn_side(last, *refs):
    if last:
        c_ref, ct, cot_ref, fi, fo, y_in, dc_in, second_ref, gain, out_ref, second_grad_ref, dy_ref, g, norm_ref, y_ref, dc_ref = refs
        y_ref[...] = y_in[...]
        dc_ref[...] = dc_in[...]
    else:
        c_ref, ct, cot_ref, fi, fo, second_ref, y_ref, dc_ref, g = refs
        y_ref[...] = second_ref[...]
        dc_ref[...] = jnp.zeros_like(dc_ref)
    dim = c_ref.shape[1]
    ff_half = fi.shape[1]
    chunk = 512
    per = dim // chunk

    def step(j, carry):
        at = pl.ds(pl.multiple_of(j * chunk, chunk), chunk)
        cot = cot_ref[...]
        h = mm(c_ref[...], fi[:, at])
        cdf, pdf = gelu_parts(h)
        act = (h * cdf).astype(BF16)
        y_ref[...] += mm(act, fo[at, :])
        dh = (mm_t(cot, fo[at, :]) * (cdf + h * pdf)).astype(BF16)
        dc_ref[...] += mm_t(dh, fi[:, at])
        gi_rows = pl.ds(pl.multiple_of(j // per * dim, dim), dim)
        g[gi_rows, pl.ds(pl.multiple_of(j % per * chunk, chunk), chunk)] = mm(ct[...], dh).astype(BF16)
        g[pl.ds(pl.multiple_of(ff_half + j * chunk, chunk), chunk), :] = mm(act.T, cot).astype(BF16)
        return carry

    lax.fori_loop(0, ff_half // chunk, step, 0)
    if last:
        out_ref[...] = y_ref[...].astype(BF16)
        n, inv = normalised(second_ref[...])
        e = dc_ref[...]
        put_norms(norm_ref, total_rows(e * n), total_rows(e))
        second_grad = cot_ref[...].astype(F32) + norm_back(n, inv, gain[2:3, :], e)
        second_grad_ref[...] = second_grad
        dy_ref[...] = second_grad.astype(BF16)


def attention_pair(pr, half, inside, *refs):
    dy_ref, w_out, xqt_ref, xt_ref, q_ref, k_ref, v_ref, o_ref, lse_ref, win_ref, tseg, segcol_ref = refs[:12]
    dq_ref, dkv_out, g_ref, do_ref, dkv_ref, *work = refs[12:]
    core = lax.axis_index("tensor")
    tokens, dim = dy_ref.shape
    cols = slice(pr * 128, (pr + 1) * 128)
    start = pr * 128 % half
    dy = dy_ref[...]
    do_ref[...] = mm_t(dy, w_out[start : start + 128, :]).astype(BF16)
    out = mm(o_ref[:, cols].T, dy).astype(BF16)
    for j in range(dim // 128):
        g_ref[3 * dim + j * 128 : 3 * dim + (j + 1) * 128, :] = out[:, j * 128 : (j + 1) * 128]
    attend_backward(core, pr, q_ref, k_ref, v_ref, win_ref, tseg, segcol_ref, o_ref, do_ref, lse_ref, dq_ref, dkv_ref, *work)
    dkv_out[:, :128] = (dkv_ref[:, :128] * LN2).astype(BF16)
    dkv_out[:, 128:] = dkv_ref[:, 128:].astype(BF16)
    xqt = xt_ref[:, pl.ds(pl.multiple_of(core * tokens, tokens), tokens)] if inside else xqt_ref[...]
    g_ref[0:dim, :] = mm(xqt, dq_ref[...]).astype(BF16)
    gkv = mm(xt_ref[...], dkv_out[...]).astype(BF16)
    g_ref[dim : 2 * dim, :] = gkv[:, :128]
    g_ref[2 * dim : 3 * dim, :] = gkv[:, 128:]


def both(first, second, cols):
    return jnp.concatenate([first[:, cols], second[:, cols]], axis=1)


def cross_join(first_ref, second_grad_ref, *refs):
    dqs, dkvs = refs[0:4], refs[4:8]
    q_own, q_oth, kv_own, kv_oth, gain, first_grad_ref, dy_ref, gm_own, gm_oth, norm_ref = refs[8:]
    core = lax.axis_index("tensor")
    tokens, _ = first_ref.shape
    half = q_own.shape[1]
    weights = []
    for pr in range(len(dqs)):
        near = pr * 128 < half
        cols = slice(pr * 128 % half, pr * 128 % half + 128)
        weights.append((q_own if near else q_oth, kv_own if near else kv_oth, cols))
    db = sum(mm_t(dq[...], q[:, cols]) for dq, (q, _, cols) in zip(dqs, weights))
    n, inv = normalised(first_ref[...])
    put_norms(norm_ref, total_rows(db * n), total_rows(db))
    first_grad = second_grad_ref[...] + norm_back(n, inv, gain[1:2, :], db)
    first_grad_ref[...] = first_grad
    dy_ref[...] = first_grad.astype(BF16)
    pairs = [both(kv.at[0], kv.at[1], cols) for _, kv, cols in weights]
    for out, place in ((gm_own, core), (gm_oth, 1 - core)):
        at = pl.ds(pl.multiple_of(place * tokens, tokens), tokens)
        out[...] = sum(mm_t(d[at, :], w) for d, w in zip(dkvs, pairs)).astype(out.dtype)


def self_join(x_own, x_oth, *refs):
    dqs, dkvs = refs[0:4], refs[4:8]
    w_own, w_oth, da_own, da_oth, norm_ref = refs[8:]
    core = lax.axis_index("tensor")
    tokens, _ = x_own.shape
    half = w_own.shape[2]
    weights = []
    for pr in range(len(dqs)):
        weights.append((w_own if pr * 128 < half else w_oth, slice(pr * 128 % half, pr * 128 % half + 128)))
    pairs = [both(w.at[1], w.at[2], cols) for w, cols in weights]
    gain_sum, shift_sum = 0.0, 0.0
    for x, out, place in ((x_own, da_own, core), (x_oth, da_oth, 1 - core)):
        at = pl.ds(pl.multiple_of(place * tokens, tokens), tokens)
        e = sum(mm_t(d[at, :], w) for d, w in zip(dkvs, pairs))
        if x is x_own:
            e = e + sum(mm_t(dq[...], w[0, :, cols]) for dq, (w, cols) in zip(dqs, weights))
        out[...] = e.astype(out.dtype)
        n, _ = normalised(x[...].astype(F32))
        gain_sum = gain_sum + total_rows(e * n)
        shift_sum = shift_sum + total_rows(e)
    put_norms(norm_ref, gain_sum, shift_sum)


def finish_input(x_own, first_grad_ref, da_own, da_got, gain, out_ref):
    n, inv = normalised(x_own[...].astype(F32))
    e = da_own[...] + da_got[...].astype(F32)
    out_ref[...] = first_grad_ref[...] + norm_back(n, inv, gain[0:1, :], e)


def finish_norms(sums_ref, gain_ref, shift_ref):
    v = sums_ref[...].astype(F32)
    width = gain_ref.shape[1] // 128
    for layer in range(gain_ref.shape[0]):
        for j in range(width):
            row = 2 * layer * width + j
            gain_ref[layer : layer + 1, j * 128 : (j + 1) * 128] = v[row : row + 1, :]
            shift_ref[layer : layer + 1, j * 128 : (j + 1) * 128] = v[row + width : row + width + 1, :]


def unpack(pieces, heads_refs, out_ref):
    dim = heads_refs[0].shape[-2]
    for p, rows in enumerate(pieces):
        cols = slice(p * 128, (p + 1) * 128)
        for j, ref in enumerate(heads_refs):
            ref[:, cols] = rows(j * dim, dim).astype(F32)
        for j in range(dim // 128):
            out_ref[cols, j * 128 : (j + 1) * 128] = rows(len(heads_refs) * dim + j * 128, 128).astype(F32)


def finish_cross(low_ref, high_ref, q_ref, kv_ref, out_ref):
    pieces = [lambda at, n, ref=ref: ref[at : at + n, :] for ref in (low_ref, high_ref)]
    unpack(pieces, [q_ref, kv_ref.at[0], kv_ref.at[1]], out_ref)


def finish_self(low_a, high_a, low_b, high_b, qkv_ref, out_ref):
    half = low_a.shape[0]

    def rows(low, high):
        return lambda at, n: low[at : at + n, :] if at < half else high[at - half : at - half + n, :]

    unpack([rows(low_a, high_a), rows(low_b, high_b)], [qkv_ref.at[j] for j in range(3)], out_ref)


def shape(dims, dtype):
    return pltpu.VMEM(dims, dtype)


def smem_shape(dims, dtype):
    return jax.ShapeDtypeStruct(dims, dtype)


def hbm_shape(dims, dtype):
    return jax.ShapeDtypeStruct(dims, dtype)


class Late:
    def __init__(self, copy, ref):
        self.copy, self.ref, self.pending = copy, ref, True

    def get(self):
        if self.pending:
            self.copy.wait()
            self.pending = False
        return self.ref


def call(body, outs, scratch, args, smem=(), smem_out=(), late=(), near=(), after=(), us=5.0, vmem=12, name=None):
    in_vmem = pl.BlockSpec(memory_space=pltpu.VMEM)
    in_smem = pl.BlockSpec(memory_space=pltpu.SMEM)
    anywhere = pl.BlockSpec(memory_space=pl.ANY)
    n_args, n_after, n_late = len(args), len(after), len(late)

    def wrapped(*refs):
        ins, rest = list(refs[:n_args]), refs[n_args + n_after :]
        if n_late:
            rest, held, sems = rest[: -n_late - 1], rest[-n_late - 1 : -1], rest[-1]
            for j, i in enumerate(late):
                copy = pltpu.make_async_copy(ins[i], held[j], sems.at[j])
                copy.start()
                ins[i] = Late(copy, held[j])
        body(*ins, *rest)

    kind = lambda i: in_smem if i in smem else anywhere if i in late else in_vmem
    held = [pltpu.VMEM(args[i].shape, args[i].dtype) for i in late]
    place = lambda i: pltpu.HBM if i in late else pltpu.VMEM
    args = [x if i in smem or i in near else pltpu.with_memory_space_constraint(x, place(i)) for i, x in enumerate(args)]
    return pl.pallas_call(
        wrapped,
        out_shape=outs,
        in_specs=[kind(i) for i in range(n_args)] + [anywhere] * n_after,
        out_specs=[in_smem if i in smem_out else in_vmem for i in range(len(outs))],
        scratch_shapes=[x if not isinstance(x, tuple) else pltpu.VMEM(*x) for x in scratch]
        + held
        + ([pltpu.SemaphoreType.DMA((n_late,))] if n_late else []),
        compiler_params=pltpu.CompilerParams(vmem_limit_bytes=vmem * 1024 * 1024),
        cost_estimate=pl.CostEstimate(flops=int(us * 1.1e9), bytes_accessed=0, transcendentals=0),
        name=name,
    )(*args, *after)


FFN, CROSS, SELF_A, SELF_B = range(4)


def mask_orders(n):
    if n == 16:
        return [[[1, 2, 4, 8], [2, 1, 4, 8]], [[1, 2, 4, 8], [2, 1, 4, 8]], [[1, 2, 4, 8], [1, 2, 4, 8]], [[4, 1, 2, 8], [4, 2, 1, 8]]]
    base = [1 << j for j in range(n.bit_length() - 1)]
    turned = [base, base[1:] + base[:1]]
    return [turned, turned, [base, base], turned]


def swap(x, n, masks):
    pairs = [(i * 2 + t, (i ^ masks[t]) * 2 + t) for i in range(n) for t in range(2)]
    return lax.ppermute(x, ("dp", "tensor"), pairs)


def other(x):
    return lax.ppermute(x, "tensor", [(0, 1), (1, 0)])


def reduction_plans():
    n = lax.axis_size("dp")
    index, core = lax.axis_index("dp").astype(jnp.uint32), lax.axis_index("tensor")
    plans = []
    for orders in mask_orders(n):
        place = lambda mask: (index >> jnp.uint32(mask.bit_length() - 1)) & jnp.uint32(1)
        bits = [jnp.where(core == 0, place(a), place(b)) for a, b in zip(*orders)]
        plans.append([(bit, jnp.uint32(1) - bit, bit == 0) for bit in bits])
    return plans


class Reduction:
    def __init__(self, g, stream, plans):
        n = lax.axis_size("dp")
        self.n, self.g = n, g
        self.masks = list(zip(*mask_orders(n)[stream]))
        self.plan = plans[stream]
        self.name = ("ffn", "cross", "self_a", "self_b")[stream]
        steps = list(range(len(self.masks)))
        split = steps[:-1] if stream in (FFN, CROSS) else steps[:-2]
        self.hops = [(j, "halve") for j in split]
        self.hops += [(j, "add") for j in steps[len(split) :]]
        self.hops += [(j, "join") for j in reversed(split)]
        self.done, self.extra = 0, None

    def send(self):
        j, kind = self.hops[self.done]
        if kind == "halve":
            halves = self.g.reshape((2, self.g.shape[0] // 2) + self.g.shape[1:])
            self.keep = lax.dynamic_index_in_dim(halves, self.plan[j][0], 0, False)
            out = lax.dynamic_index_in_dim(halves, self.plan[j][1], 0, False)
        else:
            out = self.g if self.extra is None else jnp.concatenate([self.g, self.extra], axis=0)
            self.keep = self.g
        with jax.named_scope(f"{self.name}_{kind}_{self.done}"):
            self.got = swap(out, self.n, self.masks[j])
        return out

    def receive(self, *after):
        j, kind = self.hops[self.done]
        if after:
            self.got = lax.optimization_barrier((self.got, *after))[0]
        self.done += 1
        got = self.got
        if kind != "halve" and self.extra is not None:
            rows = self.g.shape[0]
            total = self.extra.astype(F32) + got[rows:].astype(F32)
            self.extra = lax.reduce_precision(total, 8, 7).astype(BF16)
            got = got[:rows]
        if kind != "join":
            self.g = (self.keep.astype(F32) + got.astype(F32)).astype(BF16)
            return
        own, first = self.g, self.plan[j][2]
        self.low, self.high = jnp.where(first, own, got), jnp.where(first, got, own)
        if self.running():
            self.g = jnp.concatenate([self.low, self.high], axis=0)

    def hop(self, *after):
        self.receive(*after)
        return self.send()

    def running(self):
        return self.done < len(self.hops)

    def finish(self):
        while self.running():
            self.receive()
            if self.running():
                self.send()


def local(inputs, memory, tgt_seg, mem_seg, self_qkv, self_out, cross_q, cross_kv, cross_out, ffn_in, ffn_out, norm_gain, norm_bias, cotangent):
    x_own, m_own, cot = inputs[0], memory[0], cotangent[0]
    tokens, dim = x_own.shape
    seq = 2 * tokens
    half = cross_q.shape[1]
    ff = ffn_in.shape[1]
    pairs, blocks = dim // 128, tokens // QB
    flat, tree = jax.tree.flatten(reduction_plans())
    x_own, *flat = lax.optimization_barrier((x_own, *flat))
    plans = jax.tree.unflatten(tree, flat)
    x_oth, w_oth, so_oth = other(x_own), other(self_qkv), other(self_out)

    lse = shape((blocks, pairs, 1, 2 * QB), F32)
    full, part = shape((seq, dim), BF16), shape((tokens, dim), BF16)
    wide = shape((tokens, dim), F32)
    norm = shape((2 * dim // 128, 128), F32)
    col, win = shape((seq, 128), jnp.int32), shape((2 * blocks, 128), F32)
    work = [((dim, seq), BF16)]
    narrow = shape((tokens, half), BF16)
    a_own, q, k, v, tcol, mcol, gain, shift, tseg, twin, mwin = call(
        self_start,
        [part, narrow, narrow, narrow, col, col, shape((3, dim), F32), shape((3, dim), F32), shape((1, seq), jnp.int32), win, win],
        [],
        [x_own, self_qkv, norm_gain, norm_bias, tgt_seg, tgt_seg, mem_seg],
        smem=(4,), late=(5, 6, 0, 2, 3, 1), us=3.0, name="self_start",
    )
    later = lax.optimization_barrier((m_own, cross_q, cross_kv, cross_out, ffn_in, ffn_out, a_own))
    m_oth, cq_oth, ckv_oth, co_oth, fi_oth, fo_oth = [other(x) for x in later[:6]]
    at, q, k, v, o, lse_s, first = call(
        self_forward,
        [shape((dim, seq), BF16), part, full, full, part, lse, wide],
        work,
        [x_own, x_oth, self_qkv, w_oth, self_out, so_oth, a_own, q, k, v, gain, shift, twin, tseg, tcol],
        near=range(6), us=8.0, name="self_forward",
    )
    bt, mt, qc, kc, vc, oc, lse_c, second, c, ct = call(
        cross_forward,
        [shape((dim, tokens), BF16), shape((dim, seq), BF16), part, full, full, part, lse, wide, part, shape((dim, tokens), BF16)],
        work,
        [first, m_own, m_oth, cross_q, cq_oth, cross_kv, ckv_oth, cross_out, co_oth, gain, shift, mwin, tseg, mcol],
        near=range(1, 9), us=9.0, name="cross_forward",
    )
    g_ffn = shape((2 * ff, dim), BF16)
    y, dc, gf_oth = call(
        functools.partial(ffn_side, False), [wide, wide, g_ffn], [],
        [c, ct, cot, fi_oth, fo_oth, second], near=(2, 3, 4), us=6.0, name="ffn_other",
    )
    gf_got = other(gf_oth)
    out, second_grad, dy, gf_own, norm_ffn = call(
        functools.partial(ffn_side, True), [hbm_shape((tokens, dim), BF16), wide, part, g_ffn, norm],
        [((tokens, dim), F32), ((tokens, dim), F32)],
        [c, ct, cot, ffn_in, ffn_out, y, dc, second, gain], near=(2, 3, 4), after=[gf_oth], us=7.5, name="ffn_own",
    )
    red_f = Reduction(gf_own + gf_got, FFN, plans)

    def pair(pr, inside, args, after, name):
        return call(
            functools.partial(attention_pair, pr, half, inside),
            [shape((tokens, 128), BF16), shape((seq, 256), BF16), shape((4 * dim, 128), BF16)],
            [((tokens, 128), BF16), ((seq, 256), F32), ((128, seq), BF16)],
            args, near=(1,), after=after, us=4.0, name=name,
        )

    shared = [bt, mt, qc, kc, vc, oc, lse_c, mwin, tseg, mcol]
    dq2, dkv2, g2 = pair(2, False, [dy, co_oth] + shared, [red_f.send()], "cross_back_2")
    got0 = other(g2)
    dq3, dkv3, g3 = pair(3, False, [dy, co_oth] + shared, [g2], "cross_back_3")
    got1 = other(g3)
    dq0, dkv0, g0 = pair(0, False, [dy, cross_out] + shared, [g3, red_f.hop(dq3)], "cross_back_0")
    dq1, dkv1, g1 = pair(1, False, [dy, cross_out] + shared, [g0, red_f.hop(dq0)], "cross_back_1")
    red_c = Reduction(jnp.concatenate([g0 + got0, g1 + got1], axis=0), CROSS, plans)
    first_grad, dy, gm_own, gm_oth, norm_cross = call(
        cross_join, [wide, part, wide, part, norm], [],
        [first, second_grad, dq0, dq1, dq2, dq3, dkv0, dkv1, dkv2, dkv3, cross_q, cq_oth, cross_kv, ckv_oth, gain],
        near=(10, 11, 12, 13), after=[red_f.hop(dq1), red_c.send()], us=2.0, name="cross_join",
    )
    shared = [at, at, q, k, v, o, lse_s, twin, tseg, tcol]
    dq2, dkv2, g2 = pair(2, True, [dy, so_oth] + shared, [], "self_back_2")
    got0 = other(g2)
    dq3, dkv3, g3 = pair(3, True, [dy, so_oth] + shared, [g2, red_f.hop(dq2), red_c.hop(dq2)], "self_back_3")
    got1 = other(g3)
    dq0, dkv0, g0 = pair(0, True, [dy, self_out] + shared, [g3, red_f.hop(dq3), red_c.hop(dq3)], "self_back_0")
    red_s0 = Reduction(g0 + got0, SELF_A, plans)
    dq1, dkv1, g1 = pair(1, True, [dy, self_out] + shared, [red_f.hop(dq0), red_c.hop(dq0), red_s0.send()], "self_back_1")
    red_s1 = Reduction(g1 + got1, SELF_B, plans)
    first_sent = red_s1.send()
    red_s0.hop(dq1)
    red_c.hop(dq1)
    red_s1.got, red_f.got = lax.optimization_barrier((red_s1.got, red_f.got))
    red_f.finish()
    grad_ffn_in = jnp.concatenate([red_f.low[j * dim : (j + 1) * dim] for j in range(ff // dim)], axis=1).astype(F32)
    grad_ffn_out = red_f.high.astype(F32)

    def lead(*done):
        leader = red_s1.got
        red_s1.got, *done = lax.optimization_barrier((leader, *done))
        sent = red_s1.hop()
        for r in (red_s0, red_c):
            if r.running():
                r.receive(leader)
                if r.running():
                    r.send()
        return sent, done

    da_own, da_oth, norm_self = call(
        self_join, [wide, part, norm], [],
        [x_own, x_oth, dq0, dq1, dq2, dq3, dkv0, dkv1, dkv2, dkv3, self_qkv, w_oth],
        near=(0, 1, 10, 11), after=[first_sent], us=2.0, name="self_join",
    )
    da_got, gm_got = other(da_oth), other(gm_oth)
    norms = jnp.concatenate([norm_self, norm_cross, norm_ffn], axis=0)
    norms = norms + other(norms)
    norms = jnp.pad(lax.reduce_precision(norms, 8, 7).astype(BF16), ((0, -norms.shape[0] % 16), (0, 0)))
    red_s0.extra = norms
    lead(da_oth)
    sent, _ = lead()
    (grad_input,) = call(
        finish_input, [hbm_shape((tokens, dim), F32)], [], [x_own, first_grad, da_own, da_got, gain],
        near=(0, 3), after=[sent], us=2.0, name="finish_input",
    )
    grad_memory = gm_own + gm_got.astype(F32)
    sent, (grad_input, grad_memory, grad_ffn_in, grad_ffn_out) = lead(grad_input, grad_memory, grad_ffn_in, grad_ffn_out)
    while red_s1.done < len(red_s1.hops) - 1:
        lead()
    red_s0.finish()
    red_c.finish()
    norm_shape = hbm_shape((3, dim), F32)
    grad_gain, grad_shift = call(finish_norms, [norm_shape, norm_shape], [], [red_s0.extra], near=(0,), us=1.0, name="finish_norms")

    stacked = lambda n: hbm_shape((n, dim, half), F32)
    out_shape = hbm_shape((half, dim), F32)
    cross_grads = call(
        finish_cross, [hbm_shape((dim, half), F32), stacked(2), out_shape], [], [red_c.low, red_c.high],
        near=(0, 1), us=2.0, name="finish_cross",
    )
    early = [*cross_grads, grad_gain, grad_shift]
    red_s1.got, *early = lax.optimization_barrier((red_s1.got, *early))
    red_s1.receive()
    grad_self_qkv, grad_self_out = call(
        finish_self, [stacked(3), out_shape], [], [red_s0.low, red_s0.high, red_s1.low, red_s1.high],
        near=range(4), us=2.0, name="finish_self",
    )
    return (
        out[None], grad_input[None], grad_memory[None], grad_self_qkv, grad_self_out,
        *early[:3], grad_ffn_in, grad_ffn_out, *early[3:],
    )


def solution(mesh):
    tokens = P("dp", "tensor", None)
    columns, rows = P(None, "tensor"), P("tensor", None)
    stacked = P(None, None, "tensor")
    return jax.shard_map(
        local,
        mesh=mesh,
        in_specs=(tokens, tokens, P("dp", None), P("dp", None), stacked, rows, columns, stacked, rows, columns, rows, P(), P(), tokens),
        out_specs=(tokens, tokens, tokens, stacked, rows, columns, stacked, rows, columns, rows, P(), P()),
        check_vma=False,
    )
```

```python
import functools
import math

import jax
import jax.numpy as jnp
from jax import lax
from jax.experimental import pallas as pl
from jax.experimental.pallas import tpu as pltpu
from jax.sharding import PartitionSpec as P

F32 = jnp.float32
BF16 = jnp.bfloat16
HD = 64
QB = 128
EPS = 1e-05
NEG = -1e9
LN2 = math.log(2.0)
QSCALE = HD**-0.5 / LN2
SAFE = 1e4


def mm(a, b):
    return lax.dot_general(a, b, (((1,), (0,)), ((), ())), preferred_element_type=F32)


def mm_t(a, b):
    return lax.dot_general(a, b, (((1,), (1,)), ((), ())), preferred_element_type=F32)


def normalised(v):
    centred = v - jnp.mean(v, axis=-1, keepdims=True)
    inv = lax.rsqrt(jnp.mean(centred * centred, axis=-1, keepdims=True) + EPS)
    return centred * inv, inv


def norm_back(n, inv, gain, e):
    ge = gain * e
    return (ge - jnp.mean(ge, axis=-1, keepdims=True) - n * jnp.mean(ge * n, axis=-1, keepdims=True)) * inv


def put_norms(norm_ref, gain_term, shift_term):
    width = gain_term.shape[1] // 128
    for i, term in enumerate((gain_term, shift_term)):
        for j in range(width):
            norm_ref[i * width + j : i * width + j + 1, :] = term[:, j * 128 : (j + 1) * 128]


def total_rows(v):
    return jnp.sum(v, axis=0, keepdims=True)


def count_below(seg, value):
    return jnp.sum(jnp.where(seg < value, 1.0, 0.0))


def windows(core, tokens, seg_q_smem, seg_k_ref, win_ref):
    seg_k = seg_k_ref[...]
    for qb in range(tokens // QB):
        first = core * tokens + qb * QB
        win_ref[2 * qb : 2 * qb + 1, :] = jnp.full((1, 128), count_below(seg_k, seg_q_smem[0, first]))
        win_ref[2 * qb + 1 : 2 * qb + 2, :] = jnp.full((1, 128), count_below(seg_k, seg_q_smem[0, first + QB - 1] + 1))


def bounds(win_ref, qb):
    lo, hi = [jnp.max(win_ref[pl.ds(2 * qb + j, 1), :]).astype(jnp.int32) for j in range(2)]
    return lo // 128 * 128, hi


def by_width(seq, lo, hi, run, rest, safe=True):
    need = hi - lo
    few, most = seq // 4, seq // 8 * 7
    at = lambda w: pl.multiple_of(jnp.minimum(lo, seq - w), 128)
    fits = jnp.logical_and(need <= most, safe)

    @pl.when(jnp.logical_and(fits, need <= few))
    def _():
        run(few, at(few))

    @pl.when(jnp.logical_and(fits, need > few))
    def _():
        run(most, at(most))

    @pl.when(jnp.logical_not(fits))
    def _():
        rest()


def seg_columns(seg_k_ref, out_ref):
    seq = seg_k_ref.shape[1]
    for j in range(seq // 128):
        row = jnp.broadcast_to(seg_k_ref[:, j * 128 : (j + 1) * 128], (128, 128))
        out_ref[j * 128 : (j + 1) * 128, :] = row.T


def two_heads(x):
    lane = lax.broadcasted_iota(jnp.int32, x.shape, 1)
    zero = jnp.zeros_like(x)
    return jnp.concatenate([jnp.where(lane < HD, x, zero), jnp.where(lane >= HD, x, zero)], axis=0)


def masked(s, segcol_ref, keys, seg_q_row):
    same = segcol_ref[keys, :] == seg_q_row
    return jnp.concatenate([jnp.where(same, s[:, :QB], NEG), jnp.where(same, s[:, QB:], NEG)], axis=1)


def head_norms(x):
    row = lax.broadcasted_iota(jnp.int32, (x.shape[1], 128), 0) // HD
    lane = lax.broadcasted_iota(jnp.int32, (x.shape[1], 128), 1)
    pick = jnp.where(row == lane, 1.0, 0.0).astype(BF16)
    xf = x.astype(F32)
    return jnp.max(mm((xf * xf).astype(BF16), pick), axis=0, keepdims=True)


def attend_forward(core, q_ref, k_ref, v_ref, win_ref, seg_q_ref, segcol_ref, o_ref, lse_ref, vt_ref):
    tokens, width = q_ref.shape
    vt_ref[...] = v_ref[...].T
    seq = k_ref.shape[0]
    pairs = width // 128
    small = jnp.max(head_norms(q_ref[...]) * head_norms(k_ref[...])) < SAFE

    def place(qb):
        first = pl.multiple_of(core * tokens + qb * QB, QB)
        return pl.ds(pl.multiple_of(qb * QB, QB), QB), seg_q_ref[:, pl.ds(first, QB)]

    def finish(qb, pr, rows, cols, ot, total, m):
        ot = ot / total
        ot = jnp.concatenate([ot[:HD, :QB], ot[HD:, QB:]], axis=0)
        o_ref[rows, cols] = ot.T.astype(BF16)
        lse_ref[qb, pr] = m + jnp.log2(total)

    def block(qb, carry):
        rows, seg_row = place(qb)

        def run(w, base):
            for pr in range(pairs):
                cols = slice(pr * 128, (pr + 1) * 128)
                q2 = two_heads(q_ref[rows, cols])
                ot = jnp.zeros((128, 2 * QB), F32)
                total = jnp.zeros((1, 2 * QB), F32)
                for c in range(0, w, 256):
                    keys = pl.ds(base + c, min(256, w - c))
                    e = jnp.exp2(masked(mm_t(k_ref[keys, cols], q2), segcol_ref, keys, seg_row))
                    total = total + jnp.sum(e, axis=0, keepdims=True)
                    ot = ot + mm(vt_ref[cols, keys], e.astype(BF16))
                finish(qb, pr, rows, cols, ot, total, 0.0)

        def whole():
            def step(j, sums):
                keys = pl.ds(pl.multiple_of(j * 256, 256), 256)
                after = []
                for pr, (ot, total) in enumerate(sums):
                    cols = slice(pr * 128, (pr + 1) * 128)
                    q2 = two_heads(q_ref[rows, cols])
                    e = jnp.exp2(masked(mm_t(k_ref[keys, cols], q2), segcol_ref, keys, seg_row))
                    after.append((ot + mm(vt_ref[cols, keys], e.astype(BF16)), total + jnp.sum(e, axis=0, keepdims=True)))
                return tuple(after)

            start = (jnp.zeros((128, 2 * QB), F32), jnp.zeros((1, 2 * QB), F32))
            sums = lax.fori_loop(0, seq // 256, step, (start,) * pairs)
            for pr, (ot, total) in enumerate(sums):
                finish(qb, pr, rows, slice(pr * 128, (pr + 1) * 128), ot, total, 0.0)

        def with_max():
            def pair(pr, carry):
                cols = pl.ds(pl.multiple_of(pr * 128, 128), 128)
                q2 = two_heads(q_ref[rows, cols])

                def scores(j):
                    keys = pl.ds(pl.multiple_of(j * 256, 256), 256)
                    return keys, masked(mm_t(k_ref[keys, cols], q2), segcol_ref, keys, seg_row)

                def largest(j, m):
                    return jnp.maximum(m, jnp.max(scores(j)[1], axis=0, keepdims=True))

                m = lax.fori_loop(0, seq // 256, largest, jnp.full((1, 2 * QB), 2 * NEG, F32))

                def gather(j, acc):
                    keys, s = scores(j)
                    e = jnp.exp2(s - m)
                    return acc[0] + jnp.sum(e, axis=0, keepdims=True), acc[1] + mm(vt_ref[cols, keys], e.astype(BF16))

                start = (jnp.zeros((1, 2 * QB), F32), jnp.zeros((128, 2 * QB), F32))
                total, ot = lax.fori_loop(0, seq // 256, gather, start)
                finish(qb, pr, rows, cols, ot, total, m)
                return carry

            lax.fori_loop(0, pairs, pair, 0)

        def rest():
            pl.when(small)(whole)
            pl.when(jnp.logical_not(small))(with_max)

        by_width(seq, *bounds(win_ref, qb), run, rest, small)
        return carry

    lax.fori_loop(0, tokens // QB, block, 0)


def attend_backward(core, pr, q_ref, k_ref, v_ref, win_ref, seg_q_ref, segcol_ref, o_ref, do_ref, lse_ref, dq_ref, dkv_ref, kt_ref):
    tokens = q_ref.shape[0]
    seq = k_ref.shape[0]
    cols = slice(pr * 128, (pr + 1) * 128)
    kt_ref[...] = k_ref[:, cols].T
    dkv_ref[...] = jnp.zeros_like(dkv_ref)

    def block(qb, carry):
        first = pl.multiple_of(core * tokens + qb * QB, QB)
        rows = pl.ds(pl.multiple_of(qb * QB, QB), QB)
        seg_row = seg_q_ref[:, pl.ds(first, QB)]

        def operands():
            do = do_ref[rows, :]
            inner = (do.astype(F32) * o_ref[rows, cols].astype(F32)).T
            inner = jnp.concatenate([total_rows(inner[:HD]), total_rows(inner[HD:])], axis=1)
            return two_heads(q_ref[rows, cols]), two_heads(do), inner

        def part(keys, q2, do2, inner):
            s = masked(mm_t(k_ref[keys, cols], q2), segcol_ref, keys, seg_row)
            p = jnp.exp2(s - lse_ref[qb, pr])
            dkv_ref[keys, 128:] += mm(p.astype(BF16), do2)
            ds = (p * (mm_t(v_ref[keys, cols], do2) - inner)).astype(BF16)
            dkv_ref[keys, :128] += mm(ds, q2)
            return mm(kt_ref[:, keys], ds)

        def finish(dqt):
            dqt = jnp.concatenate([dqt[:HD, :QB], dqt[HD:, QB:]], axis=0) * HD**-0.5
            dq_ref[rows, :] = dqt.T.astype(BF16)

        def run(w, base):
            finish(part(pl.ds(base, w), *operands()))

        def rest():
            given = operands()
            step = lambda j, dqt: dqt + part(pl.ds(pl.multiple_of(j * 512, 512), 512), *given)
            finish(lax.fori_loop(0, seq // 512, step, jnp.zeros((128, 2 * QB), F32)))

        by_width(seq, *bounds(win_ref, qb), run, rest)
        return carry

    lax.fori_loop(0, tokens // QB, block, 0)


def self_start(
    x_own, w_own, gain, shift, tseg_s, tseg, mseg,
    a_ref, q_ref, k_ref, v_ref, tcol_ref, mcol_ref, gain_ref, shift_ref, seg_ref, twin_ref, mwin_ref,
):
    core = lax.axis_index("tensor")
    tseg, mseg = tseg.get(), mseg.get()
    seg_ref[...] = tseg[...]
    windows(core, q_ref.shape[0], tseg_s, tseg, twin_ref)
    windows(core, q_ref.shape[0], tseg_s, mseg, mwin_ref)
    seg_columns(tseg, tcol_ref)
    seg_columns(mseg, mcol_ref)
    gain_ref[...] = gain.get()[...]
    shift_ref[...] = shift.get()[...]
    n, _ = normalised(x_own.get()[...].astype(F32))
    a = (n * gain_ref[0:1, :] + shift_ref[0:1, :]).astype(BF16)
    a_ref[...] = a
    w = w_own.get()
    q_ref[...] = (mm(a, w[0]) * QSCALE).astype(BF16)
    k_ref[...] = mm(a, w[1]).astype(BF16)
    v_ref[...] = mm(a, w[2]).astype(BF16)


def self_forward(
    x_own, x_oth, w_own, w_oth, so_own, so_oth, a_own, q_in, k_in, v_in, gain, shift, twin_ref, tseg, tcol_ref,
    at_ref, q_ref, k_ref, v_ref, o_ref, lse_ref, first_ref,
    *work,
):
    core = lax.axis_index("tensor")
    tokens, half = q_in.shape
    own, oth = slice(0, half), slice(half, 2 * half)
    here = pl.ds(pl.multiple_of(core * tokens, tokens), tokens)
    there = pl.ds(pl.multiple_of((1 - core) * tokens, tokens), tokens)
    a = a_own[...]
    at_ref[:, here] = a.T
    q_ref[:, own] = q_in[...]
    k_ref[here, own] = k_in[...]
    v_ref[here, own] = v_in[...]
    n, _ = normalised(x_oth[...].astype(F32))
    a2 = (n * gain[0:1, :] + shift[0:1, :]).astype(BF16)
    at_ref[:, there] = a2.T
    w = w_oth
    q_ref[:, oth] = (mm(a, w[0]) * QSCALE).astype(BF16)
    k_ref[here, oth] = mm(a, w[1]).astype(BF16)
    v_ref[here, oth] = mm(a, w[2]).astype(BF16)
    k_ref[there, oth] = mm(a2, w[1]).astype(BF16)
    v_ref[there, oth] = mm(a2, w[2]).astype(BF16)
    w = w_own
    k_ref[there, own] = mm(a2, w[1]).astype(BF16)
    v_ref[there, own] = mm(a2, w[2]).astype(BF16)
    attend_forward(core, q_ref, k_ref, v_ref, twin_ref, tseg, tcol_ref, o_ref, lse_ref, *work)
    first_ref[...] = x_own[...].astype(F32) + mm(o_ref[:, own], so_own[...]) + mm(o_ref[:, oth], so_oth[...])


def gelu_parts(h):
    z = jnp.abs(h)
    t = 1.0 / (1.0 + (0.3275911 / math.sqrt(2.0)) * z)
    poly = t * (0.254829592 + t * (-0.284496736 + t * (1.421413741 + t * (-1.453152027 + t * 1.061405429))))
    gauss = jnp.exp2(h * h * (-0.5 / LN2))
    tail = 0.5 * poly * gauss
    cdf = jnp.where(h >= 0, 1.0 - tail, tail)
    return cdf, gauss * (1.0 / math.sqrt(2.0 * math.pi))


def cross_forward(
    first_ref, m_own, m_oth, q_own, q_oth, kv_own, kv_oth, co_own, co_oth, gain, shift, win_ref, tseg, mcol_ref,
    bt_ref, mt_ref, q_ref, k_ref, v_ref, o_ref, lse_ref, second_ref, c_ref, ct_ref,
    *work,
):
    core = lax.axis_index("tensor")
    tokens, _ = first_ref.shape
    half = kv_own.shape[2]
    n, _ = normalised(first_ref[...])
    b = (n * gain[1:2, :] + shift[1:2, :]).astype(BF16)
    bt_ref[...] = b.T
    sides = ((q_own, kv_own, slice(0, half)), (q_oth, kv_oth, slice(half, 2 * half)))
    for w, _, cols in sides:
        q_ref[:, cols] = (mm(b, w[...]) * QSCALE).astype(BF16)
    for m, place in ((m_own, core), (m_oth, 1 - core)):
        at = pl.ds(pl.multiple_of(place * tokens, tokens), tokens)
        m = m[...]
        mt_ref[:, at] = m.T
        for _, kv, cols in sides:
            k_ref[at, cols] = mm(m, kv[0]).astype(BF16)
            v_ref[at, cols] = mm(m, kv[1]).astype(BF16)
    attend_forward(core, q_ref, k_ref, v_ref, win_ref, tseg, mcol_ref, o_ref, lse_ref, *work)
    second = first_ref[...] + mm(o_ref[:, :half], co_own[...]) + mm(o_ref[:, half:], co_oth[...])
    second_ref[...] = second
    n, _ = normalised(second)
    c = (n * gain[2:3, :] + shift[2:3, :]).astype(BF16)
    c_ref[...] = c
    ct_ref[...] = c.T


def ffn_side(last, *refs):
    if last:
        c_ref, ct, cot_ref, fi, fo, y_in, dc_in, second_ref, gain, out_ref, second_grad_ref, dy_ref, g, norm_ref, y_ref, dc_ref = refs
        y_ref[...] = y_in[...]
        dc_ref[...] = dc_in[...]
    else:
        c_ref, ct, cot_ref, fi, fo, second_ref, y_ref, dc_ref, g = refs
        y_ref[...] = second_ref[...]
        dc_ref[...] = jnp.zeros_like(dc_ref)
    dim = c_ref.shape[1]
    ff_half = fi.shape[1]
    chunk = 512
    per = dim // chunk

    def step(j, carry):
        at = pl.ds(pl.multiple_of(j * chunk, chunk), chunk)
        cot = cot_ref[...]
        h = mm(c_ref[...], fi[:, at])
        cdf, pdf = gelu_parts(h)
        act = (h * cdf).astype(BF16)
        y_ref[...] += mm(act, fo[at, :])
        dh = (mm_t(cot, fo[at, :]) * (cdf + h * pdf)).astype(BF16)
        dc_ref[...] += mm_t(dh, fi[:, at])
        gi_rows = pl.ds(pl.multiple_of(j // per * dim, dim), dim)
        g[gi_rows, pl.ds(pl.multiple_of(j % per * chunk, chunk), chunk)] = mm(ct[...], dh).astype(BF16)
        g[pl.ds(pl.multiple_of(ff_half + j * chunk, chunk), chunk), :] = mm(act.T, cot).astype(BF16)
        return carry

    lax.fori_loop(0, ff_half // chunk, step, 0)
    if last:
        out_ref[...] = y_ref[...].astype(BF16)
        n, inv = normalised(second_ref[...])
        e = dc_ref[...]
        put_norms(norm_ref, total_rows(e * n), total_rows(e))
        second_grad = cot_ref[...].astype(F32) + norm_back(n, inv, gain[2:3, :], e)
        second_grad_ref[...] = second_grad
        dy_ref[...] = second_grad.astype(BF16)


def attention_pair(pr, half, inside, *refs):
    dy_ref, w_out, xqt_ref, xt_ref, q_ref, k_ref, v_ref, o_ref, lse_ref, win_ref, tseg, segcol_ref = refs[:12]
    dq_ref, dkv_out, g_ref, do_ref, dkv_ref, *work = refs[12:]
    core = lax.axis_index("tensor")
    tokens, dim = dy_ref.shape
    cols = slice(pr * 128, (pr + 1) * 128)
    start = pr * 128 % half
    dy = dy_ref[...]
    do_ref[...] = mm_t(dy, w_out[start : start + 128, :]).astype(BF16)
    out = mm(o_ref[:, cols].T, dy).astype(BF16)
    for j in range(dim // 128):
        g_ref[3 * dim + j * 128 : 3 * dim + (j + 1) * 128, :] = out[:, j * 128 : (j + 1) * 128]
    attend_backward(core, pr, q_ref, k_ref, v_ref, win_ref, tseg, segcol_ref, o_ref, do_ref, lse_ref, dq_ref, dkv_ref, *work)
    dkv_out[:, :128] = (dkv_ref[:, :128] * LN2).astype(BF16)
    dkv_out[:, 128:] = dkv_ref[:, 128:].astype(BF16)
    xqt = xt_ref[:, pl.ds(pl.multiple_of(core * tokens, tokens), tokens)] if inside else xqt_ref[...]
    g_ref[0:dim, :] = mm(xqt, dq_ref[...]).astype(BF16)
    gkv = mm(xt_ref[...], dkv_out[...]).astype(BF16)
    g_ref[dim : 2 * dim, :] = gkv[:, :128]
    g_ref[2 * dim : 3 * dim, :] = gkv[:, 128:]


def both(first, second, cols):
    return jnp.concatenate([first[:, cols], second[:, cols]], axis=1)


def cross_join(first_ref, second_grad_ref, *refs):
    dqs, dkvs = refs[0:4], refs[4:8]
    q_own, q_oth, kv_own, kv_oth, gain, first_grad_ref, dy_ref, gm_own, gm_oth, norm_ref = refs[8:]
    core = lax.axis_index("tensor")
    tokens, _ = first_ref.shape
    half = q_own.shape[1]
    weights = []
    for pr in range(len(dqs)):
        near = pr * 128 < half
        cols = slice(pr * 128 % half, pr * 128 % half + 128)
        weights.append((q_own if near else q_oth, kv_own if near else kv_oth, cols))
    db = sum(mm_t(dq[...], q[:, cols]) for dq, (q, _, cols) in zip(dqs, weights))
    n, inv = normalised(first_ref[...])
    put_norms(norm_ref, total_rows(db * n), total_rows(db))
    first_grad = second_grad_ref[...] + norm_back(n, inv, gain[1:2, :], db)
    first_grad_ref[...] = first_grad
    dy_ref[...] = first_grad.astype(BF16)
    pairs = [both(kv.at[0], kv.at[1], cols) for _, kv, cols in weights]
    for out, place in ((gm_own, core), (gm_oth, 1 - core)):
        at = pl.ds(pl.multiple_of(place * tokens, tokens), tokens)
        out[...] = sum(mm_t(d[at, :], w) for d, w in zip(dkvs, pairs)).astype(out.dtype)


def self_join(x_own, x_oth, *refs):
    dqs, dkvs = refs[0:4], refs[4:8]
    w_own, w_oth, da_own, da_oth, norm_ref = refs[8:]
    core = lax.axis_index("tensor")
    tokens, _ = x_own.shape
    half = w_own.shape[2]
    weights = []
    for pr in range(len(dqs)):
        weights.append((w_own if pr * 128 < half else w_oth, slice(pr * 128 % half, pr * 128 % half + 128)))
    pairs = [both(w.at[1], w.at[2], cols) for w, cols in weights]
    gain_sum, shift_sum = 0.0, 0.0
    for x, out, place in ((x_own, da_own, core), (x_oth, da_oth, 1 - core)):
        at = pl.ds(pl.multiple_of(place * tokens, tokens), tokens)
        e = sum(mm_t(d[at, :], w) for d, w in zip(dkvs, pairs))
        if x is x_own:
            e = e + sum(mm_t(dq[...], w[0, :, cols]) for dq, (w, cols) in zip(dqs, weights))
        out[...] = e.astype(out.dtype)
        n, _ = normalised(x[...].astype(F32))
        gain_sum = gain_sum + total_rows(e * n)
        shift_sum = shift_sum + total_rows(e)
    put_norms(norm_ref, gain_sum, shift_sum)


def finish_input(x_own, first_grad_ref, da_own, da_got, gain, out_ref):
    n, inv = normalised(x_own[...].astype(F32))
    e = da_own[...] + da_got[...].astype(F32)
    out_ref[...] = first_grad_ref[...] + norm_back(n, inv, gain[0:1, :], e)


def finish_norms(sums_ref, gain_ref, shift_ref):
    v = sums_ref[...].astype(F32)
    width = gain_ref.shape[1] // 128
    for layer in range(gain_ref.shape[0]):
        for j in range(width):
            row = 2 * layer * width + j
            gain_ref[layer : layer + 1, j * 128 : (j + 1) * 128] = v[row : row + 1, :]
            shift_ref[layer : layer + 1, j * 128 : (j + 1) * 128] = v[row + width : row + width + 1, :]


def unpack(pieces, heads_refs, out_ref):
    dim = heads_refs[0].shape[-2]
    for p, rows in enumerate(pieces):
        cols = slice(p * 128, (p + 1) * 128)
        for j, ref in enumerate(heads_refs):
            ref[:, cols] = rows(j * dim, dim).astype(F32)
        for j in range(dim // 128):
            out_ref[cols, j * 128 : (j + 1) * 128] = rows(len(heads_refs) * dim + j * 128, 128).astype(F32)


def finish_cross(low_ref, high_ref, q_ref, kv_ref, out_ref):
    pieces = [lambda at, n, ref=ref: ref[at : at + n, :] for ref in (low_ref, high_ref)]
    unpack(pieces, [q_ref, kv_ref.at[0], kv_ref.at[1]], out_ref)


def finish_self(low_a, high_a, low_b, high_b, qkv_ref, out_ref):
    half = low_a.shape[0]

    def rows(low, high):
        return lambda at, n: low[at : at + n, :] if at < half else high[at - half : at - half + n, :]

    unpack([rows(low_a, high_a), rows(low_b, high_b)], [qkv_ref.at[j] for j in range(3)], out_ref)


def shape(dims, dtype):
    return pltpu.VMEM(dims, dtype)


def smem_shape(dims, dtype):
    return jax.ShapeDtypeStruct(dims, dtype)


def hbm_shape(dims, dtype):
    return jax.ShapeDtypeStruct(dims, dtype)


class Late:
    def __init__(self, copy, ref):
        self.copy, self.ref, self.pending = copy, ref, True

    def get(self):
        if self.pending:
            self.copy.wait()
            self.pending = False
        return self.ref


def call(body, outs, scratch, args, smem=(), smem_out=(), late=(), near=(), after=(), us=5.0, vmem=12, name=None):
    in_vmem = pl.BlockSpec(memory_space=pltpu.VMEM)
    in_smem = pl.BlockSpec(memory_space=pltpu.SMEM)
    anywhere = pl.BlockSpec(memory_space=pl.ANY)
    n_args, n_after, n_late = len(args), len(after), len(late)

    def wrapped(*refs):
        ins, rest = list(refs[:n_args]), refs[n_args + n_after :]
        if n_late:
            rest, held, sems = rest[: -n_late - 1], rest[-n_late - 1 : -1], rest[-1]
            for j, i in enumerate(late):
                copy = pltpu.make_async_copy(ins[i], held[j], sems.at[j])
                copy.start()
                ins[i] = Late(copy, held[j])
        body(*ins, *rest)

    kind = lambda i: in_smem if i in smem else anywhere if i in late else in_vmem
    held = [pltpu.VMEM(args[i].shape, args[i].dtype) for i in late]
    place = lambda i: pltpu.HBM if i in late else pltpu.VMEM
    args = [x if i in smem or i in near else pltpu.with_memory_space_constraint(x, place(i)) for i, x in enumerate(args)]
    return pl.pallas_call(
        wrapped,
        out_shape=outs,
        in_specs=[kind(i) for i in range(n_args)] + [anywhere] * n_after,
        out_specs=[in_smem if i in smem_out else in_vmem for i in range(len(outs))],
        scratch_shapes=[x if not isinstance(x, tuple) else pltpu.VMEM(*x) for x in scratch]
        + held
        + ([pltpu.SemaphoreType.DMA((n_late,))] if n_late else []),
        compiler_params=pltpu.CompilerParams(vmem_limit_bytes=vmem * 1024 * 1024),
        cost_estimate=pl.CostEstimate(flops=int(us * 1.1e9), bytes_accessed=0, transcendentals=0),
        name=name,
    )(*args, *after)


FFN, CROSS, SELF_A, SELF_B = range(4)


def mask_orders(n):
    if n == 16:
        return [[[1, 2, 4, 8], [2, 1, 4, 8]], [[1, 2, 4, 8], [2, 1, 4, 8]], [[1, 2, 4, 8], [1, 2, 4, 8]], [[4, 1, 2, 8], [4, 2, 1, 8]]]
    base = [1 << j for j in range(n.bit_length() - 1)]
    turned = [base, base[1:] + base[:1]]
    return [turned, turned, [base, base], turned]


def swap(x, n, masks):
    pairs = [(i * 2 + t, (i ^ masks[t]) * 2 + t) for i in range(n) for t in range(2)]
    return lax.ppermute(x, ("dp", "tensor"), pairs)


def other(x):
    return lax.ppermute(x, "tensor", [(0, 1), (1, 0)])


def reduction_plans():
    n = lax.axis_size("dp")
    index, core = lax.axis_index("dp").astype(jnp.uint32), lax.axis_index("tensor")
    plans = []
    for orders in mask_orders(n):
        place = lambda mask: (index >> jnp.uint32(mask.bit_length() - 1)) & jnp.uint32(1)
        bits = [jnp.where(core == 0, place(a), place(b)) for a, b in zip(*orders)]
        plans.append([(bit, jnp.uint32(1) - bit, bit == 0) for bit in bits])
    return plans


class Reduction:
    def __init__(self, g, stream, plans):
        n = lax.axis_size("dp")
        self.n, self.g = n, g
        self.masks = list(zip(*mask_orders(n)[stream]))
        self.plan = plans[stream]
        self.name = ("ffn", "cross", "self_a", "self_b")[stream]
        steps = list(range(len(self.masks)))
        split = steps[:-1] if stream in (FFN, CROSS) else steps[:-2]
        self.hops = [(j, "halve") for j in split]
        self.hops += [(j, "add") for j in steps[len(split) :]]
        self.hops += [(j, "join") for j in reversed(split)]
        self.done, self.extra = 0, None

    def send(self):
        j, kind = self.hops[self.done]
        if kind == "halve":
            halves = self.g.reshape((2, self.g.shape[0] // 2) + self.g.shape[1:])
            self.keep = lax.dynamic_index_in_dim(halves, self.plan[j][0], 0, False)
            out = lax.dynamic_index_in_dim(halves, self.plan[j][1], 0, False)
        else:
            out = self.g if self.extra is None else jnp.concatenate([self.g, self.extra], axis=0)
            self.keep = self.g
        with jax.named_scope(f"{self.name}_{kind}_{self.done}"):
            self.got = swap(out, self.n, self.masks[j])
        return out

    def receive(self, *after):
        j, kind = self.hops[self.done]
        if after:
            self.got = lax.optimization_barrier((self.got, *after))[0]
        self.done += 1
        got = self.got
        if kind != "halve" and self.extra is not None:
            rows = self.g.shape[0]
            total = self.extra.astype(F32) + got[rows:].astype(F32)
            self.extra = lax.reduce_precision(total, 8, 7).astype(BF16)
            got = got[:rows]
        if kind != "join":
            self.g = (self.keep.astype(F32) + got.astype(F32)).astype(BF16)
            return
        own, first = self.g, self.plan[j][2]
        self.low, self.high = jnp.where(first, own, got), jnp.where(first, got, own)
        if self.running():
            self.g = jnp.concatenate([self.low, self.high], axis=0)

    def hop(self, *after):
        self.receive(*after)
        return self.send()

    def running(self):
        return self.done < len(self.hops)

    def finish(self):
        while self.running():
            self.receive()
            if self.running():
                self.send()


def local(inputs, memory, tgt_seg, mem_seg, self_qkv, self_out, cross_q, cross_kv, cross_out, ffn_in, ffn_out, norm_gain, norm_bias, cotangent):
    x_own, m_own, cot = inputs[0], memory[0], cotangent[0]
    tokens, dim = x_own.shape
    seq = 2 * tokens
    half = cross_q.shape[1]
    ff = ffn_in.shape[1]
    pairs, blocks = dim // 128, tokens // QB
    flat, tree = jax.tree.flatten(reduction_plans())
    x_own, *flat = lax.optimization_barrier((x_own, *flat))
    plans = jax.tree.unflatten(tree, flat)
    x_oth, w_oth, so_oth = other(x_own), other(self_qkv), other(self_out)

    lse = shape((blocks, pairs, 1, 2 * QB), F32)
    full, part = shape((seq, dim), BF16), shape((tokens, dim), BF16)
    wide = shape((tokens, dim), F32)
    norm = shape((2 * dim // 128, 128), F32)
    col, win = shape((seq, 128), jnp.int32), shape((2 * blocks, 128), F32)
    work = [((dim, seq), BF16)]
    narrow = shape((tokens, half), BF16)
    a_own, q, k, v, tcol, mcol, gain, shift, tseg, twin, mwin = call(
        self_start,
        [part, narrow, narrow, narrow, col, col, shape((3, dim), F32), shape((3, dim), F32), shape((1, seq), jnp.int32), win, win],
        [],
        [x_own, self_qkv, norm_gain, norm_bias, tgt_seg, tgt_seg, mem_seg],
        smem=(4,), late=(5, 6, 0, 2, 3, 1), us=3.0, name="self_start",
    )
    later = lax.optimization_barrier((m_own, cross_q, cross_kv, cross_out, ffn_in, ffn_out, a_own))
    m_oth, cq_oth, ckv_oth, co_oth, fi_oth, fo_oth = [other(x) for x in later[:6]]
    at, q, k, v, o, lse_s, first = call(
        self_forward,
        [shape((dim, seq), BF16), part, full, full, part, lse, wide],
        work,
        [x_own, x_oth, self_qkv, w_oth, self_out, so_oth, a_own, q, k, v, gain, shift, twin, tseg, tcol],
        near=range(6), us=8.0, name="self_forward",
    )
    bt, mt, qc, kc, vc, oc, lse_c, second, c, ct = call(
        cross_forward,
        [shape((dim, tokens), BF16), shape((dim, seq), BF16), part, full, full, part, lse, wide, part, shape((dim, tokens), BF16)],
        work,
        [first, m_own, m_oth, cross_q, cq_oth, cross_kv, ckv_oth, cross_out, co_oth, gain, shift, mwin, tseg, mcol],
        near=range(1, 9), us=9.0, name="cross_forward",
    )
    g_ffn = shape((2 * ff, dim), BF16)
    y, dc, gf_oth = call(
        functools.partial(ffn_side, False), [wide, wide, g_ffn], [],
        [c, ct, cot, fi_oth, fo_oth, second], near=(2, 3, 4), us=6.0, name="ffn_other",
    )
    gf_got = other(gf_oth)
    out, second_grad, dy, gf_own, norm_ffn = call(
        functools.partial(ffn_side, True), [hbm_shape((tokens, dim), BF16), wide, part, g_ffn, norm],
        [((tokens, dim), F32), ((tokens, dim), F32)],
        [c, ct, cot, ffn_in, ffn_out, y, dc, second, gain], near=(2, 3, 4), after=[gf_oth], us=7.5, name="ffn_own",
    )
    red_f = Reduction(gf_own + gf_got, FFN, plans)

    def pair(pr, inside, args, after, name):
        return call(
            functools.partial(attention_pair, pr, half, inside),
            [shape((tokens, 128), BF16), shape((seq, 256), BF16), shape((4 * dim, 128), BF16)],
            [((tokens, 128), BF16), ((seq, 256), F32), ((128, seq), BF16)],
            args, near=(1,), after=after, us=4.0, name=name,
        )

    shared = [bt, mt, qc, kc, vc, oc, lse_c, mwin, tseg, mcol]
    dq2, dkv2, g2 = pair(2, False, [dy, co_oth] + shared, [red_f.send()], "cross_back_2")
    got0 = other(g2)
    dq3, dkv3, g3 = pair(3, False, [dy, co_oth] + shared, [g2], "cross_back_3")
    got1 = other(g3)
    dq0, dkv0, g0 = pair(0, False, [dy, cross_out] + shared, [g3, red_f.hop(dq3)], "cross_back_0")
    dq1, dkv1, g1 = pair(1, False, [dy, cross_out] + shared, [g0, red_f.hop(dq0)], "cross_back_1")
    red_c = Reduction(jnp.concatenate([g0 + got0, g1 + got1], axis=0), CROSS, plans)
    first_grad, dy, gm_own, gm_oth, norm_cross = call(
        cross_join, [wide, part, wide, part, norm], [],
        [first, second_grad, dq0, dq1, dq2, dq3, dkv0, dkv1, dkv2, dkv3, cross_q, cq_oth, cross_kv, ckv_oth, gain],
        near=(10, 11, 12, 13), after=[red_f.hop(dq1), red_c.send()], us=2.0, name="cross_join",
    )
    shared = [at, at, q, k, v, o, lse_s, twin, tseg, tcol]
    dq2, dkv2, g2 = pair(2, True, [dy, so_oth] + shared, [], "self_back_2")
    got0 = other(g2)
    dq3, dkv3, g3 = pair(3, True, [dy, so_oth] + shared, [g2, red_f.hop(dq2), red_c.hop(dq2)], "self_back_3")
    got1 = other(g3)
    dq0, dkv0, g0 = pair(0, True, [dy, self_out] + shared, [g3, red_f.hop(dq3), red_c.hop(dq3)], "self_back_0")
    red_s0 = Reduction(g0 + got0, SELF_A, plans)
    dq1, dkv1, g1 = pair(1, True, [dy, self_out] + shared, [red_f.hop(dq0), red_c.hop(dq0), red_s0.send()], "self_back_1")
    red_s1 = Reduction(g1 + got1, SELF_B, plans)
    first_sent = red_s1.send()
    red_s0.hop(dq1)
    red_c.hop(dq1)
    red_s1.got, red_f.got = lax.optimization_barrier((red_s1.got, red_f.got))
    red_f.finish()
    grad_ffn_in = jnp.concatenate([red_f.low[j * dim : (j + 1) * dim] for j in range(ff // dim)], axis=1).astype(F32)
    grad_ffn_out = red_f.high.astype(F32)

    def lead(*done):
        leader = red_s1.got
        red_s1.got, *done = lax.optimization_barrier((leader, *done))
        sent = red_s1.hop()
        for r in (red_s0, red_c):
            if r.running():
                r.receive(leader)
                if r.running():
                    r.send()
        return sent, done

    da_own, da_oth, norm_self = call(
        self_join, [wide, part, norm], [],
        [x_own, x_oth, dq0, dq1, dq2, dq3, dkv0, dkv1, dkv2, dkv3, self_qkv, w_oth],
        near=(0, 1, 10, 11), after=[first_sent], us=2.0, name="self_join",
    )
    da_got, gm_got = other(da_oth), other(gm_oth)
    norms = jnp.concatenate([norm_self, norm_cross, norm_ffn], axis=0)
    norms = norms + other(norms)
    norms = jnp.pad(lax.reduce_precision(norms, 8, 7).astype(BF16), ((0, -norms.shape[0] % 16), (0, 0)))
    red_s0.extra = norms
    lead(da_oth)
    sent, _ = lead()
    (grad_input,) = call(
        finish_input, [hbm_shape((tokens, dim), F32)], [], [x_own, first_grad, da_own, da_got, gain],
        near=(0, 3), after=[sent], us=2.0, name="finish_input",
    )
    grad_memory = gm_own + gm_got.astype(F32)
    sent, (grad_input, grad_memory, grad_ffn_in, grad_ffn_out) = lead(grad_input, grad_memory, grad_ffn_in, grad_ffn_out)
    while red_s1.done < len(red_s1.hops) - 1:
        lead()
    red_s0.finish()
    red_c.finish()
    norm_shape = hbm_shape((3, dim), F32)
    grad_gain, grad_shift = call(finish_norms, [norm_shape, norm_shape], [], [red_s0.extra], near=(0,), us=1.0, name="finish_norms")

    stacked = lambda n: hbm_shape((n, dim, half), F32)
    out_shape = hbm_shape((half, dim), F32)
    cross_grads = call(
        finish_cross, [hbm_shape((dim, half), F32), stacked(2), out_shape], [], [red_c.low, red_c.high],
        near=(0, 1), us=2.0, name="finish_cross",
    )
    early = [*cross_grads, grad_gain, grad_shift]
    red_s1.got, *early = lax.optimization_barrier((red_s1.got, *early))
    red_s1.receive()
    grad_self_qkv, grad_self_out = call(
        finish_self, [stacked(3), out_shape], [], [red_s0.low, red_s0.high, red_s1.low, red_s1.high],
        near=range(4), us=2.0, name="finish_self",
    )
    return (
        out[None], grad_input[None], grad_memory[None], grad_self_qkv, grad_self_out,
        *early[:3], grad_ffn_in, grad_ffn_out, *early[3:],
    )


def solution(mesh):
    tokens = P("dp", "tensor", None)
    columns, rows = P(None, "tensor"), P("tensor", None)
    stacked = P(None, None, "tensor")
    return jax.shard_map(
        local,
        mesh=mesh,
        in_specs=(tokens, tokens, P("dp", None), P("dp", None), stacked, rows, columns, stacked, rows, columns, rows, P(), P(), tokens),
        out_specs=(tokens, tokens, tokens, stacked, rows, columns, stacked, rows, columns, rows, P(), P()),
        check_vma=False,
    )
```

```python
import functools
import math

import jax
import jax.numpy as jnp
from jax import lax
from jax.experimental import pallas as pl
from jax.experimental.pallas import tpu as pltpu
from jax.sharding import PartitionSpec as P

F32 = jnp.float32
BF16 = jnp.bfloat16
HD = 64
QB = 128
EPS = 1e-05
NEG = -1e9
LN2 = math.log(2.0)
QSCALE = HD**-0.5 / LN2
SAFE = 1e4


def mm(a, b):
    return lax.dot_general(a, b, (((1,), (0,)), ((), ())), preferred_element_type=F32)


def mm_t(a, b):
    return lax.dot_general(a, b, (((1,), (1,)), ((), ())), preferred_element_type=F32)


def normalised(v):
    centred = v - jnp.mean(v, axis=-1, keepdims=True)
    inv = lax.rsqrt(jnp.mean(centred * centred, axis=-1, keepdims=True) + EPS)
    return centred * inv, inv


def norm_back(n, inv, gain, e):
    ge = gain * e
    return (ge - jnp.mean(ge, axis=-1, keepdims=True) - n * jnp.mean(ge * n, axis=-1, keepdims=True)) * inv


def put_norms(norm_ref, gain_term, shift_term):
    width = gain_term.shape[1] // 128
    for i, term in enumerate((gain_term, shift_term)):
        for j in range(width):
            norm_ref[i * width + j : i * width + j + 1, :] = term[:, j * 128 : (j + 1) * 128]


def total_rows(v):
    return jnp.sum(v, axis=0, keepdims=True)


def count_below(seg, value):
    return jnp.sum(jnp.where(seg < value, 1.0, 0.0))


def windows(core, tokens, seg_q_smem, seg_k_ref, win_ref):
    seg_k = seg_k_ref[...]
    for qb in range(tokens // QB):
        first = core * tokens + qb * QB
        win_ref[2 * qb : 2 * qb + 1, :] = jnp.full((1, 128), count_below(seg_k, seg_q_smem[0, first]))
        win_ref[2 * qb + 1 : 2 * qb + 2, :] = jnp.full((1, 128), count_below(seg_k, seg_q_smem[0, first + QB - 1] + 1))


def bounds(win_ref, qb):
    lo, hi = [jnp.max(win_ref[pl.ds(2 * qb + j, 1), :]).astype(jnp.int32) for j in range(2)]
    return lo // 128 * 128, hi


def by_width(seq, lo, hi, run, rest, safe=True):
    need = hi - lo
    few, most = seq // 4, seq // 8 * 7
    at = lambda w: pl.multiple_of(jnp.minimum(lo, seq - w), 128)
    fits = jnp.logical_and(need <= most, safe)

    @pl.when(jnp.logical_and(fits, need <= few))
    def _():
        run(few, at(few))

    @pl.when(jnp.logical_and(fits, need > few))
    def _():
        run(most, at(most))

    @pl.when(jnp.logical_not(fits))
    def _():
        rest()


def seg_columns(seg_k_ref, out_ref):
    seq = seg_k_ref.shape[1]
    for j in range(seq // 128):
        row = jnp.broadcast_to(seg_k_ref[:, j * 128 : (j + 1) * 128], (128, 128))
        out_ref[j * 128 : (j + 1) * 128, :] = row.T


def two_heads(x):
    lane = lax.broadcasted_iota(jnp.int32, x.shape, 1)
    zero = jnp.zeros_like(x)
    return jnp.concatenate([jnp.where(lane < HD, x, zero), jnp.where(lane >= HD, x, zero)], axis=0)


def masked(s, segcol_ref, keys, seg_q_row):
    same = segcol_ref[keys, :] == seg_q_row
    return jnp.concatenate([jnp.where(same, s[:, :QB], NEG), jnp.where(same, s[:, QB:], NEG)], axis=1)


def head_norms(x):
    row = lax.broadcasted_iota(jnp.int32, (x.shape[1], 128), 0) // HD
    lane = lax.broadcasted_iota(jnp.int32, (x.shape[1], 128), 1)
    pick = jnp.where(row == lane, 1.0, 0.0).astype(BF16)
    xf = x.astype(F32)
    return jnp.max(mm((xf * xf).astype(BF16), pick), axis=0, keepdims=True)


def attend_forward(core, q_ref, k_ref, v_ref, win_ref, seg_q_ref, segcol_ref, o_ref, lse_ref, vt_ref):
    tokens, width = q_ref.shape
    vt_ref[...] = v_ref[...].T
    seq = k_ref.shape[0]
    pairs = width // 128
    small = jnp.max(head_norms(q_ref[...]) * head_norms(k_ref[...])) < SAFE

    def place(qb):
        first = pl.multiple_of(core * tokens + qb * QB, QB)
        return pl.ds(pl.multiple_of(qb * QB, QB), QB), seg_q_ref[:, pl.ds(first, QB)]

    def finish(qb, pr, rows, cols, ot, total, m):
        ot = ot / total
        ot = jnp.concatenate([ot[:HD, :QB], ot[HD:, QB:]], axis=0)
        o_ref[rows, cols] = ot.T.astype(BF16)
        lse_ref[qb, pr] = m + jnp.log2(total)

    def block(qb, carry):
        rows, seg_row = place(qb)

        def run(w, base):
            for pr in range(pairs):
                cols = slice(pr * 128, (pr + 1) * 128)
                q2 = two_heads(q_ref[rows, cols])
                ot = jnp.zeros((128, 2 * QB), F32)
                total = jnp.zeros((1, 2 * QB), F32)
                for c in range(0, w, 256):
                    keys = pl.ds(base + c, min(256, w - c))
                    e = jnp.exp2(masked(mm_t(k_ref[keys, cols], q2), segcol_ref, keys, seg_row))
                    total = total + jnp.sum(e, axis=0, keepdims=True)
                    ot = ot + mm(vt_ref[cols, keys], e.astype(BF16))
                finish(qb, pr, rows, cols, ot, total, 0.0)

        def with_max():
            def pair(pr, carry):
                cols = pl.ds(pl.multiple_of(pr * 128, 128), 128)
                q2 = two_heads(q_ref[rows, cols])

                def scores(j):
                    keys = pl.ds(pl.multiple_of(j * 256, 256), 256)
                    return keys, masked(mm_t(k_ref[keys, cols], q2), segcol_ref, keys, seg_row)

                def largest(j, m):
                    return jnp.maximum(m, jnp.max(scores(j)[1], axis=0, keepdims=True))

                m = lax.fori_loop(0, seq // 256, largest, jnp.full((1, 2 * QB), 2 * NEG, F32))

                def gather(j, acc):
                    keys, s = scores(j)
                    e = jnp.exp2(s - m)
                    return acc[0] + jnp.sum(e, axis=0, keepdims=True), acc[1] + mm(vt_ref[cols, keys], e.astype(BF16))

                start = (jnp.zeros((1, 2 * QB), F32), jnp.zeros((128, 2 * QB), F32))
                total, ot = lax.fori_loop(0, seq // 256, gather, start)
                finish(qb, pr, rows, cols, ot, total, m)
                return carry

            lax.fori_loop(0, pairs, pair, 0)

        def rest():
            pl.when(small)(lambda: run(seq, 0))
            pl.when(jnp.logical_not(small))(with_max)

        by_width(seq, *bounds(win_ref, qb), run, rest, small)
        return carry

    lax.fori_loop(0, tokens // QB, block, 0)


def attend_backward(core, pr, q_ref, k_ref, v_ref, win_ref, seg_q_ref, segcol_ref, o_ref, do_ref, lse_ref, dq_ref, dkv_ref, kt_ref):
    tokens = q_ref.shape[0]
    seq = k_ref.shape[0]
    cols = slice(pr * 128, (pr + 1) * 128)
    kt_ref[...] = k_ref[:, cols].T
    dkv_ref[...] = jnp.zeros_like(dkv_ref)

    def block(qb, carry):
        first = pl.multiple_of(core * tokens + qb * QB, QB)
        rows = pl.ds(pl.multiple_of(qb * QB, QB), QB)
        seg_row = seg_q_ref[:, pl.ds(first, QB)]

        def operands():
            do = do_ref[rows, :]
            inner = (do.astype(F32) * o_ref[rows, cols].astype(F32)).T
            inner = jnp.concatenate([total_rows(inner[:HD]), total_rows(inner[HD:])], axis=1)
            return two_heads(q_ref[rows, cols]), two_heads(do), inner

        def part(keys, q2, do2, inner):
            s = masked(mm_t(k_ref[keys, cols], q2), segcol_ref, keys, seg_row)
            p = jnp.exp2(s - lse_ref[qb, pr])
            dkv_ref[keys, 128:] += mm(p.astype(BF16), do2)
            ds = (p * (mm_t(v_ref[keys, cols], do2) - inner)).astype(BF16)
            dkv_ref[keys, :128] += mm(ds, q2)
            return mm(kt_ref[:, keys], ds)

        def finish(dqt):
            dqt = jnp.concatenate([dqt[:HD, :QB], dqt[HD:, QB:]], axis=0) * HD**-0.5
            dq_ref[rows, :] = dqt.T.astype(BF16)

        def run(w, base):
            finish(part(pl.ds(base, w), *operands()))

        def rest():
            given = operands()
            step = lambda j, dqt: dqt + part(pl.ds(pl.multiple_of(j * 512, 512), 512), *given)
            finish(lax.fori_loop(0, seq // 512, step, jnp.zeros((128, 2 * QB), F32)))

        by_width(seq, *bounds(win_ref, qb), run, rest)
        return carry

    lax.fori_loop(0, tokens // QB, block, 0)


def self_start(
    x_own, w_own, gain, shift, tseg_s, tseg, mseg,
    a_ref, q_ref, k_ref, v_ref, tcol_ref, mcol_ref, gain_ref, shift_ref, seg_ref, twin_ref, mwin_ref,
):
    core = lax.axis_index("tensor")
    tseg, mseg = tseg.get(), mseg.get()
    seg_ref[...] = tseg[...]
    windows(core, q_ref.shape[0], tseg_s, tseg, twin_ref)
    windows(core, q_ref.shape[0], tseg_s, mseg, mwin_ref)
    seg_columns(tseg, tcol_ref)
    seg_columns(mseg, mcol_ref)
    gain_ref[...] = gain.get()[...]
    shift_ref[...] = shift.get()[...]
    n, _ = normalised(x_own.get()[...].astype(F32))
    a = (n * gain_ref[0:1, :] + shift_ref[0:1, :]).astype(BF16)
    a_ref[...] = a
    w = w_own.get()
    q_ref[...] = (mm(a, w[0]) * QSCALE).astype(BF16)
    k_ref[...] = mm(a, w[1]).astype(BF16)
    v_ref[...] = mm(a, w[2]).astype(BF16)


def self_forward(
    x_own, x_oth, w_own, w_oth, so_own, so_oth, a_own, q_in, k_in, v_in, gain, shift, twin_ref, tseg, tcol_ref,
    at_ref, q_ref, k_ref, v_ref, o_ref, lse_ref, first_ref,
    *work,
):
    core = lax.axis_index("tensor")
    tokens, half = q_in.shape
    own, oth = slice(0, half), slice(half, 2 * half)
    here = pl.ds(pl.multiple_of(core * tokens, tokens), tokens)
    there = pl.ds(pl.multiple_of((1 - core) * tokens, tokens), tokens)
    a = a_own[...]
    at_ref[:, here] = a.T
    q_ref[:, own] = q_in[...]
    k_ref[here, own] = k_in[...]
    v_ref[here, own] = v_in[...]
    n, _ = normalised(x_oth[...].astype(F32))
    a2 = (n * gain[0:1, :] + shift[0:1, :]).astype(BF16)
    at_ref[:, there] = a2.T
    w = w_oth
    q_ref[:, oth] = (mm(a, w[0]) * QSCALE).astype(BF16)
    k_ref[here, oth] = mm(a, w[1]).astype(BF16)
    v_ref[here, oth] = mm(a, w[2]).astype(BF16)
    k_ref[there, oth] = mm(a2, w[1]).astype(BF16)
    v_ref[there, oth] = mm(a2, w[2]).astype(BF16)
    w = w_own
    k_ref[there, own] = mm(a2, w[1]).astype(BF16)
    v_ref[there, own] = mm(a2, w[2]).astype(BF16)
    attend_forward(core, q_ref, k_ref, v_ref, twin_ref, tseg, tcol_ref, o_ref, lse_ref, *work)
    first_ref[...] = x_own[...].astype(F32) + mm(o_ref[:, own], so_own[...]) + mm(o_ref[:, oth], so_oth[...])


def gelu_parts(h):
    z = jnp.abs(h)
    t = 1.0 / (1.0 + (0.3275911 / math.sqrt(2.0)) * z)
    poly = t * (0.254829592 + t * (-0.284496736 + t * (1.421413741 + t * (-1.453152027 + t * 1.061405429))))
    gauss = jnp.exp2(h * h * (-0.5 / LN2))
    tail = 0.5 * poly * gauss
    cdf = jnp.where(h >= 0, 1.0 - tail, tail)
    return cdf, gauss * (1.0 / math.sqrt(2.0 * math.pi))


def cross_forward(
    first_ref, m_own, m_oth, q_own, q_oth, kv_own, kv_oth, co_own, co_oth, gain, shift, win_ref, tseg, mcol_ref,
    bt_ref, mt_ref, q_ref, k_ref, v_ref, o_ref, lse_ref, second_ref, c_ref, ct_ref,
    *work,
):
    core = lax.axis_index("tensor")
    tokens, _ = first_ref.shape
    half = kv_own.shape[2]
    n, _ = normalised(first_ref[...])
    b = (n * gain[1:2, :] + shift[1:2, :]).astype(BF16)
    bt_ref[...] = b.T
    sides = ((q_own, kv_own, slice(0, half)), (q_oth, kv_oth, slice(half, 2 * half)))
    for w, _, cols in sides:
        q_ref[:, cols] = (mm(b, w[...]) * QSCALE).astype(BF16)
    for m, place in ((m_own, core), (m_oth, 1 - core)):
        at = pl.ds(pl.multiple_of(place * tokens, tokens), tokens)
        m = m[...]
        mt_ref[:, at] = m.T
        for _, kv, cols in sides:
            k_ref[at, cols] = mm(m, kv[0]).astype(BF16)
            v_ref[at, cols] = mm(m, kv[1]).astype(BF16)
    attend_forward(core, q_ref, k_ref, v_ref, win_ref, tseg, mcol_ref, o_ref, lse_ref, *work)
    second = first_ref[...] + mm(o_ref[:, :half], co_own[...]) + mm(o_ref[:, half:], co_oth[...])
    second_ref[...] = second
    n, _ = normalised(second)
    c = (n * gain[2:3, :] + shift[2:3, :]).astype(BF16)
    c_ref[...] = c
    ct_ref[...] = c.T


def ffn_side(last, *refs):
    if last:
        c_ref, ct, cot_ref, fi, fo, y_in, dc_in, second_ref, gain, out_ref, second_grad_ref, dy_ref, g, norm_ref, y_ref, dc_ref = refs
        y_ref[...] = y_in[...]
        dc_ref[...] = dc_in[...]
    else:
        c_ref, ct, cot_ref, fi, fo, second_ref, y_ref, dc_ref, g = refs
        y_ref[...] = second_ref[...]
        dc_ref[...] = jnp.zeros_like(dc_ref)
    dim = c_ref.shape[1]
    ff_half = fi.shape[1]
    chunk = 512
    per = dim // chunk

    def step(j, carry):
        at = pl.ds(pl.multiple_of(j * chunk, chunk), chunk)
        cot = cot_ref[...]
        h = mm(c_ref[...], fi[:, at])
        cdf, pdf = gelu_parts(h)
        act = (h * cdf).astype(BF16)
        y_ref[...] += mm(act, fo[at, :])
        dh = (mm_t(cot, fo[at, :]) * (cdf + h * pdf)).astype(BF16)
        dc_ref[...] += mm_t(dh, fi[:, at])
        gi_rows = pl.ds(pl.multiple_of(j // per * dim, dim), dim)
        g[gi_rows, pl.ds(pl.multiple_of(j % per * chunk, chunk), chunk)] = mm(ct[...], dh).astype(BF16)
        g[pl.ds(pl.multiple_of(ff_half + j * chunk, chunk), chunk), :] = mm(act.T, cot).astype(BF16)
        return carry

    lax.fori_loop(0, ff_half // chunk, step, 0)
    if last:
        out_ref[...] = y_ref[...].astype(BF16)
        n, inv = normalised(second_ref[...])
        e = dc_ref[...]
        put_norms(norm_ref, total_rows(e * n), total_rows(e))
        second_grad = cot_ref[...].astype(F32) + norm_back(n, inv, gain[2:3, :], e)
        second_grad_ref[...] = second_grad
        dy_ref[...] = second_grad.astype(BF16)


def attention_pair(pr, half, inside, *refs):
    dy_ref, w_out, xqt_ref, xt_ref, q_ref, k_ref, v_ref, o_ref, lse_ref, win_ref, tseg, segcol_ref = refs[:12]
    dq_ref, dkv_out, g_ref, do_ref, dkv_ref, *work = refs[12:]
    core = lax.axis_index("tensor")
    tokens, dim = dy_ref.shape
    cols = slice(pr * 128, (pr + 1) * 128)
    start = pr * 128 % half
    dy = dy_ref[...]
    do_ref[...] = mm_t(dy, w_out[start : start + 128, :]).astype(BF16)
    out = mm(o_ref[:, cols].T, dy).astype(BF16)
    for j in range(dim // 128):
        g_ref[3 * dim + j * 128 : 3 * dim + (j + 1) * 128, :] = out[:, j * 128 : (j + 1) * 128]
    attend_backward(core, pr, q_ref, k_ref, v_ref, win_ref, tseg, segcol_ref, o_ref, do_ref, lse_ref, dq_ref, dkv_ref, *work)
    dkv_out[:, :128] = (dkv_ref[:, :128] * LN2).astype(BF16)
    dkv_out[:, 128:] = dkv_ref[:, 128:].astype(BF16)
    xqt = xt_ref[:, pl.ds(pl.multiple_of(core * tokens, tokens), tokens)] if inside else xqt_ref[...]
    g_ref[0:dim, :] = mm(xqt, dq_ref[...]).astype(BF16)
    gkv = mm(xt_ref[...], dkv_out[...]).astype(BF16)
    g_ref[dim : 2 * dim, :] = gkv[:, :128]
    g_ref[2 * dim : 3 * dim, :] = gkv[:, 128:]


def both(first, second, cols):
    return jnp.concatenate([first[:, cols], second[:, cols]], axis=1)


def cross_join(first_ref, second_grad_ref, *refs):
    dqs, dkvs = refs[0:4], refs[4:8]
    q_own, q_oth, kv_own, kv_oth, gain, first_grad_ref, dy_ref, gm_own, gm_oth, norm_ref = refs[8:]
    core = lax.axis_index("tensor")
    tokens, _ = first_ref.shape
    half = q_own.shape[1]
    weights = []
    for pr in range(len(dqs)):
        near = pr * 128 < half
        cols = slice(pr * 128 % half, pr * 128 % half + 128)
        weights.append((q_own if near else q_oth, kv_own if near else kv_oth, cols))
    db = sum(mm_t(dq[...], q[:, cols]) for dq, (q, _, cols) in zip(dqs, weights))
    n, inv = normalised(first_ref[...])
    put_norms(norm_ref, total_rows(db * n), total_rows(db))
    first_grad = second_grad_ref[...] + norm_back(n, inv, gain[1:2, :], db)
    first_grad_ref[...] = first_grad
    dy_ref[...] = first_grad.astype(BF16)
    pairs = [both(kv.at[0], kv.at[1], cols) for _, kv, cols in weights]
    for out, place in ((gm_own, core), (gm_oth, 1 - core)):
        at = pl.ds(pl.multiple_of(place * tokens, tokens), tokens)
        out[...] = sum(mm_t(d[at, :], w) for d, w in zip(dkvs, pairs)).astype(out.dtype)


def self_join(x_own, x_oth, *refs):
    dqs, dkvs = refs[0:4], refs[4:8]
    w_own, w_oth, da_own, da_oth, norm_ref = refs[8:]
    core = lax.axis_index("tensor")
    tokens, _ = x_own.shape
    half = w_own.shape[2]
    weights = []
    for pr in range(len(dqs)):
        weights.append((w_own if pr * 128 < half else w_oth, slice(pr * 128 % half, pr * 128 % half + 128)))
    pairs = [both(w.at[1], w.at[2], cols) for w, cols in weights]
    gain_sum, shift_sum = 0.0, 0.0
    for x, out, place in ((x_own, da_own, core), (x_oth, da_oth, 1 - core)):
        at = pl.ds(pl.multiple_of(place * tokens, tokens), tokens)
        e = sum(mm_t(d[at, :], w) for d, w in zip(dkvs, pairs))
        if x is x_own:
            e = e + sum(mm_t(dq[...], w[0, :, cols]) for dq, (w, cols) in zip(dqs, weights))
        out[...] = e.astype(out.dtype)
        n, _ = normalised(x[...].astype(F32))
        gain_sum = gain_sum + total_rows(e * n)
        shift_sum = shift_sum + total_rows(e)
    put_norms(norm_ref, gain_sum, shift_sum)


def finish_input(x_own, first_grad_ref, da_own, da_got, gain, out_ref):
    n, inv = normalised(x_own[...].astype(F32))
    e = da_own[...] + da_got[...].astype(F32)
    out_ref[...] = first_grad_ref[...] + norm_back(n, inv, gain[0:1, :], e)


def finish_norms(sums_ref, gain_ref, shift_ref):
    v = sums_ref[...].astype(F32)
    width = gain_ref.shape[1] // 128
    for layer in range(gain_ref.shape[0]):
        for j in range(width):
            row = 2 * layer * width + j
            gain_ref[layer : layer + 1, j * 128 : (j + 1) * 128] = v[row : row + 1, :]
            shift_ref[layer : layer + 1, j * 128 : (j + 1) * 128] = v[row + width : row + width + 1, :]


def unpack(pieces, heads_refs, out_ref):
    dim = heads_refs[0].shape[-2]
    for p, rows in enumerate(pieces):
        cols = slice(p * 128, (p + 1) * 128)
        for j, ref in enumerate(heads_refs):
            ref[:, cols] = rows(j * dim, dim).astype(F32)
        for j in range(dim // 128):
            out_ref[cols, j * 128 : (j + 1) * 128] = rows(len(heads_refs) * dim + j * 128, 128).astype(F32)


def finish_cross(low_ref, high_ref, q_ref, kv_ref, out_ref):
    pieces = [lambda at, n, ref=ref: ref[at : at + n, :] for ref in (low_ref, high_ref)]
    unpack(pieces, [q_ref, kv_ref.at[0], kv_ref.at[1]], out_ref)


def finish_self(low_a, high_a, low_b, high_b, qkv_ref, out_ref):
    half = low_a.shape[0]

    def rows(low, high):
        return lambda at, n: low[at : at + n, :] if at < half else high[at - half : at - half + n, :]

    unpack([rows(low_a, high_a), rows(low_b, high_b)], [qkv_ref.at[j] for j in range(3)], out_ref)


def shape(dims, dtype):
    return pltpu.VMEM(dims, dtype)


def smem_shape(dims, dtype):
    return jax.ShapeDtypeStruct(dims, dtype)


def hbm_shape(dims, dtype):
    return jax.ShapeDtypeStruct(dims, dtype)


class Late:
    def __init__(self, copy, ref):
        self.copy, self.ref, self.pending = copy, ref, True

    def get(self):
        if self.pending:
            self.copy.wait()
            self.pending = False
        return self.ref


def call(body, outs, scratch, args, smem=(), smem_out=(), late=(), near=(), after=(), us=5.0, vmem=12, name=None):
    in_vmem = pl.BlockSpec(memory_space=pltpu.VMEM)
    in_smem = pl.BlockSpec(memory_space=pltpu.SMEM)
    anywhere = pl.BlockSpec(memory_space=pl.ANY)
    n_args, n_after, n_late = len(args), len(after), len(late)

    def wrapped(*refs):
        ins, rest = list(refs[:n_args]), refs[n_args + n_after :]
        if n_late:
            rest, held, sems = rest[: -n_late - 1], rest[-n_late - 1 : -1], rest[-1]
            for j, i in enumerate(late):
                copy = pltpu.make_async_copy(ins[i], held[j], sems.at[j])
                copy.start()
                ins[i] = Late(copy, held[j])
        body(*ins, *rest)

    kind = lambda i: in_smem if i in smem else anywhere if i in late else in_vmem
    held = [pltpu.VMEM(args[i].shape, args[i].dtype) for i in late]
    place = lambda i: pltpu.HBM if i in late else pltpu.VMEM
    args = [x if i in smem or i in near else pltpu.with_memory_space_constraint(x, place(i)) for i, x in enumerate(args)]
    return pl.pallas_call(
        wrapped,
        out_shape=outs,
        in_specs=[kind(i) for i in range(n_args)] + [anywhere] * n_after,
        out_specs=[in_smem if i in smem_out else in_vmem for i in range(len(outs))],
        scratch_shapes=[x if not isinstance(x, tuple) else pltpu.VMEM(*x) for x in scratch]
        + held
        + ([pltpu.SemaphoreType.DMA((n_late,))] if n_late else []),
        compiler_params=pltpu.CompilerParams(vmem_limit_bytes=vmem * 1024 * 1024),
        cost_estimate=pl.CostEstimate(flops=int(us * 1.1e9), bytes_accessed=0, transcendentals=0),
        name=name,
    )(*args, *after)


FFN, CROSS, SELF_A, SELF_B = range(4)


def mask_orders(n):
    if n == 16:
        return [[[1, 2, 4, 8], [2, 1, 4, 8]], [[1, 2, 4, 8], [2, 1, 4, 8]], [[1, 2, 4, 8], [1, 2, 4, 8]], [[4, 1, 2, 8], [4, 2, 1, 8]]]
    base = [1 << j for j in range(n.bit_length() - 1)]
    turned = [base, base[1:] + base[:1]]
    return [turned, turned, [base, base], turned]


def swap(x, n, masks):
    pairs = [(i * 2 + t, (i ^ masks[t]) * 2 + t) for i in range(n) for t in range(2)]
    return lax.ppermute(x, ("dp", "tensor"), pairs)


def other(x):
    return lax.ppermute(x, "tensor", [(0, 1), (1, 0)])


def reduction_plans():
    n = lax.axis_size("dp")
    index, core = lax.axis_index("dp").astype(jnp.uint32), lax.axis_index("tensor")
    plans = []
    for orders in mask_orders(n):
        place = lambda mask: (index >> jnp.uint32(mask.bit_length() - 1)) & jnp.uint32(1)
        bits = [jnp.where(core == 0, place(a), place(b)) for a, b in zip(*orders)]
        plans.append([(bit, jnp.uint32(1) - bit, bit == 0) for bit in bits])
    return plans


class Reduction:
    def __init__(self, g, stream, plans):
        n = lax.axis_size("dp")
        self.n, self.g = n, g
        self.masks = list(zip(*mask_orders(n)[stream]))
        self.plan = plans[stream]
        self.name = ("ffn", "cross", "self_a", "self_b")[stream]
        steps = list(range(len(self.masks)))
        split = steps[:-1] if stream in (FFN, CROSS) else steps[:-2]
        self.hops = [(j, "halve") for j in split]
        self.hops += [(j, "add") for j in steps[len(split) :]]
        self.hops += [(j, "join") for j in reversed(split)]
        self.done, self.extra = 0, None

    def send(self):
        j, kind = self.hops[self.done]
        if kind == "halve":
            halves = self.g.reshape((2, self.g.shape[0] // 2) + self.g.shape[1:])
            self.keep = lax.dynamic_index_in_dim(halves, self.plan[j][0], 0, False)
            out = lax.dynamic_index_in_dim(halves, self.plan[j][1], 0, False)
        else:
            out = self.g if self.extra is None else jnp.concatenate([self.g, self.extra], axis=0)
            self.keep = self.g
        with jax.named_scope(f"{self.name}_{kind}_{self.done}"):
            self.got = swap(out, self.n, self.masks[j])
        return out

    def receive(self, *after):
        j, kind = self.hops[self.done]
        if after:
            self.got = lax.optimization_barrier((self.got, *after))[0]
        self.done += 1
        got = self.got
        if kind != "halve" and self.extra is not None:
            rows = self.g.shape[0]
            total = self.extra.astype(F32) + got[rows:].astype(F32)
            self.extra = lax.reduce_precision(total, 8, 7).astype(BF16)
            got = got[:rows]
        if kind != "join":
            self.g = (self.keep.astype(F32) + got.astype(F32)).astype(BF16)
            return
        own, first = self.g, self.plan[j][2]
        self.low, self.high = jnp.where(first, own, got), jnp.where(first, got, own)
        if self.running():
            self.g = jnp.concatenate([self.low, self.high], axis=0)

    def hop(self, *after):
        self.receive(*after)
        return self.send()

    def running(self):
        return self.done < len(self.hops)

    def finish(self):
        while self.running():
            self.receive()
            if self.running():
                self.send()


def local(inputs, memory, tgt_seg, mem_seg, self_qkv, self_out, cross_q, cross_kv, cross_out, ffn_in, ffn_out, norm_gain, norm_bias, cotangent):
    x_own, m_own, cot = inputs[0], memory[0], cotangent[0]
    tokens, dim = x_own.shape
    seq = 2 * tokens
    half = cross_q.shape[1]
    ff = ffn_in.shape[1]
    pairs, blocks = dim // 128, tokens // QB
    flat, tree = jax.tree.flatten(reduction_plans())
    x_own, *flat = lax.optimization_barrier((x_own, *flat))
    plans = jax.tree.unflatten(tree, flat)
    x_oth, w_oth, so_oth = other(x_own), other(self_qkv), other(self_out)

    lse = shape((blocks, pairs, 1, 2 * QB), F32)
    full, part = shape((seq, dim), BF16), shape((tokens, dim), BF16)
    wide = shape((tokens, dim), F32)
    norm = shape((2 * dim // 128, 128), F32)
    col, win = shape((seq, 128), jnp.int32), shape((2 * blocks, 128), F32)
    work = [((dim, seq), BF16)]
    narrow = shape((tokens, half), BF16)
    a_own, q, k, v, tcol, mcol, gain, shift, tseg, twin, mwin = call(
        self_start,
        [part, narrow, narrow, narrow, col, col, shape((3, dim), F32), shape((3, dim), F32), shape((1, seq), jnp.int32), win, win],
        [],
        [x_own, self_qkv, norm_gain, norm_bias, tgt_seg, tgt_seg, mem_seg],
        smem=(4,), late=(5, 6, 0, 2, 3, 1), us=3.0, name="self_start",
    )
    later = lax.optimization_barrier((m_own, cross_q, cross_kv, cross_out, ffn_in, ffn_out, a_own))
    m_oth, cq_oth, ckv_oth, co_oth, fi_oth, fo_oth = [other(x) for x in later[:6]]
    at, q, k, v, o, lse_s, first = call(
        self_forward,
        [shape((dim, seq), BF16), part, full, full, part, lse, wide],
        work,
        [x_own, x_oth, self_qkv, w_oth, self_out, so_oth, a_own, q, k, v, gain, shift, twin, tseg, tcol],
        near=range(6), us=8.0, name="self_forward",
    )
    bt, mt, qc, kc, vc, oc, lse_c, second, c, ct = call(
        cross_forward,
        [shape((dim, tokens), BF16), shape((dim, seq), BF16), part, full, full, part, lse, wide, part, shape((dim, tokens), BF16)],
        work,
        [first, m_own, m_oth, cross_q, cq_oth, cross_kv, ckv_oth, cross_out, co_oth, gain, shift, mwin, tseg, mcol],
        near=range(1, 9), us=9.0, name="cross_forward",
    )
    g_ffn = shape((2 * ff, dim), BF16)
    y, dc, gf_oth = call(
        functools.partial(ffn_side, False), [wide, wide, g_ffn], [],
        [c, ct, cot, fi_oth, fo_oth, second], near=(2, 3, 4), us=6.0, name="ffn_other",
    )
    gf_got = other(gf_oth)
    out, second_grad, dy, gf_own, norm_ffn = call(
        functools.partial(ffn_side, True), [hbm_shape((tokens, dim), BF16), wide, part, g_ffn, norm],
        [((tokens, dim), F32), ((tokens, dim), F32)],
        [c, ct, cot, ffn_in, ffn_out, y, dc, second, gain], near=(2, 3, 4), after=[gf_oth], us=7.5, name="ffn_own",
    )
    red_f = Reduction(gf_own + gf_got, FFN, plans)

    def pair(pr, inside, args, after, name):
        return call(
            functools.partial(attention_pair, pr, half, inside),
            [shape((tokens, 128), BF16), shape((seq, 256), BF16), shape((4 * dim, 128), BF16)],
            [((tokens, 128), BF16), ((seq, 256), F32), ((128, seq), BF16)],
            args, near=(1,), after=after, us=4.0, name=name,
        )

    shared = [bt, mt, qc, kc, vc, oc, lse_c, mwin, tseg, mcol]
    dq2, dkv2, g2 = pair(2, False, [dy, co_oth] + shared, [red_f.send()], "cross_back_2")
    got0 = other(g2)
    dq3, dkv3, g3 = pair(3, False, [dy, co_oth] + shared, [g2], "cross_back_3")
    got1 = other(g3)
    dq0, dkv0, g0 = pair(0, False, [dy, cross_out] + shared, [g3, red_f.hop(dq3)], "cross_back_0")
    dq1, dkv1, g1 = pair(1, False, [dy, cross_out] + shared, [g0, red_f.hop(dq0)], "cross_back_1")
    red_c = Reduction(jnp.concatenate([g0 + got0, g1 + got1], axis=0), CROSS, plans)
    first_grad, dy, gm_own, gm_oth, norm_cross = call(
        cross_join, [wide, part, wide, part, norm], [],
        [first, second_grad, dq0, dq1, dq2, dq3, dkv0, dkv1, dkv2, dkv3, cross_q, cq_oth, cross_kv, ckv_oth, gain],
        near=(10, 11, 12, 13), after=[red_f.hop(dq1), red_c.send()], us=2.0, name="cross_join",
    )
    shared = [at, at, q, k, v, o, lse_s, twin, tseg, tcol]
    dq2, dkv2, g2 = pair(2, True, [dy, so_oth] + shared, [], "self_back_2")
    got0 = other(g2)
    dq3, dkv3, g3 = pair(3, True, [dy, so_oth] + shared, [g2, red_f.hop(dq2), red_c.hop(dq2)], "self_back_3")
    got1 = other(g3)
    dq0, dkv0, g0 = pair(0, True, [dy, self_out] + shared, [g3, red_f.hop(dq3), red_c.hop(dq3)], "self_back_0")
    red_s0 = Reduction(g0 + got0, SELF_A, plans)
    dq1, dkv1, g1 = pair(1, True, [dy, self_out] + shared, [red_f.hop(dq0), red_c.hop(dq0), red_s0.send()], "self_back_1")
    red_s1 = Reduction(g1 + got1, SELF_B, plans)
    first_sent = red_s1.send()
    red_s0.hop(dq1)
    red_c.hop(dq1)
    red_s1.got, red_f.got = lax.optimization_barrier((red_s1.got, red_f.got))
    red_f.finish()
    grad_ffn_in = jnp.concatenate([red_f.low[j * dim : (j + 1) * dim] for j in range(ff // dim)], axis=1).astype(F32)
    grad_ffn_out = red_f.high.astype(F32)

    def lead(*done):
        leader = red_s1.got
        red_s1.got, *done = lax.optimization_barrier((leader, *done))
        sent = red_s1.hop()
        for r in (red_s0, red_c):
            if r.running():
                r.receive(leader)
                if r.running():
                    r.send()
        return sent, done

    da_own, da_oth, norm_self = call(
        self_join, [wide, part, norm], [],
        [x_own, x_oth, dq0, dq1, dq2, dq3, dkv0, dkv1, dkv2, dkv3, self_qkv, w_oth],
        near=(0, 1, 10, 11), after=[first_sent], us=2.0, name="self_join",
    )
    da_got, gm_got = other(da_oth), other(gm_oth)
    norms = jnp.concatenate([norm_self, norm_cross, norm_ffn], axis=0)
    norms = norms + other(norms)
    norms = jnp.pad(lax.reduce_precision(norms, 8, 7).astype(BF16), ((0, -norms.shape[0] % 16), (0, 0)))
    red_s0.extra = norms
    lead(da_oth)
    sent, _ = lead()
    (grad_input,) = call(
        finish_input, [hbm_shape((tokens, dim), F32)], [], [x_own, first_grad, da_own, da_got, gain],
        near=(0, 3), after=[sent], us=2.0, name="finish_input",
    )
    grad_memory = gm_own + gm_got.astype(F32)
    sent, (grad_input, grad_memory, grad_ffn_in, grad_ffn_out) = lead(grad_input, grad_memory, grad_ffn_in, grad_ffn_out)
    while red_s1.done < len(red_s1.hops) - 1:
        lead()
    red_s0.finish()
    red_c.finish()
    norm_shape = hbm_shape((3, dim), F32)
    grad_gain, grad_shift = call(finish_norms, [norm_shape, norm_shape], [], [red_s0.extra], near=(0,), us=1.0, name="finish_norms")

    stacked = lambda n: hbm_shape((n, dim, half), F32)
    out_shape = hbm_shape((half, dim), F32)
    cross_grads = call(
        finish_cross, [hbm_shape((dim, half), F32), stacked(2), out_shape], [], [red_c.low, red_c.high],
        near=(0, 1), us=2.0, name="finish_cross",
    )
    early = [*cross_grads, grad_gain, grad_shift]
    red_s1.got, *early = lax.optimization_barrier((red_s1.got, *early))
    red_s1.receive()
    grad_self_qkv, grad_self_out = call(
        finish_self, [stacked(3), out_shape], [], [red_s0.low, red_s0.high, red_s1.low, red_s1.high],
        near=range(4), us=2.0, name="finish_self",
    )
    return (
        out[None], grad_input[None], grad_memory[None], grad_self_qkv, grad_self_out,
        *early[:3], grad_ffn_in, grad_ffn_out, *early[3:],
    )


def solution(mesh):
    tokens = P("dp", "tensor", None)
    columns, rows = P(None, "tensor"), P("tensor", None)
    stacked = P(None, None, "tensor")
    return jax.shard_map(
        local,
        mesh=mesh,
        in_specs=(tokens, tokens, P("dp", None), P("dp", None), stacked, rows, columns, stacked, rows, columns, rows, P(), P(), tokens),
        out_specs=(tokens, tokens, tokens, stacked, rows, columns, stacked, rows, columns, rows, P(), P()),
        check_vma=False,
    )
```
